512 devices in a mesh: dp: 16 (over y, core), rows: 16 (over x, z_hi), cols: 2 (over z_lo).
Axes of the slice: x: 4, y: 8, z: 8 (z_hi: 4, z_lo: 2; z = z_hi * 2 + z_lo), core: 2. Of those that a mesh axis runs over, the one named last changes fastest.
Arguments:
- c3: bfloat16 [16, 128, 128, 512], P('dp', 'rows', 'cols'), may hold values from -6 to 6
- c4: bfloat16 [16, 64, 64, 1024], P('dp', 'rows', 'cols'), may hold values from -6 to 6
- top_down: bfloat16 [16, 32, 32, 256], P('dp', 'rows', 'cols'), may hold values from -6 to 6
- lat3_weight: bfloat16 [512, 256], replicated, may hold values from -0.25 to 0.25
- lat4_weight: bfloat16 [1024, 256], replicated, may hold values from -0.1875 to 0.1875
- conv_weight: bfloat16 [2304, 256], replicated, may hold values from -0.125 to 0.125
- p3_cot: bfloat16 [16, 128, 128, 256], P('dp', 'rows', 'cols'), may hold values from -6 to 6
- m4_cot: bfloat16 [16, 64, 64, 256], P('dp', 'rows', 'cols'), may hold values from -6 to 6
Outputs:
- p3: bfloat16 [16, 128, 128, 256], P('dp', 'rows', 'cols')
- c3_grad: bfloat16 [16, 128, 128, 512], P('dp', 'rows', 'cols')
- c4_grad: bfloat16 [16, 64, 64, 1024], P('dp', 'rows', 'cols')
- top_grad: bfloat16 [16, 32, 32, 256], P('dp', 'rows', 'cols')
- weight_grads: float32 [3840, 256], P('dp')
The draws below stay inside these ranges and needn't reach their ends.
All inputs are finite; a program needn't handle non-finite values.
Results may differ from the reference program's by a relative error of at most 0.02.
Values may be sent and summed in bfloat16 or wider, within the bound.
No kernel may reach another device: no remote copies, remote signals or barrier semaphores. Data moves between devices by JAX's collectives and lax.ppermute only.
A program may use at most 64 MiB of HBM per device.

```python
import math
import jax
import jax.numpy as jnp
from jax import lax

CH = 256
C3CH = 512
C4CH = 1024
IMAGES = 16
H4 = 64
W4 = 64
H3 = 128
W3 = 128
H5 = 32
W5 = 32
GROWS = 3840


def spiked(result, rng, source, target, parts, factor):
    owner, partner = [(jnp.arange(result.shape[dim]) // (result.shape[dim] // parts)).reshape([-1 if axis == dim else 1 for axis in range(result.ndim)]) for dim in (source, target)]
    chosen = jax.random.permutation(rng, parts)[partner]
    strong = (owner == chosen) | (owner == (partner + parts // 2) % parts)
    return jnp.where(strong, factor * result, result)


def steps_of(own_key, extent, shards, smallest, largest):
    level, own = 1.0, jax.random.fold_in(own_key, 6)
    for axis_at, blocks in shards:
        steps = jnp.exp(jax.random.uniform(jax.random.fold_in(own, axis_at), (blocks,), jnp.float32, smallest / len(shards), largest / len(shards)))
        level = level * jnp.repeat(steps, extent[axis_at] // blocks).reshape([-1 if axis == axis_at else 1 for axis in range(len(extent))])
    return level


def noise(own_key, shape, scale, limit, pieces=(), held_as=jnp.bfloat16):
    result = jax.random.normal(own_key, shape, jnp.float32) * scale
    if len(pieces) > 0:
        result = steps_of(own_key, shape, pieces, -0.22, 0.18) * result
    return jnp.clip(result, min=-limit, max=limit).astype(held_as)


def noise_with(own_key, extent, scale, bound, split, heavy, dtype=jnp.bfloat16):
    values = scale * jax.random.normal(own_key, extent, jnp.float32)
    if split:
        values = values * steps_of(own_key, extent, split, -0.22, 0.18)
    return jnp.clip(spiked(values, jax.random.fold_in(own_key, 3), *heavy), -bound, bound).astype(dtype)


def setup_inputs(seed: int = 0) -> dict:
    streams_of = jax.random.split(jax.random.key(seed), 9)
    return {
        "c3": noise_with(streams_of[0], (IMAGES, H3, W3, C3CH), 1.0, 6.0, ((0, 16), (1, 16), (2, 2)), (0, 3, 16, 2.0)),
        "c4": noise_with(streams_of[1], (IMAGES, H4, W4, C4CH), 1.0, 6.0, ((0, 16), (1, 16), (2, 2)), (0, 3, 16, 2.0)),
        "top_down": noise(streams_of[2], (IMAGES, H5, W5, CH), 1.0, 6.0, ((0, 16), (1, 16), (2, 2))),
        "lat3_weight": noise(streams_of[3], (C3CH, CH), C3CH ** -0.5, 0.25),
        "lat4_weight": noise(streams_of[4], (C4CH, CH), C4CH ** -0.5, 0.1875),
        "conv_weight": noise(streams_of[5], (9 * CH, CH), (9 * CH) ** -0.5, 0.125),
        "p3_cot": noise(streams_of[6], (IMAGES, H3, W3, CH), 1.0, 6.0, ((0, 16), (1, 16), (2, 2))),
        "m4_cot": noise(streams_of[7], (IMAGES, H4, W4, CH), 1.0, 6.0, ((0, 16), (1, 16), (2, 2))),
    }


def upsample(field):
    return jnp.repeat(jnp.repeat(field, 2, axis=0), 2, axis=1)

def downsum(field):
    height, width, depth = field.shape
    return field.reshape(height // 2, 2, width // 2, 2, depth).sum(axis=(1, 3))

def one_image(c3, c4, top_down, p3_cot, m4_cot, lat3_weight, lat4_weight, conv_weight):
    c3_flat = c3.reshape(-1, C3CH)
    c4_flat = c4.reshape(-1, C4CH)
    lat4 = jnp.dot(c4_flat, lat4_weight, preferred_element_type=jnp.float32).reshape(H4, W4, CH)
    m4 = lat4 + upsample(top_down.astype(jnp.float32))
    lat3 = jnp.dot(c3_flat, lat3_weight, preferred_element_type=jnp.float32).reshape(H3, W3, CH)
    m3 = (lat3 + upsample(m4)).astype(jnp.bfloat16)
    padded = jnp.pad(m3, ((1, 1), (1, 1), (0, 0)))
    patches = jnp.concatenate([padded[a:a + H3, b:b + W3, :] for a in range(3) for b in range(3)], axis=-1).reshape(-1, 9 * CH)
    p3 = jnp.dot(patches, conv_weight, preferred_element_type=jnp.float32).astype(jnp.bfloat16)
    cot_pad = jnp.pad(p3_cot, ((1, 1), (1, 1), (0, 0)))
    cot_patches = jnp.concatenate([cot_pad[2 - a:2 - a + H3, 2 - b:2 - b + W3, :] for a in range(3) for b in range(3)], axis=-1).reshape(-1, 9 * CH)
    flipped = conv_weight.reshape(9, CH, CH).transpose(0, 2, 1).reshape(9 * CH, CH)
    m3_grad = jnp.dot(cot_patches, flipped, preferred_element_type=jnp.float32)
    m3_grad_b = m3_grad.astype(jnp.bfloat16)
    c3_grad = jnp.dot(m3_grad_b, lat3_weight.T, preferred_element_type=jnp.float32).astype(jnp.bfloat16)
    m4_grad = m4_cot.astype(jnp.float32) + downsum(m3_grad.reshape(H3, W3, CH))
    m4_grad_b = m4_grad.astype(jnp.bfloat16).reshape(-1, CH)
    c4_grad = jnp.dot(m4_grad_b, lat4_weight.T, preferred_element_type=jnp.float32).astype(jnp.bfloat16)
    top_grad = downsum(m4_grad).astype(jnp.bfloat16)
    grad3 = jnp.dot(c3_flat.T, m3_grad_b, preferred_element_type=jnp.float32)
    grad4 = jnp.dot(c4_flat.T, m4_grad_b, preferred_element_type=jnp.float32)
    gradc = jnp.dot(patches.T, p3_cot.reshape(-1, CH), preferred_element_type=jnp.float32)
    term = jnp.concatenate([grad3, grad4, gradc], axis=0)
    return (p3.reshape(H3, W3, CH), c3_grad.reshape(H3, W3, C3CH), c4_grad.reshape(H4, W4, C4CH), top_grad, term)

def reference(c3, c4, top_down, lat3_weight, lat4_weight, conv_weight, p3_cot, m4_cot):
    scale = 1.0 / math.sqrt(IMAGES * H3 * W3)

    def step(total, items):
        p3, c3_grad, c4_grad, top_grad, term = one_image(items[0], items[1], items[2], items[3], items[4], lat3_weight, lat4_weight, conv_weight)
        return (total + term * scale, (p3, c3_grad, c4_grad, top_grad))
    start = jnp.zeros((GROWS, CH), jnp.float32)
    total, outputs = lax.scan(step, start, (c3, c4, top_down, p3_cot, m4_cot))
    return (outputs[0], outputs[1], outputs[2], outputs[3], total)
```

```python
import functools
import math

import jax
import jax.numpy as jnp
from jax import lax
from jax.experimental import pallas as pl
from jax.experimental.pallas import tpu as pltpu
from jax.sharding import PartitionSpec as P

F32 = jnp.float32
BF16 = jnp.bfloat16
ROWS = ("x", "z_hi")
LIMIT = 32 * 1024 * 1024
NT = (((1,), (1,)), ((), ()))
TN = (((0,), (0,)), ((), ()))


def dot(lhs, rhs, dims=(((1,), (0,)), ((), ()))):
    return lax.dot_general(lhs, rhs, dims, preferred_element_type=F32)


def call(kernel, out_shape, scratch, flops, moved, *args):
    in_vmem = pl.BlockSpec(memory_space=pltpu.VMEM)
    return pl.pallas_call(
        kernel,
        out_shape=out_shape,
        in_specs=[in_vmem] * len(args),
        out_specs=[in_vmem] * len(out_shape),
        scratch_shapes=scratch,
        compiler_params=pltpu.CompilerParams(vmem_limit_bytes=LIMIT),
        cost_estimate=pl.CostEstimate(flops=flops, bytes_accessed=moved, transcendentals=0),
    )(*args)


def merge_kernel(width4, c3, c4, top, lat3, lat4, m3, up4):
    n4, n5 = c4.shape[0], top.shape[0]
    n3 = c3.shape[0]
    width3, width5 = 2 * width4, width4 // 2
    row = lax.broadcasted_iota(jnp.int32, (n4, n5), 0)
    col = lax.broadcasted_iota(jnp.int32, (n4, n5), 1)
    source = (row // width4 // 2) * width5 + (row % width4) // 2
    pick = jnp.where(source == col, 1.0, 0.0).astype(BF16)
    m4 = dot(c4[...], lat4[...]) + dot(pick, top[...])
    up4[0, pl.ds(0, n4, stride=2), :] = m4[:, :128]
    up4[0, pl.ds(1, n4, stride=2), :] = m4[:, :128]
    up4[1, pl.ds(0, n4, stride=2), :] = m4[:, 128:]
    up4[1, pl.ds(1, n4, stride=2), :] = m4[:, 128:]
    lat = dot(c3[...], lat3[...])
    for y in range(n3 // width3):
        rows = slice(y * width3, (y + 1) * width3)
        above = slice((y // 2) * width3, (y // 2 + 1) * width3)
        m3[rows, :128] = (lat[rows, :128] + up4[0, above]).astype(BF16)
        m3[rows, 128:] = (lat[rows, 128:] + up4[1, above]).astype(BF16)


def fill_shifted(own, before, after, left, right, shifted, width):
    n = own.shape[0]
    shifted[1, 0:width] = before[...]
    shifted[1, width : width + n] = own[...]
    shifted[1, width + n :] = after[...]
    at = lax.broadcasted_iota(jnp.int32, (width, own.shape[1]), 0)
    for y in range(n // width + 2):
        rows = slice(y * width, (y + 1) * width)
        line = shifted[1, rows].astype(F32)
        to_left = pltpu.roll(line, 1, 0)
        to_right = pltpu.roll(line, width - 1, 0)
        shifted[0, rows] = jnp.where(at == 0, left[y : y + 1, :], to_left).astype(BF16)
        shifted[2, rows] = jnp.where(at == width - 1, right[y : y + 1, :], to_right).astype(BF16)


def pieces_of(block, each):
    per = each // 16
    return block // per // 2, (block // per) % 2, block % per


def grads_kernel(
    width, each, scale, core, cot, before, after, left, right, m3, c3, c4, conv, m4_cot,
    m3_grad_b, m4_grad_b, top_grad, term, shifted, sums, sums5,
):
    n3, chans = cot.shape
    n4 = c4.shape[0]
    me = core[0]
    per = each // 16

    def put(first, value):
        value = (value * scale).astype(BF16)
        for k in range(value.shape[0] // 16):
            y, owner, r = pieces_of(first // 16 + k, each)
            slot = jnp.where(me == owner, 0, 1)
            for h in range(2):
                p = h * 16 + r
                x, z_hi, z_lo = p // 8, (p // 2) % 4, p % 2
                term[slot, x * 2 + z_lo, y * 4 + z_hi] = value[
                    16 * k : 16 * k + 16, 128 * h : 128 * h + 128
                ]

    blank = jnp.zeros((16, 128), BF16)
    for y in range(8):
        for r in range(per, 16):
            for h in range(2):
                p = h * 16 + r
                x, z_hi, z_lo = p // 8, (p // 2) % 4, p % 2
                for slot in range(2):
                    term[slot, x * 2 + z_lo, y * 4 + z_hi] = blank

    fill_shifted(cot, before, after, left, right, shifted, width)

    def cot_at(a, b):
        return shifted[2 - b, (2 - a) * width : (2 - a) * width + n3]

    total = None
    for a in range(3):
        for b in range(3):
            tap = 3 * a + b
            weight = conv[tap * chans : (tap + 1) * chans]
            part = dot(cot_at(a, b), weight, NT)
            total = part if total is None else total + part
    m3_grad_b[...] = total.astype(BF16)
    for y in range(n4 // (width // 2)):
        pair = total[2 * y * width : (2 * y + 1) * width] + total[(2 * y + 1) * width : (2 * y + 2) * width]
        sums[0, y * width : (y + 1) * width] = pair[:, :128]
        sums[1, y * width : (y + 1) * width] = pair[:, 128:]
    for h in range(2):
        cols = slice(128 * h, 128 * h + 128)
        m4_grad = (
            m4_cot[:, cols].astype(F32)
            + sums[h, pl.ds(0, n4, stride=2), :]
            + sums[h, pl.ds(1, n4, stride=2), :]
        )
        m4_grad_b[:, cols] = m4_grad.astype(BF16)
        half = width // 2
        for y in range(n4 // width):
            sums5[h, y * half : (y + 1) * half] = (
                m4_grad[2 * y * half : (2 * y + 1) * half]
                + m4_grad[(2 * y + 1) * half : (2 * y + 2) * half]
            )
        n5 = n4 // 4
        top_grad[:, cols] = (
            sums5[h, pl.ds(0, n5, stride=2), :] + sums5[h, pl.ds(1, n5, stride=2), :]
        ).astype(BF16)

    depth3, depth4 = c3.shape[1], c4.shape[1]
    put(0, dot(c3[...], m3_grad_b[...], TN))
    put(depth3, dot(c4[...], m4_grad_b[...], TN))
    m3_t = m3[...].T
    for a in range(3):
        for b in range(3):
            tap = 3 * a + b
            put(depth3 + depth4 + tap * chans, dot(m3_t, cot_at(a, b)))


def outputs_kernel(
    width, m3, before, after, left, right, conv, m3_grad_b, lat3, m4_grad_b, lat4,
    p3, c3_grad, c4_grad, shifted,
):
    n3, chans = m3.shape
    fill_shifted(m3, before, after, left, right, shifted, width)
    total = None
    for a in range(3):
        for b in range(3):
            tap = 3 * a + b
            part = dot(shifted[b, a * width : a * width + n3], conv[tap * chans : (tap + 1) * chans])
            total = part if total is None else total + part
    p3[...] = total.astype(BF16)
    c3_grad[...] = dot(m3_grad_b[...], lat3[...], NT).astype(BF16)
    c4_grad[...] = dot(m4_grad_b[...], lat4[...], NT).astype(BF16)


def run_grads(width, each, scale, core, cot, cot_borders, m3, c3, c4, conv, m4_cot):
    n3, chans = cot.shape
    n4 = c4.shape[0]
    depth = c3.shape[1] + c4.shape[1] + conv.shape[0]
    in_vmem = pl.BlockSpec(memory_space=pltpu.VMEM)
    return pl.pallas_call(
        functools.partial(grads_kernel, width, each, scale),
        out_shape=[
            jax.ShapeDtypeStruct((n3, chans), BF16),
            jax.ShapeDtypeStruct((n4, chans), BF16),
            jax.ShapeDtypeStruct((n4 // 4, chans), BF16),
            jax.ShapeDtypeStruct((2, 8, 32, 16, 128), BF16),
        ],
        in_specs=[pl.BlockSpec(memory_space=pltpu.SMEM)] + [in_vmem] * 10,
        out_specs=[in_vmem] * 4,
        scratch_shapes=[
            pltpu.VMEM((3, n3 + 2 * width, chans), BF16),
            pltpu.VMEM((2, n3 // 2, 128), F32),
            pltpu.VMEM((2, n4 // 2, 128), F32),
        ],
        compiler_params=pltpu.CompilerParams(vmem_limit_bytes=LIMIT),
        cost_estimate=pl.CostEstimate(
            flops=2 * chans * (n3 * c3.shape[1] + n4 * c4.shape[1] + 18 * n3 * chans),
            bytes_accessed=2 * (n3 * c3.shape[1] + n4 * c4.shape[1] + 2 * depth * chans),
            transcendentals=0,
        ),
    )(core, cot, *cot_borders, m3, c3, c4, conv, m4_cot)


def run_outputs(width, m3, m3_borders, conv, m3_grad_b, lat3, m4_grad_b, lat4):
    n3, chans = m3.shape
    n4 = m4_grad_b.shape[0]
    depth3, depth4 = lat3.shape[0], lat4.shape[0]
    return call(
        functools.partial(outputs_kernel, width),
        [
            jax.ShapeDtypeStruct((n3, chans), BF16),
            jax.ShapeDtypeStruct((n3, depth3), BF16),
            jax.ShapeDtypeStruct((n4, depth4), BF16),
        ],
        [pltpu.VMEM((3, n3 + 2 * width, chans), BF16)],
        2 * chans * (n3 * depth3 + n4 * depth4 + 9 * n3 * chans),
        4 * (n3 * depth3 + n4 * depth4 + 9 * chans * chans),
        m3, *m3_borders, conv, m3_grad_b, lat3, m4_grad_b, lat4,
    )


def borders(tile):
    height, width, chans = tile.shape
    z_lo = lax.axis_index("z_lo")
    col = jnp.where(z_lo == 0, tile[:, -1], tile[:, 0])
    col = lax.ppermute(col, "z_lo", [(0, 1), (1, 0)])
    n_rows = lax.axis_size(ROWS)
    odd = lax.axis_index(ROWS) % 2 == 1
    pad = jnp.zeros((15, chans), tile.dtype)
    top = jnp.concatenate([tile[0], col[:1], pad], axis=0)
    bottom = jnp.concatenate([tile[-1], col[-1:], pad], axis=0)
    pairs = [(i, i + 1) for i in range(0, n_rows - 1, 2)]
    between = [(i, i + 1) for i in range(1, n_rows - 1, 2)]
    first = lax.ppermute(jnp.where(odd, top, bottom), ROWS, pairs + [(j, i) for i, j in pairs])
    second = lax.ppermute(
        jnp.where(odd, bottom, top), ROWS, between + [(j, i) for i, j in between]
    )
    before = jnp.where(odd, first, second)
    after = jnp.where(odd, second, first)
    sides = jnp.concatenate([before[width : width + 1], col, after[width : width + 1]], axis=0)
    sides = jnp.concatenate([sides, pad[: 14 - height]], axis=0).astype(F32)
    left = jnp.where(z_lo == 1, sides, 0.0)
    right = jnp.where(z_lo == 0, sides, 0.0)
    return before[:width], after[:width], left, right


def add_up(parts):
    return parts.astype(F32).sum(axis=0).astype(BF16)


def add_cores(term):
    got = lax.ppermute(term[1], "core", [(0, 1), (1, 0)])
    return (term[0].astype(F32) + got.astype(F32)).astype(BF16)


def reduce_grads(part):
    part = add_up(lax.all_to_all(part, ("x", "z_lo"), 0, 0, tiled=True))
    return add_up(lax.all_to_all(part, ("y", "z_hi"), 0, 0, tiled=True))


def share_grads(part, each):
    everywhere = ("x", "z_hi", "z_lo")
    n = lax.axis_size(everywhere)
    part = jnp.broadcast_to(part[None], (n,) + part.shape)
    part = lax.all_to_all(part, everywhere, 0, 0, tiled=True)
    halves = part.reshape(2, -1, part.shape[-1])[:, :each].astype(F32)
    return jnp.concatenate([halves[0], halves[1]], axis=1)


def shards(c3, c4, top_down, lat3_weight, lat4_weight, conv_weight, p3_cot, m4_cot):
    count, height, width, depth3 = c3.shape
    depth4 = c4.shape[3]
    chans = conv_weight.shape[1]
    n3 = height * width
    n4 = n3 // 4
    n5 = n4 // 4
    c3_flat = c3.reshape(n3, depth3)
    c4_flat = c4.reshape(n4, depth4)
    stacked = depth3 + depth4 + 9 * chans
    each = stacked // lax.axis_size(("y", "core"))
    total_pixels = n3 * lax.axis_size(("y", "core", "x", "z_hi", "z_lo"))
    scale = 1.0 / math.sqrt(total_pixels)

    cot_borders = borders(p3_cot[0])
    (m3,) = call(
        functools.partial(merge_kernel, width // 2),
        [jax.ShapeDtypeStruct((n3, chans), BF16)],
        [pltpu.VMEM((2, 2 * n4, 128), F32)],
        2 * chans * (n3 * depth3 + n4 * depth4),
        2 * (n3 * depth3 + n4 * depth4 + chans * (depth3 + depth4 + n3)),
        c3_flat, c4_flat, top_down.reshape(n5, chans), lat3_weight, lat4_weight,
    )
    core = lax.axis_index("core").astype(jnp.int32).reshape(1)
    m3_grad_b, m4_grad_b, top_grad, term = run_grads(
        width, each, scale, core, p3_cot.reshape(n3, chans), cot_borders, m3, c3_flat, c4_flat,
        conv_weight, m4_cot.reshape(n4, chans),
    )
    part = add_cores(term)
    part, m3 = lax.optimization_barrier((part, m3))
    weight_grads = share_grads(reduce_grads(part), each)
    m3_borders = borders(m3.reshape(height, width, chans))
    p3, c3_grad, c4_grad = run_outputs(
        width, m3, m3_borders, conv_weight, m3_grad_b, lat3_weight, m4_grad_b, lat4_weight
    )
    return (
        p3.reshape(count, height, width, chans),
        c3_grad.reshape(count, height, width, depth3),
        c4_grad.reshape(count, height // 2, width // 2, depth4),
        top_grad.reshape(top_down.shape),
        weight_grads,
    )


def solution(mesh):
    split = jax.sharding.Mesh(
        mesh.devices.reshape(8, 2, 4, 4, 2), ("y", "core", "x", "z_hi", "z_lo")
    )
    tiles = P(("y", "core"), ("x", "z_hi"), "z_lo", None)
    return jax.shard_map(
        shards,
        mesh=split,
        in_specs=(tiles, tiles, tiles, P(), P(), P(), tiles, tiles),
        out_specs=(tiles, tiles, tiles, tiles, P(("y", "core"), None)),
        check_vma=False,
    )
```

```python
import functools
import math

import jax
import jax.numpy as jnp
from jax import lax
from jax.experimental import pallas as pl
from jax.experimental.pallas import tpu as pltpu
from jax.sharding import PartitionSpec as P

F32 = jnp.float32
BF16 = jnp.bfloat16
ROWS = ("x_hi", "x_lo", "z_hi")
NEAR = ("x_lo", "y_lo", "z_lo")
FAR = ("x_hi", "y_hi", "z_hi")
SHARED = ("x_hi", "x_lo", "z_hi", "z_lo")
LIMIT = 32 * 1024 * 1024
NT = (((1,), (1,)), ((), ()))
TN = (((0,), (0,)), ((), ()))


def dot(lhs, rhs, dims=(((1,), (0,)), ((), ()))):
    return lax.dot_general(lhs, rhs, dims, preferred_element_type=F32)


def place_of_device():
    return lax.axis_index("core"), lax.axis_index("z_lo"), lax.axis_index("z_hi") % 2


def call(kernel, out_shape, scratch, flops, moved, fetched, held=()):
    in_vmem = pl.BlockSpec(memory_space=pltpu.VMEM)
    n, m, k = len(fetched), len(held), len(out_shape)

    def body(*refs):
        sources, refs = refs[:n], refs[n:]
        held_refs, refs = refs[:m], refs[m:]
        outs, refs = refs[:k], refs[k:]
        arrived, refs = refs[:n], refs[n:]
        if n == 0:
            kernel(place_of_device(), *held_refs, *outs, *refs)
            return
        copies = [
            pltpu.make_async_copy(source, target, refs[0].at[i])
            for i, (source, target) in enumerate(zip(sources, arrived))
        ]
        for copy in copies:
            copy.start()
        waits = [copy.wait for copy in copies]
        kernel(place_of_device(), waits, *arrived, *held_refs, *outs, *refs[1:])

    return pl.pallas_call(
        body,
        out_shape=list(out_shape) + [jax.ShapeDtypeStruct(x.shape, x.dtype) for x in fetched],
        in_specs=[pl.BlockSpec(memory_space=pltpu.HBM)] * n + [in_vmem] * m,
        out_specs=[in_vmem] * (k + n),
        scratch_shapes=([pltpu.SemaphoreType.DMA((n,))] if n else []) + scratch,
        compiler_params=pltpu.CompilerParams(vmem_limit_bytes=LIMIT),
        cost_estimate=pl.CostEstimate(flops=flops, bytes_accessed=moved, transcendentals=0),
    )(*[pltpu.with_memory_space_constraint(x, pltpu.HBM) for x in fetched], *held)


def merge_kernel(
    width4, place, waits, c4, lat4, top, c3, lat3, cot, conv, m4_cot,
    m3, col, row_a, row_b, up4,
):
    n4, n5 = c4.shape[0], top.shape[0]
    n3 = c3.shape[0]
    width3, width5 = 2 * width4, width4 // 2
    row = lax.broadcasted_iota(jnp.int32, (n4, n5), 0)
    at = lax.broadcasted_iota(jnp.int32, (n4, n5), 1)
    source = (row // width4 // 2) * width5 + (row % width4) // 2
    pick = jnp.where(source == at, 1.0, 0.0).astype(BF16)
    for wait in waits[:3]:
        wait()
    m4 = dot(c4[...], lat4[...]) + dot(pick, top[...])
    for h in range(2):
        half = m4[:, 128 * h : 128 * h + 128]
        up4[h, pl.ds(0, n4, stride=2), :] = half
        up4[h, pl.ds(1, n4, stride=2), :] = half
    for wait in waits[3:5]:
        wait()
    lat = dot(c3[...], lat3[...])
    for y in range(n3 // width3):
        rows = slice(y * width3, (y + 1) * width3)
        above = slice((y // 2) * width3, (y // 2 + 1) * width3)
        for h in range(2):
            cols = slice(128 * h, 128 * h + 128)
            m3[rows, cols] = (lat[rows, cols] + up4[h, above]).astype(BF16)
    waits[5]()
    edge = jnp.where(place[1] == 0, width3 - 1, 0)
    lines = n3 // width3
    row = lax.broadcasted_iota(jnp.int32, (2 * lines, n3), 0)
    at = lax.broadcasted_iota(jnp.int32, (2 * lines, n3), 1)
    take_cot = jnp.where(at == row * width3 + edge, 1.0, 0.0).astype(BF16)
    take_m3 = jnp.where(at == (row - lines) * width3 + edge, 1.0, 0.0).astype(BF16)
    col[...] = (dot(take_cot, cot[...]) + dot(take_m3, m3[...])).astype(BF16)
    odd = place[2] == 1
    first = pl.multiple_of(jnp.where(odd, 0, n3 - width3), width3)
    second = pl.multiple_of(jnp.where(odd, n3 - width3, 0), width3)
    for start, out in ((first, row_a), (second, row_b)):
        out[:width3] = cot[pl.ds(start, width3)]
        out[width3 : 2 * width3] = m3[pl.ds(start, width3)]
        out[2 * width3 :] = jnp.zeros((2 * lines, out.shape[1]), BF16)
    for wait in waits[6:]:
        wait()


def fill_shifted(place, field, own, row_a, row_b, col, shifted, width):
    n, chans = own.shape
    lines = n // width
    z_lo, odd = place[1], place[2] == 1
    rows = slice(field * width, (field + 1) * width)
    corner = slice(2 * width, 2 * width + 2 * lines)
    line_a, line_b = row_a[rows].astype(F32), row_b[rows].astype(F32)
    ends_a, ends_b = row_a[corner].astype(F32), row_b[corner].astype(F32)
    first, last = field * lines, (field + 1) * lines - 1
    sides = col[...].astype(F32)
    before = jnp.where(odd, ends_a, ends_b)[last : last + 1]
    after = jnp.where(odd, ends_b, ends_a)[first : first + 1]
    sides = [before] + [sides[first + y : first + y + 1] for y in range(lines)] + [after]
    at = lax.broadcasted_iota(jnp.int32, (width, chans), 0)
    to_the_left = jnp.where(z_lo == 1, 1.0, 0.0)
    to_the_right = 1.0 - to_the_left
    for y in range(lines + 2):
        if y == 0:
            line = jnp.where(odd, line_a, line_b)
            shifted[1, :width] = line.astype(BF16)
        elif y == lines + 1:
            line = jnp.where(odd, line_b, line_a)
            shifted[1, y * width :] = line.astype(BF16)
        else:
            line = own[(y - 1) * width : y * width]
            shifted[1, y * width : (y + 1) * width] = line
            line = line.astype(F32)
        rows = slice(y * width, (y + 1) * width)
        left, right = sides[y] * to_the_left, sides[y] * to_the_right
        shifted[0, rows] = jnp.where(at == 0, left, pltpu.roll(line, 1, 0)).astype(BF16)
        shifted[2, rows] = jnp.where(
            at == width - 1, right, pltpu.roll(line, width - 1, 0)
        ).astype(BF16)


def pieces_of(block, each):
    per = each // 16
    return block // per // 2, (block // per) % 2, block % per


def groups_of(y, piece):
    x, z_hi, z_lo = piece // 8, (piece // 2) % 4, piece % 2
    return (x % 2) * 4 + (y % 2) * 2 + z_lo, (x // 2) * 16 + (y // 2) * 4 + z_hi


def grads_kernel(
    width, each, scale, place, cot, conv, m4_cot, c3, c4, m3, row_a, row_b, col,
    m3_grad_b, m4_grad_b, top_grad, term, shifted, sums, sums5,
):
    n3, chans = cot.shape
    n4 = c4.shape[0]
    me = place[0]
    per = each // 16

    def put(first, value):
        value = (value * scale).astype(BF16)
        for k in range(value.shape[0] // 16):
            y, owner, r = pieces_of(first // 16 + k, each)
            slot = jnp.where(me == owner, 0, 1)
            for h in range(2):
                near, far = groups_of(y, h * 16 + r)
                term[slot, near, far] = value[16 * k : 16 * k + 16, 128 * h : 128 * h + 128]

    blank = jnp.zeros((16, 128), BF16)
    for y in range(8):
        for r in range(per, 16):
            for h in range(2):
                near, far = groups_of(y, h * 16 + r)
                for slot in range(2):
                    term[slot, near, far] = blank

    fill_shifted(place, 0, cot, row_a, row_b, col, shifted, width)

    def cot_at(a, b):
        return shifted[2 - b, (2 - a) * width : (2 - a) * width + n3]

    total = None
    for a in range(3):
        for b in range(3):
            tap = 3 * a + b
            weight = conv[tap * chans : (tap + 1) * chans]
            part = dot(cot_at(a, b), weight, NT)
            total = part if total is None else total + part
    m3_grad_b[...] = total.astype(BF16)
    for y in range(n4 // (width // 2)):
        pair = total[2 * y * width : (2 * y + 1) * width] + total[(2 * y + 1) * width : (2 * y + 2) * width]
        sums[0, y * width : (y + 1) * width] = pair[:, :128]
        sums[1, y * width : (y + 1) * width] = pair[:, 128:]
    for h in range(2):
        cols = slice(128 * h, 128 * h + 128)
        m4_grad = (
            m4_cot[:, cols].astype(F32)
            + sums[h, pl.ds(0, n4, stride=2), :]
            + sums[h, pl.ds(1, n4, stride=2), :]
        )
        m4_grad_b[:, cols] = m4_grad.astype(BF16)
        half = width // 2
        for y in range(n4 // width):
            sums5[h, y * half : (y + 1) * half] = (
                m4_grad[2 * y * half : (2 * y + 1) * half]
                + m4_grad[(2 * y + 1) * half : (2 * y + 2) * half]
            )
        n5 = n4 // 4
        top_grad[:, cols] = (
            sums5[h, pl.ds(0, n5, stride=2), :] + sums5[h, pl.ds(1, n5, stride=2), :]
        ).astype(BF16)

    depth3, depth4 = c3.shape[1], c4.shape[1]
    put(0, dot(c3[...], m3_grad_b[...], TN))
    put(depth3, dot(c4[...], m4_grad_b[...], TN))
    m3_t = m3[...].T
    for a in range(3):
        for b in range(3):
            tap = 3 * a + b
            put(depth3 + depth4 + tap * chans, dot(m3_t, cot_at(a, b)))


def outputs_kernel(
    width, place, conv, lat3, lat4, m3, row_a, row_b, col, m3_grad_b, m4_grad_b,
    p3, c3_grad, c4_grad, shifted,
):
    n3, chans = m3.shape
    fill_shifted(place, 1, m3, row_a, row_b, col, shifted, width)
    total = None
    for a in range(3):
        for b in range(3):
            tap = 3 * a + b
            part = dot(shifted[b, a * width : a * width + n3], conv[tap * chans : (tap + 1) * chans])
            total = part if total is None else total + part
    p3[...] = total.astype(BF16)
    c3_grad[...] = dot(m3_grad_b[...], lat3[...], NT).astype(BF16)
    c4_grad[...] = dot(m4_grad_b[...], lat4[...], NT).astype(BF16)


def shape_of(*dims):
    return jax.ShapeDtypeStruct(dims, BF16)


def run_merge(width, c3, c4, top, lat3, lat4, cot, conv, m4_cot):
    n3, n4, chans = c3.shape[0], c4.shape[0], lat3.shape[1]
    lines = n3 // width
    border = shape_of(2 * width + 2 * lines, chans)
    return call(
        functools.partial(merge_kernel, width // 2),
        [shape_of(n3, chans), shape_of(2 * lines, chans), border, border],
        [pltpu.VMEM((2, 2 * n4, 128), F32)],
        2 * chans * (c3.size + c4.size),
        2 * (c3.size + c4.size + lat3.size + lat4.size + 2 * cot.size + conv.size),
        (c4, lat4, top, c3, lat3, cot, conv, m4_cot),
    )


def run_grads(width, each, scale, cot, conv, m4_cot, c3, c4, m3, row_a, row_b, col):
    n3, chans = cot.shape
    n4 = c4.shape[0]
    return call(
        functools.partial(grads_kernel, width, each, scale),
        [
            shape_of(n3, chans),
            shape_of(n4, chans),
            shape_of(n4 // 4, chans),
            shape_of(2, 8, 32, 16, 128),
        ],
        [
            pltpu.VMEM((3, n3 + 2 * width, chans), BF16),
            pltpu.VMEM((2, n3 // 2, 128), F32),
            pltpu.VMEM((2, n4 // 2, 128), F32),
        ],
        2 * chans * (c3.size + c4.size + 2 * 9 * n3 * chans),
        2 * (c3.size + c4.size + 2 * conv.size),
        (),
        (cot, conv, m4_cot, c3, c4, m3, row_a, row_b, col),
    )


def run_outputs(width, conv, lat3, lat4, m3, row_a, row_b, col, m3_grad_b, m4_grad_b):
    n3, chans = m3.shape
    n4 = m4_grad_b.shape[0]
    return call(
        functools.partial(outputs_kernel, width),
        [shape_of(n3, chans), shape_of(n3, lat3.shape[0]), shape_of(n4, lat4.shape[0])],
        [pltpu.VMEM((3, n3 + 2 * width, chans), BF16)],
        2 * chans * (n3 * lat3.shape[0] + n4 * lat4.shape[0] + 9 * n3 * chans),
        4 * (n3 * lat3.shape[0] + n4 * lat4.shape[0] + conv.size),
        (),
        (conv, lat3, lat4, m3, row_a, row_b, col, m3_grad_b, m4_grad_b),
    )


def swap_borders(col, row_a, row_b):
    col = lax.ppermute(col, "z_lo", [(0, 1), (1, 0)])
    n_rows = lax.axis_size(ROWS)
    pairs = [(i, i + 1) for i in range(0, n_rows - 1, 2)]
    between = [(i, i + 1) for i in range(1, n_rows - 1, 2)]
    start = (row_a.shape[0] - col.shape[0], 0)
    row_a = lax.dynamic_update_slice(row_a, col, start)
    row_b = lax.dynamic_update_slice(row_b, col, start)
    row_a = lax.ppermute(row_a, ROWS, pairs + [(j, i) for i, j in pairs])
    row_b = lax.ppermute(row_b, ROWS, between + [(j, i) for i, j in between])
    return row_a, row_b, col


def add_kernel(count, *refs):
    parts, out = refs[:-1], refs[-1]
    total = None
    for part in parts:
        for i in range(part.shape[0]):
            value = part[i].astype(F32)
            total = value if total is None else total + value
    total = total.astype(BF16)
    if count is None:
        out[...] = total
    else:
        for i in range(count):
            out[i] = total


def add_up(*parts, count=None):
    shape = parts[0].shape[1:]
    in_vmem = pl.BlockSpec(memory_space=pltpu.VMEM)
    return pl.pallas_call(
        functools.partial(add_kernel, count),
        out_shape=shape_of(*shape) if count is None else shape_of(count, *shape),
        in_specs=[in_vmem] * len(parts),
        out_specs=in_vmem,
        compiler_params=pltpu.CompilerParams(vmem_limit_bytes=LIMIT),
        cost_estimate=pl.CostEstimate(
            flops=sum(p.size for p in parts),
            bytes_accessed=2 * sum(p.size for p in parts),
            transcendentals=0,
        ),
    )(*parts)


def add_grads(term, each):
    _, near, far, rows, cols = term.shape
    got = lax.ppermute(term[1], "core", [(0, 1), (1, 0)])
    part = add_up(term[:1].reshape(1, -1, cols), got.reshape(1, -1, cols))
    part = lax.all_to_all(part.reshape(near, far * rows, cols), NEAR, 0, 0, tiled=True)
    part = add_up(part)
    part = lax.all_to_all(part.reshape(far, rows, cols), FAR, 0, 0, tiled=True)
    part = add_up(part, count=lax.axis_size(SHARED))
    part = lax.all_to_all(part, SHARED, 0, 0, tiled=True)
    halves = part.reshape(2, -1, cols)[:, :each].astype(F32)
    return jnp.concatenate([halves[0], halves[1]], axis=1)


def shards(c3, c4, top_down, lat3_weight, lat4_weight, conv_weight, p3_cot, m4_cot):
    count, height, width, depth3 = c3.shape
    depth4 = c4.shape[3]
    chans = conv_weight.shape[1]
    n3 = height * width
    n4 = n3 // 4
    n5 = n4 // 4
    stacked = depth3 + depth4 + 9 * chans
    owners = lax.axis_size(("y_hi", "y_lo", "core"))
    each = stacked // owners
    total_pixels = n3 * owners * lax.axis_size(SHARED)
    scale = 1.0 / math.sqrt(total_pixels)

    m3, col, row_a, row_b, *fetched = run_merge(
        width, c3.reshape(n3, depth3), c4.reshape(n4, depth4), top_down.reshape(n5, chans),
        lat3_weight, lat4_weight, p3_cot.reshape(n3, chans), conv_weight, m4_cot.reshape(n4, chans),
    )
    c4_v, lat4_v, _, c3_v, lat3_v, cot_v, conv_v, m4_cot_v = fetched
    borders = swap_borders(col, row_a, row_b)
    m3_grad_b, m4_grad_b, top_grad, term = run_grads(
        width, each, scale, cot_v, conv_v, m4_cot_v, c3_v, c4_v, m3, *borders
    )
    weight_grads = add_grads(term, each)
    p3, c3_grad, c4_grad = run_outputs(
        width, conv_v, lat3_v, lat4_v, m3, *borders, m3_grad_b, m4_grad_b
    )
    return (
        p3.reshape(count, height, width, chans),
        c3_grad.reshape(count, height, width, depth3),
        c4_grad.reshape(count, height // 2, width // 2, depth4),
        top_grad.reshape(top_down.shape),
        weight_grads,
    )


def solution(mesh):
    split = jax.sharding.Mesh(
        mesh.devices.reshape(4, 2, 2, 2, 2, 4, 2),
        ("y_hi", "y_lo", "core", "x_hi", "x_lo", "z_hi", "z_lo"),
    )
    owners = ("y_hi", "y_lo", "core")
    tiles = P(owners, ROWS, "z_lo", None)
    return jax.shard_map(
        shards,
        mesh=split,
        in_specs=(tiles, tiles, tiles, P(), P(), P(), tiles, tiles),
        out_specs=(tiles, tiles, tiles, tiles, P(owners, None)),
        check_vma=False,
    )
```

```python
import functools
import math

import jax
import jax.numpy as jnp
from jax import lax
from jax.experimental import pallas as pl
from jax.experimental.pallas import tpu as pltpu
from jax.sharding import PartitionSpec as P

F32 = jnp.float32
BF16 = jnp.bfloat16
ROWS = ("x", "z_hi")
OWNERS = ("y", "core")
SHARED = ("x", "z_hi", "z_lo")
SIZES = {"x": 4, "y": 8, "z": 8}
LIMIT = 32 * 1024 * 1024
NT = (((1,), (1,)), ((), ()))
TN = (((0,), (0,)), ((), ()))


def dot(lhs, rhs, dims=(((1,), (0,)), ((), ()))):
    return lax.dot_general(lhs, rhs, dims, preferred_element_type=F32)


def place_of_device():
    return lax.axis_index("core"), lax.axis_index("z_lo"), lax.axis_index("z_hi") % 2


def call(kernel, out_shape, scratch, flops, moved, fetched, held=()):
    in_vmem = pl.BlockSpec(memory_space=pltpu.VMEM)
    n, m, k = len(fetched), len(held), len(out_shape)

    def body(*refs):
        sources, refs = refs[:n], refs[n:]
        held_refs, refs = refs[:m], refs[m:]
        outs, refs = refs[:k], refs[k:]
        arrived, refs = refs[:n], refs[n:]
        if n == 0:
            kernel(place_of_device(), *held_refs, *outs, *refs)
            return
        copies = [
            pltpu.make_async_copy(source, target, refs[0].at[i])
            for i, (source, target) in enumerate(zip(sources, arrived))
        ]
        for copy in copies:
            copy.start()
        waits = [copy.wait for copy in copies]
        kernel(place_of_device(), waits, *arrived, *held_refs, *outs, *refs[1:])

    return pl.pallas_call(
        body,
        out_shape=list(out_shape) + [jax.ShapeDtypeStruct(x.shape, x.dtype) for x in fetched],
        in_specs=[pl.BlockSpec(memory_space=pltpu.HBM)] * n + [in_vmem] * m,
        out_specs=[in_vmem] * (k + n),
        scratch_shapes=([pltpu.SemaphoreType.DMA((n,))] if n else []) + scratch,
        compiler_params=pltpu.CompilerParams(vmem_limit_bytes=LIMIT),
        cost_estimate=pl.CostEstimate(flops=flops, bytes_accessed=moved, transcendentals=0),
    )(*[pltpu.with_memory_space_constraint(x, pltpu.HBM) for x in fetched], *held)


def merge_kernel(
    width4, place, waits, c4, lat4, top, c3, lat3, cot, conv, m4_cot,
    m3, col, row_a, row_b, up4,
):
    n4, n5 = c4.shape[0], top.shape[0]
    n3 = c3.shape[0]
    width3, width5 = 2 * width4, width4 // 2
    row = lax.broadcasted_iota(jnp.int32, (n4, n5), 0)
    at = lax.broadcasted_iota(jnp.int32, (n4, n5), 1)
    source = (row // width4 // 2) * width5 + (row % width4) // 2
    pick = jnp.where(source == at, 1.0, 0.0).astype(BF16)
    for wait in waits[:3]:
        wait()
    m4 = dot(c4[...], lat4[...]) + dot(pick, top[...])
    for h in range(2):
        half = m4[:, 128 * h : 128 * h + 128]
        up4[h, pl.ds(0, n4, stride=2), :] = half
        up4[h, pl.ds(1, n4, stride=2), :] = half
    for wait in waits[3:5]:
        wait()
    lat = dot(c3[...], lat3[...])
    for y in range(n3 // width3):
        rows = slice(y * width3, (y + 1) * width3)
        above = slice((y // 2) * width3, (y // 2 + 1) * width3)
        for h in range(2):
            cols = slice(128 * h, 128 * h + 128)
            m3[rows, cols] = (lat[rows, cols] + up4[h, above]).astype(BF16)
    waits[5]()
    edge = jnp.where(place[1] == 0, width3 - 1, 0)
    lines = n3 // width3
    row = lax.broadcasted_iota(jnp.int32, (2 * lines, n3), 0)
    at = lax.broadcasted_iota(jnp.int32, (2 * lines, n3), 1)
    take_cot = jnp.where(at == row * width3 + edge, 1.0, 0.0).astype(BF16)
    take_m3 = jnp.where(at == (row - lines) * width3 + edge, 1.0, 0.0).astype(BF16)
    col[...] = (dot(take_cot, cot[...]) + dot(take_m3, m3[...])).astype(BF16)
    odd = place[2] == 1
    first = pl.multiple_of(jnp.where(odd, 0, n3 - width3), width3)
    second = pl.multiple_of(jnp.where(odd, n3 - width3, 0), width3)
    for start, out in ((first, row_a), (second, row_b)):
        out[:width3] = cot[pl.ds(start, width3)]
        out[width3 : 2 * width3] = m3[pl.ds(start, width3)]
        out[2 * width3 :] = jnp.zeros((2 * lines, out.shape[1]), BF16)
    for wait in waits[6:]:
        wait()


def fill_shifted(place, field, own, row_a, row_b, col, shifted, width):
    n, chans = own.shape
    lines = n // width
    z_lo, odd = place[1], place[2] == 1
    rows = slice(field * width, (field + 1) * width)
    corner = slice(2 * width, 2 * width + 2 * lines)
    line_a, line_b = row_a[rows].astype(F32), row_b[rows].astype(F32)
    ends_a, ends_b = row_a[corner].astype(F32), row_b[corner].astype(F32)
    first, last = field * lines, (field + 1) * lines - 1
    sides = col[...].astype(F32)
    before = jnp.where(odd, ends_a, ends_b)[last : last + 1]
    after = jnp.where(odd, ends_b, ends_a)[first : first + 1]
    sides = [before] + [sides[first + y : first + y + 1] for y in range(lines)] + [after]
    at = lax.broadcasted_iota(jnp.int32, (width, chans), 0)
    to_the_left = jnp.where(z_lo == 1, 1.0, 0.0)
    to_the_right = 1.0 - to_the_left
    for y in range(lines + 2):
        if y == 0:
            line = jnp.where(odd, line_a, line_b)
            shifted[1, :width] = line.astype(BF16)
        elif y == lines + 1:
            line = jnp.where(odd, line_b, line_a)
            shifted[1, y * width :] = line.astype(BF16)
        else:
            line = own[(y - 1) * width : y * width]
            shifted[1, y * width : (y + 1) * width] = line
            line = line.astype(F32)
        rows = slice(y * width, (y + 1) * width)
        left, right = sides[y] * to_the_left, sides[y] * to_the_right
        shifted[0, rows] = jnp.where(at == 0, left, pltpu.roll(line, 1, 0)).astype(BF16)
        shifted[2, rows] = jnp.where(
            at == width - 1, right, pltpu.roll(line, width - 1, 0)
        ).astype(BF16)


def pieces_of(block, each):
    per = each // 16
    return block // per // 2, (block // per) % 2, block % per


def groups_of(core, x, y, z):
    x, y, z = (x + core) % SIZES["x"], (y + core) % SIZES["y"], (z + core) % SIZES["z"]
    return (x % 2) * 4 + (y % 2) * 2 + z % 2, (x // 2) * 16 + (y // 2) * 4 + z // 2


def group_lists():
    near, far = {}, {}
    index = 0
    for y in range(SIZES["y"]):
        for core in range(2):
            for x in range(SIZES["x"]):
                for z in range(SIZES["z"]):
                    in_near, in_far = groups_of(core, x, y, z)
                    near.setdefault((core, in_far), [None] * 8)[in_near] = index
                    far.setdefault((core, in_near), [None] * 32)[in_far] = index
                    index += 1
    return list(near.values()), list(far.values())


def grads_kernel(
    width, each, scale, place, cot, conv, m4_cot, c3, c4, m3, row_a, row_b, col,
    m3_grad_b, m4_grad_b, top_grad, term, shifted, sums, sums5,
):
    n3, chans = cot.shape
    n4 = c4.shape[0]
    me = place[0]
    per = each // 16

    def put(first, value):
        value = (value * scale).astype(BF16)
        for k in range(value.shape[0] // 16):
            y, owner, r = pieces_of(first // 16 + k, each)
            slot = jnp.where(me == owner, 0, 1)
            for h in range(2):
                p = h * 16 + r
                near, far = groups_of(owner, p // SIZES["z"], y, p % SIZES["z"])
                term[slot, near, far] = value[16 * k : 16 * k + 16, 128 * h : 128 * h + 128]

    blank = jnp.zeros((16, 128), BF16)
    for y in range(SIZES["y"]):
        for p in [h * 16 + r for r in range(per, 16) for h in range(2)]:
            for owner in range(2):
                near, far = groups_of(owner, p // SIZES["z"], y, p % SIZES["z"])
                term[jnp.where(me == owner, 0, 1), near, far] = blank

    fill_shifted(place, 0, cot, row_a, row_b, col, shifted, width)

    def cot_at(a, b):
        return shifted[2 - b, (2 - a) * width : (2 - a) * width + n3]

    total = None
    for a in range(3):
        for b in range(3):
            tap = 3 * a + b
            weight = conv[tap * chans : (tap + 1) * chans]
            part = dot(cot_at(a, b), weight, NT)
            total = part if total is None else total + part
    m3_grad_b[...] = total.astype(BF16)
    for y in range(n4 // (width // 2)):
        pair = total[2 * y * width : (2 * y + 1) * width] + total[(2 * y + 1) * width : (2 * y + 2) * width]
        sums[0, y * width : (y + 1) * width] = pair[:, :128]
        sums[1, y * width : (y + 1) * width] = pair[:, 128:]
    for h in range(2):
        cols = slice(128 * h, 128 * h + 128)
        m4_grad = (
            m4_cot[:, cols].astype(F32)
            + sums[h, pl.ds(0, n4, stride=2), :]
            + sums[h, pl.ds(1, n4, stride=2), :]
        )
        m4_grad_b[:, cols] = m4_grad.astype(BF16)
        half = width // 2
        for y in range(n4 // width):
            sums5[h, y * half : (y + 1) * half] = (
                m4_grad[2 * y * half : (2 * y + 1) * half]
                + m4_grad[(2 * y + 1) * half : (2 * y + 2) * half]
            )
        n5 = n4 // 4
        top_grad[:, cols] = (
            sums5[h, pl.ds(0, n5, stride=2), :] + sums5[h, pl.ds(1, n5, stride=2), :]
        ).astype(BF16)

    depth3, depth4 = c3.shape[1], c4.shape[1]
    put(0, dot(c3[...], m3_grad_b[...], TN))
    put(depth3, dot(c4[...], m4_grad_b[...], TN))
    m3_t = m3[...].T
    for a in range(3):
        for b in range(3):
            tap = 3 * a + b
            put(depth3 + depth4 + tap * chans, dot(m3_t, cot_at(a, b)))


def outputs_kernel(
    width, place, conv, lat3, lat4, m3, row_a, row_b, col, m3_grad_b, m4_grad_b,
    p3, c3_grad, c4_grad, shifted,
):
    n3, chans = m3.shape
    fill_shifted(place, 1, m3, row_a, row_b, col, shifted, width)
    total = None
    for a in range(3):
        for b in range(3):
            tap = 3 * a + b
            part = dot(shifted[b, a * width : a * width + n3], conv[tap * chans : (tap + 1) * chans])
            total = part if total is None else total + part
    p3[...] = total.astype(BF16)
    c3_grad[...] = dot(m3_grad_b[...], lat3[...], NT).astype(BF16)
    c4_grad[...] = dot(m4_grad_b[...], lat4[...], NT).astype(BF16)


def shape_of(*dims):
    return jax.ShapeDtypeStruct(dims, BF16)


def run_merge(width, c3, c4, top, lat3, lat4, cot, conv, m4_cot):
    n3, n4, chans = c3.shape[0], c4.shape[0], lat3.shape[1]
    lines = n3 // width
    border = shape_of(2 * width + 2 * lines, chans)
    return call(
        functools.partial(merge_kernel, width // 2),
        [shape_of(n3, chans), shape_of(2 * lines, chans), border, border],
        [pltpu.VMEM((2, 2 * n4, 128), F32)],
        2 * chans * (c3.size + c4.size),
        2 * (c3.size + c4.size + lat3.size + lat4.size + 2 * cot.size + conv.size),
        (c4, lat4, top, c3, lat3, cot, conv, m4_cot),
    )


def run_grads(width, each, scale, cot, conv, m4_cot, c3, c4, m3, row_a, row_b, col):
    n3, chans = cot.shape
    n4 = c4.shape[0]
    return call(
        functools.partial(grads_kernel, width, each, scale),
        [
            shape_of(n3, chans),
            shape_of(n4, chans),
            shape_of(n4 // 4, chans),
            shape_of(2, 8, 32, 16, 128),
        ],
        [
            pltpu.VMEM((3, n3 + 2 * width, chans), BF16),
            pltpu.VMEM((2, n3 // 2, 128), F32),
            pltpu.VMEM((2, n4 // 2, 128), F32),
        ],
        2 * chans * (c3.size + c4.size + 2 * 9 * n3 * chans),
        2 * (c3.size + c4.size + 2 * conv.size),
        (),
        (cot, conv, m4_cot, c3, c4, m3, row_a, row_b, col),
    )


def run_outputs(width, conv, lat3, lat4, m3, row_a, row_b, col, m3_grad_b, m4_grad_b):
    n3, chans = m3.shape
    n4 = m4_grad_b.shape[0]
    return call(
        functools.partial(outputs_kernel, width),
        [shape_of(n3, chans), shape_of(n3, lat3.shape[0]), shape_of(n4, lat4.shape[0])],
        [pltpu.VMEM((3, n3 + 2 * width, chans), BF16)],
        2 * chans * (n3 * lat3.shape[0] + n4 * lat4.shape[0] + 9 * n3 * chans),
        4 * (n3 * lat3.shape[0] + n4 * lat4.shape[0] + conv.size),
        (),
        (conv, lat3, lat4, m3, row_a, row_b, col, m3_grad_b, m4_grad_b),
    )


def swap_borders(col, row_a, row_b):
    col = lax.ppermute(col, "z_lo", [(0, 1), (1, 0)])
    n_rows = lax.axis_size(ROWS)
    pairs = [(i, i + 1) for i in range(0, n_rows - 1, 2)]
    between = [(i, i + 1) for i in range(1, n_rows - 1, 2)]
    start = (row_a.shape[0] - col.shape[0], 0)
    row_a = lax.dynamic_update_slice(row_a, col, start)
    row_b = lax.dynamic_update_slice(row_b, col, start)
    row_a = lax.ppermute(row_a, ROWS, pairs + [(j, i) for i, j in pairs])
    row_b = lax.ppermute(row_b, ROWS, between + [(j, i) for i, j in between])
    return row_a, row_b, col


def add_kernel(count, *refs):
    parts, out = refs[:-1], refs[-1]
    total = None
    for part in parts:
        for i in range(part.shape[0]):
            value = part[i].astype(F32)
            total = value if total is None else total + value
    total = total.astype(BF16)
    if count is None:
        out[...] = total
    else:
        for i in range(count):
            out[i] = total


def add_up(*parts, count=None):
    shape = parts[0].shape[1:]
    in_vmem = pl.BlockSpec(memory_space=pltpu.VMEM)
    return pl.pallas_call(
        functools.partial(add_kernel, count),
        out_shape=shape_of(*shape) if count is None else shape_of(count, *shape),
        in_specs=[in_vmem] * len(parts),
        out_specs=in_vmem,
        compiler_params=pltpu.CompilerParams(vmem_limit_bytes=LIMIT),
        cost_estimate=pl.CostEstimate(
            flops=sum(p.size for p in parts),
            bytes_accessed=2 * sum(p.size for p in parts),
            transcendentals=0,
        ),
    )(*parts)


def add_grads(term, each):
    everyone = OWNERS + SHARED
    near_groups, far_groups = group_lists()
    _, near, far, rows, cols = term.shape
    got = lax.ppermute(term[1], "core", [(0, 1), (1, 0)])
    part = add_up(term[:1].reshape(1, -1, cols), got.reshape(1, -1, cols))
    part = lax.all_to_all(part.reshape(near, far * rows, cols), everyone, 0, 0, axis_index_groups=near_groups, tiled=True)
    part = add_up(part)
    part = lax.all_to_all(part.reshape(far, rows, cols), everyone, 0, 0, axis_index_groups=far_groups, tiled=True)
    part = add_up(part, count=lax.axis_size(SHARED))
    part = lax.all_to_all(part, SHARED, 0, 0, tiled=True)
    halves = part.reshape(2, -1, cols)[:, :each].astype(F32)
    return jnp.concatenate([halves[0], halves[1]], axis=1)


def shards(c3, c4, top_down, lat3_weight, lat4_weight, conv_weight, p3_cot, m4_cot):
    count, height, width, depth3 = c3.shape
    depth4 = c4.shape[3]
    chans = conv_weight.shape[1]
    n3 = height * width
    n4 = n3 // 4
    n5 = n4 // 4
    stacked = depth3 + depth4 + 9 * chans
    owners = lax.axis_size(OWNERS)
    each = stacked // owners
    total_pixels = n3 * owners * lax.axis_size(SHARED)
    scale = 1.0 / math.sqrt(total_pixels)

    m3, col, row_a, row_b, *fetched = run_merge(
        width, c3.reshape(n3, depth3), c4.reshape(n4, depth4), top_down.reshape(n5, chans),
        lat3_weight, lat4_weight, p3_cot.reshape(n3, chans), conv_weight, m4_cot.reshape(n4, chans),
    )
    c4_v, lat4_v, _, c3_v, lat3_v, cot_v, conv_v, m4_cot_v = fetched
    borders = swap_borders(col, row_a, row_b)
    m3_grad_b, m4_grad_b, top_grad, term = run_grads(
        width, each, scale, cot_v, conv_v, m4_cot_v, c3_v, c4_v, m3, *borders
    )
    weight_grads = add_grads(term, each)
    p3, c3_grad, c4_grad = run_outputs(
        width, conv_v, lat3_v, lat4_v, m3, *borders, m3_grad_b, m4_grad_b
    )
    return (
        p3.reshape(count, height, width, chans),
        c3_grad.reshape(count, height, width, depth3),
        c4_grad.reshape(count, height // 2, width // 2, depth4),
        top_grad.reshape(top_down.shape),
        weight_grads,
    )


def solution(mesh):
    split = jax.sharding.Mesh(
        mesh.devices.reshape(8, 2, 4, 4, 2), ("y", "core", "x", "z_hi", "z_lo")
    )
    tiles = P(OWNERS, ROWS, "z_lo", None)
    return jax.shard_map(
        shards,
        mesh=split,
        in_specs=(tiles, tiles, tiles, P(), P(), P(), tiles, tiles),
        out_specs=(tiles, tiles, tiles, tiles, P(OWNERS, None)),
        check_vma=False,
    )
```

```python
import functools
import math

import jax
import jax.numpy as jnp
from jax import lax
from jax.experimental import pallas as pl
from jax.experimental.pallas import tpu as pltpu
from jax.sharding import PartitionSpec as P

F32 = jnp.float32
BF16 = jnp.bfloat16
ROWS = ("x", "z_hi")
OWNERS = ("y", "core")
SHARED = ("x", "z_hi", "z_lo")
SIZES = {"x": 4, "y": 8, "z": 8}
LIMIT = 32 * 1024 * 1024
NT = (((1,), (1,)), ((), ()))
TN = (((0,), (0,)), ((), ()))


def dot(lhs, rhs, dims=(((1,), (0,)), ((), ()))):
    return lax.dot_general(lhs, rhs, dims, preferred_element_type=F32)


def place_of_device():
    return lax.axis_index("core"), lax.axis_index("z_lo"), lax.axis_index("z_hi") % 2


def call(kernel, out_shape, scratch, flops, moved, fetched, held=()):
    in_vmem = pl.BlockSpec(memory_space=pltpu.VMEM)
    n, m, k = len(fetched), len(held), len(out_shape)

    def body(*refs):
        sources, refs = refs[:n], refs[n:]
        held_refs, refs = refs[:m], refs[m:]
        outs, refs = refs[:k], refs[k:]
        arrived, refs = refs[:n], refs[n:]
        if n == 0:
            kernel(place_of_device(), *held_refs, *outs, *refs)
            return
        copies = [
            pltpu.make_async_copy(source, target, refs[0].at[i])
            for i, (source, target) in enumerate(zip(sources, arrived))
        ]
        for copy in copies:
            copy.start()
        waits = [copy.wait for copy in copies]
        kernel(place_of_device(), waits, *arrived, *held_refs, *outs, *refs[1:])

    return pl.pallas_call(
        body,
        out_shape=list(out_shape) + [jax.ShapeDtypeStruct(x.shape, x.dtype) for x in fetched],
        in_specs=[pl.BlockSpec(memory_space=pltpu.HBM)] * n + [in_vmem] * m,
        out_specs=[in_vmem] * (k + n),
        scratch_shapes=([pltpu.SemaphoreType.DMA((n,))] if n else []) + scratch,
        compiler_params=pltpu.CompilerParams(vmem_limit_bytes=LIMIT),
        cost_estimate=pl.CostEstimate(flops=flops, bytes_accessed=moved, transcendentals=0),
    )(*[pltpu.with_memory_space_constraint(x, pltpu.HBM) for x in fetched], *held)


def merge_kernel(
    width4, place, waits, c4, lat4, top, c3, lat3, cot, conv, m4_cot,
    m3, col, row_a, row_b, up4,
):
    n4, n5 = c4.shape[0], top.shape[0]
    n3 = c3.shape[0]
    width3, width5 = 2 * width4, width4 // 2
    row = lax.broadcasted_iota(jnp.int32, (n4, n5), 0)
    at = lax.broadcasted_iota(jnp.int32, (n4, n5), 1)
    source = (row // width4 // 2) * width5 + (row % width4) // 2
    pick = jnp.where(source == at, 1.0, 0.0).astype(BF16)
    for wait in waits[:3]:
        wait()
    m4 = dot(c4[...], lat4[...]) + dot(pick, top[...])
    for h in range(2):
        half = m4[:, 128 * h : 128 * h + 128]
        up4[h, pl.ds(0, n4, stride=2), :] = half
        up4[h, pl.ds(1, n4, stride=2), :] = half
    for wait in waits[3:5]:
        wait()
    lat = dot(c3[...], lat3[...])
    for y in range(n3 // width3):
        rows = slice(y * width3, (y + 1) * width3)
        above = slice((y // 2) * width3, (y // 2 + 1) * width3)
        for h in range(2):
            cols = slice(128 * h, 128 * h + 128)
            m3[rows, cols] = (lat[rows, cols] + up4[h, above]).astype(BF16)
    waits[5]()
    edge = jnp.where(place[1] == 0, width3 - 1, 0)
    lines = n3 // width3
    row = lax.broadcasted_iota(jnp.int32, (2 * lines, n3), 0)
    at = lax.broadcasted_iota(jnp.int32, (2 * lines, n3), 1)
    take_cot = jnp.where(at == row * width3 + edge, 1.0, 0.0).astype(BF16)
    take_m3 = jnp.where(at == (row - lines) * width3 + edge, 1.0, 0.0).astype(BF16)
    col[...] = (dot(take_cot, cot[...]) + dot(take_m3, m3[...])).astype(BF16)
    odd = place[2] == 1
    first = pl.multiple_of(jnp.where(odd, 0, n3 - width3), width3)
    second = pl.multiple_of(jnp.where(odd, n3 - width3, 0), width3)
    for start, out in ((first, row_a), (second, row_b)):
        out[:width3] = cot[pl.ds(start, width3)]
        out[width3 : 2 * width3] = m3[pl.ds(start, width3)]
        out[2 * width3 :] = jnp.zeros((2 * lines, out.shape[1]), BF16)
    for wait in waits[6:]:
        wait()


def fill_shifted(place, field, own, row_a, row_b, col, shifted, width):
    n, chans = own.shape
    lines = n // width
    z_lo, odd = place[1], place[2] == 1
    rows = slice(field * width, (field + 1) * width)
    corner = slice(2 * width, 2 * width + 2 * lines)
    line_a, line_b = row_a[rows].astype(F32), row_b[rows].astype(F32)
    ends_a, ends_b = row_a[corner].astype(F32), row_b[corner].astype(F32)
    first, last = field * lines, (field + 1) * lines - 1
    sides = col[...].astype(F32)
    before = jnp.where(odd, ends_a, ends_b)[last : last + 1]
    after = jnp.where(odd, ends_b, ends_a)[first : first + 1]
    sides = [before] + [sides[first + y : first + y + 1] for y in range(lines)] + [after]
    at = lax.broadcasted_iota(jnp.int32, (width, chans), 0)
    to_the_left = jnp.where(z_lo == 1, 1.0, 0.0)
    to_the_right = 1.0 - to_the_left
    for y in range(lines + 2):
        if y == 0:
            line = jnp.where(odd, line_a, line_b)
            shifted[1, :width] = line.astype(BF16)
        elif y == lines + 1:
            line = jnp.where(odd, line_b, line_a)
            shifted[1, y * width :] = line.astype(BF16)
        else:
            line = own[(y - 1) * width : y * width]
            shifted[1, y * width : (y + 1) * width] = line
            line = line.astype(F32)
        rows = slice(y * width, (y + 1) * width)
        left, right = sides[y] * to_the_left, sides[y] * to_the_right
        shifted[0, rows] = jnp.where(at == 0, left, pltpu.roll(line, 1, 0)).astype(BF16)
        shifted[2, rows] = jnp.where(
            at == width - 1, right, pltpu.roll(line, width - 1, 0)
        ).astype(BF16)


def pieces_of(block, each):
    per = each // 16
    return block // per // 2, (block // per) % 2, block % per


def groups_of(core, x_lo, y, z):
    y, z = (y + core) % SIZES["y"], (z + core) % SIZES["z"]
    return x_lo * 4 + (y % 2) * 2 + z % 2, (y // 2) * (SIZES["z"] // 2) + z // 2


def group_lists():
    near, far = {}, {}
    index = 0
    for y in range(SIZES["y"]):
        for core in range(2):
            for x in range(SIZES["x"]):
                pair, x_lo = divmod((x + core) % SIZES["x"], 2)
                for z in range(SIZES["z"]):
                    in_near, in_far = groups_of(core, x_lo, y, z)
                    near.setdefault((core, pair, in_far), [None] * 8)[in_near] = index
                    far.setdefault((core, pair, in_near), [None] * 16)[in_far] = index
                    index += 1
    return list(near.values()), list(far.values())


def grads_kernel(
    width, each, scale, place, cot, conv, m4_cot, c3, c4, m3, row_a, row_b, col,
    m3_grad_b, m4_grad_b, top_grad, own, other, shifted, sums, sums5,
):
    n3, chans = cot.shape
    n4 = c4.shape[0]
    me = place[0]
    def store(blocks):
        for core in range(2):

            @pl.when(me == core)
            def _():
                for owner, near, far, value in blocks:
                    (own if owner == core else other)[near, far] = value

    def put(first, value):
        value = (value * scale).astype(BF16)
        blocks = []
        for k in range(value.shape[0] // 16):
            y, owner, p = pieces_of(first // 16 + k, each)
            near, far = groups_of(owner, p // SIZES["z"], y, p % SIZES["z"])
            blocks.append((owner, near, far, value[16 * k : 16 * k + 16]))
        store(blocks)

    blank = jnp.zeros((16, chans), BF16)
    for y in range(SIZES["y"]):
        for p in range(each // 16, 16):
            for owner in range(2):
                near, far = groups_of(owner, p // SIZES["z"], y, p % SIZES["z"])
                store([(owner, near, far, blank)])

    fill_shifted(place, 0, cot, row_a, row_b, col, shifted, width)

    def cot_at(a, b):
        return shifted[2 - b, (2 - a) * width : (2 - a) * width + n3]

    total = None
    for a in range(3):
        for b in range(3):
            tap = 3 * a + b
            weight = conv[tap * chans : (tap + 1) * chans]
            part = dot(cot_at(a, b), weight, NT)
            total = part if total is None else total + part
    m3_grad_b[...] = total.astype(BF16)
    for y in range(n4 // (width // 2)):
        pair = total[2 * y * width : (2 * y + 1) * width] + total[(2 * y + 1) * width : (2 * y + 2) * width]
        sums[0, y * width : (y + 1) * width] = pair[:, :128]
        sums[1, y * width : (y + 1) * width] = pair[:, 128:]
    for h in range(2):
        cols = slice(128 * h, 128 * h + 128)
        m4_grad = (
            m4_cot[:, cols].astype(F32)
            + sums[h, pl.ds(0, n4, stride=2), :]
            + sums[h, pl.ds(1, n4, stride=2), :]
        )
        m4_grad_b[:, cols] = m4_grad.astype(BF16)
        half = width // 2
        for y in range(n4 // width):
            sums5[h, y * half : (y + 1) * half] = (
                m4_grad[2 * y * half : (2 * y + 1) * half]
                + m4_grad[(2 * y + 1) * half : (2 * y + 2) * half]
            )
        n5 = n4 // 4
        top_grad[:, cols] = (
            sums5[h, pl.ds(0, n5, stride=2), :] + sums5[h, pl.ds(1, n5, stride=2), :]
        ).astype(BF16)

    depth3, depth4 = c3.shape[1], c4.shape[1]
    put(0, dot(c3[...], m3_grad_b[...], TN))
    put(depth3, dot(c4[...], m4_grad_b[...], TN))
    m3_t = m3[...].T
    for a in range(3):
        for b in range(3):
            tap = 3 * a + b
            put(depth3 + depth4 + tap * chans, dot(m3_t, cot_at(a, b)))


def outputs_kernel(
    width, place, conv, lat3, lat4, m3, row_a, row_b, col, m3_grad_b, m4_grad_b,
    p3, c3_grad, c4_grad, shifted,
):
    n3, chans = m3.shape
    fill_shifted(place, 1, m3, row_a, row_b, col, shifted, width)
    total = None
    for a in range(3):
        for b in range(3):
            tap = 3 * a + b
            part = dot(shifted[b, a * width : a * width + n3], conv[tap * chans : (tap + 1) * chans])
            total = part if total is None else total + part
    p3[...] = total.astype(BF16)
    c3_grad[...] = dot(m3_grad_b[...], lat3[...], NT).astype(BF16)
    c4_grad[...] = dot(m4_grad_b[...], lat4[...], NT).astype(BF16)


def shape_of(*dims):
    return jax.ShapeDtypeStruct(dims, BF16)


def run_merge(width, c3, c4, top, lat3, lat4, cot, conv, m4_cot):
    n3, n4, chans = c3.shape[0], c4.shape[0], lat3.shape[1]
    lines = n3 // width
    border = shape_of(2 * width + 2 * lines, chans)
    return call(
        functools.partial(merge_kernel, width // 2),
        [shape_of(n3, chans), shape_of(2 * lines, chans), border, border],
        [pltpu.VMEM((2, 2 * n4, 128), F32)],
        2 * chans * (c3.size + c4.size),
        2 * (c3.size + c4.size + lat3.size + lat4.size + 2 * cot.size + conv.size),
        (c4, lat4, top, c3, lat3, cot, conv, m4_cot),
    )


def run_grads(width, each, scale, cot, conv, m4_cot, c3, c4, m3, row_a, row_b, col):
    n3, chans = cot.shape
    n4 = c4.shape[0]
    return call(
        functools.partial(grads_kernel, width, each, scale),
        [
            shape_of(n3, chans),
            shape_of(n4, chans),
            shape_of(n4 // 4, chans),
            shape_of(8, 16, 16, chans),
            shape_of(8, 16, 16, chans),
        ],
        [
            pltpu.VMEM((3, n3 + 2 * width, chans), BF16),
            pltpu.VMEM((2, n3 // 2, 128), F32),
            pltpu.VMEM((2, n4 // 2, 128), F32),
        ],
        2 * chans * (c3.size + c4.size + 2 * 9 * n3 * chans),
        2 * (c3.size + c4.size + 2 * conv.size),
        (),
        (cot, conv, m4_cot, c3, c4, m3, row_a, row_b, col),
    )


def run_outputs(width, conv, lat3, lat4, m3, row_a, row_b, col, m3_grad_b, m4_grad_b):
    n3, chans = m3.shape
    n4 = m4_grad_b.shape[0]
    return call(
        functools.partial(outputs_kernel, width),
        [shape_of(n3, chans), shape_of(n3, lat3.shape[0]), shape_of(n4, lat4.shape[0])],
        [pltpu.VMEM((3, n3 + 2 * width, chans), BF16)],
        2 * chans * (n3 * lat3.shape[0] + n4 * lat4.shape[0] + 9 * n3 * chans),
        4 * (n3 * lat3.shape[0] + n4 * lat4.shape[0] + conv.size),
        (),
        (conv, lat3, lat4, m3, row_a, row_b, col, m3_grad_b, m4_grad_b),
    )


def swap_borders(col, row_a, row_b):
    col = lax.ppermute(col, "z_lo", [(0, 1), (1, 0)])
    n_rows = lax.axis_size(ROWS)
    pairs = [(i, i + 1) for i in range(0, n_rows - 1, 2)]
    between = [(i, i + 1) for i in range(1, n_rows - 1, 2)]
    start = (row_a.shape[0] - col.shape[0], 0)
    row_a = lax.dynamic_update_slice(row_a, col, start)
    row_b = lax.dynamic_update_slice(row_b, col, start)
    row_a = lax.ppermute(row_a, ROWS, pairs + [(j, i) for i, j in pairs])
    row_b = lax.ppermute(row_b, ROWS, between + [(j, i) for i, j in between])
    return row_a, row_b, col


def add_kernel(count, *refs):
    parts, out = refs[:-1], refs[-1]
    total = None
    for part in parts:
        for i in range(part.shape[0]):
            value = part[i].astype(F32)
            total = value if total is None else total + value
    total = total.astype(BF16)
    if count is None:
        out[...] = total
    else:
        for i in range(count):
            out[i] = total


def add_up(*parts, count=None):
    shape = parts[0].shape[1:]
    in_vmem = pl.BlockSpec(memory_space=pltpu.VMEM)
    return pl.pallas_call(
        functools.partial(add_kernel, count),
        out_shape=shape_of(*shape) if count is None else shape_of(count, *shape),
        in_specs=[in_vmem] * len(parts),
        out_specs=in_vmem,
        compiler_params=pltpu.CompilerParams(vmem_limit_bytes=LIMIT),
        cost_estimate=pl.CostEstimate(
            flops=sum(p.size for p in parts),
            bytes_accessed=2 * sum(p.size for p in parts),
            transcendentals=0,
        ),
    )(*parts)


def finish_kernel(parts, out):
    core = lax.axis_index("core")
    rows = parts.shape[2]
    for x_lo in range(2):
        x = jnp.where(core == x_lo, 0, 1)
        for z in range(parts.shape[1]):
            first = (x_lo * parts.shape[1] + z) * rows
            if first < out.shape[0]:
                value = parts[x, z].astype(F32) + parts[x + 2, z].astype(F32)
                out[first : first + rows] = value


def add_grads(own, other, each):
    everyone = OWNERS + SHARED
    near_groups, far_groups = group_lists()
    near, far, rows, cols = own.shape
    got = lax.ppermute(other, "core", [(0, 1), (1, 0)])
    part = add_up(own.reshape(1, -1, cols), got.reshape(1, -1, cols))
    part = part.reshape(near, far * rows, cols)
    part = lax.all_to_all(part, everyone, 0, 0, axis_index_groups=near_groups, tiled=True)
    part = add_up(part).reshape(far, rows, cols)
    part = lax.all_to_all(part, everyone, 0, 0, axis_index_groups=far_groups, tiled=True)
    part = add_up(part, count=lax.axis_size(SHARED))
    part = lax.all_to_all(part, SHARED, 0, 0, tiled=True)
    part = part.reshape(SIZES["x"], SIZES["z"], rows, cols)
    in_vmem = pl.BlockSpec(memory_space=pltpu.VMEM)
    return pl.pallas_call(
        finish_kernel,
        out_shape=jax.ShapeDtypeStruct((each, cols), F32),
        in_specs=[in_vmem],
        out_specs=in_vmem,
        compiler_params=pltpu.CompilerParams(vmem_limit_bytes=LIMIT),
    )(part)


def shards(c3, c4, top_down, lat3_weight, lat4_weight, conv_weight, p3_cot, m4_cot):
    count, height, width, depth3 = c3.shape
    depth4 = c4.shape[3]
    chans = conv_weight.shape[1]
    n3 = height * width
    n4 = n3 // 4
    n5 = n4 // 4
    stacked = depth3 + depth4 + 9 * chans
    owners = lax.axis_size(OWNERS)
    each = stacked // owners
    total_pixels = n3 * owners * lax.axis_size(SHARED)
    scale = 1.0 / math.sqrt(total_pixels)

    m3, col, row_a, row_b, *fetched = run_merge(
        width, c3.reshape(n3, depth3), c4.reshape(n4, depth4), top_down.reshape(n5, chans),
        lat3_weight, lat4_weight, p3_cot.reshape(n3, chans), conv_weight, m4_cot.reshape(n4, chans),
    )
    c4_v, lat4_v, _, c3_v, lat3_v, cot_v, conv_v, m4_cot_v = fetched
    borders = swap_borders(col, row_a, row_b)
    m3_grad_b, m4_grad_b, top_grad, own, other = run_grads(
        width, each, scale, cot_v, conv_v, m4_cot_v, c3_v, c4_v, m3, *borders
    )
    weight_grads = add_grads(own, other, each)
    p3, c3_grad, c4_grad = run_outputs(
        width, conv_v, lat3_v, lat4_v, m3, *borders, m3_grad_b, m4_grad_b
    )
    return (
        p3.reshape(count, height, width, chans),
        c3_grad.reshape(count, height, width, depth3),
        c4_grad.reshape(count, height // 2, width // 2, depth4),
        top_grad.reshape(top_down.shape),
        weight_grads,
    )


def solution(mesh):
    split = jax.sharding.Mesh(
        mesh.devices.reshape(8, 2, 4, 4, 2), ("y", "core", "x", "z_hi", "z_lo")
    )
    tiles = P(OWNERS, ROWS, "z_lo", None)
    return jax.shard_map(
        shards,
        mesh=split,
        in_specs=(tiles, tiles, tiles, P(), P(), P(), tiles, tiles),
        out_specs=(tiles, tiles, tiles, tiles, P(OWNERS, None)),
        check_vma=False,
    )
```

```python
import functools
import math

import jax
import jax.numpy as jnp
from jax import lax
from jax.experimental import pallas as pl
from jax.experimental.pallas import tpu as pltpu
from jax.sharding import PartitionSpec as P

F32 = jnp.float32
BF16 = jnp.bfloat16
ROWS = ("x", "z_hi")
OWNERS = ("y", "core")
SHARED = ("x", "z_hi", "z_lo")
SIZES = {"x": 4, "y": 8, "z": 8}
LIMIT = 32 * 1024 * 1024
NT = (((1,), (1,)), ((), ()))
TN = (((0,), (0,)), ((), ()))


def dot(lhs, rhs, dims=(((1,), (0,)), ((), ()))):
    return lax.dot_general(lhs, rhs, dims, preferred_element_type=F32)


def place_of_device():
    return lax.axis_index("core"), lax.axis_index("z_lo"), lax.axis_index("z_hi") % 2


def call(kernel, out_shape, scratch, flops, moved, fetched, held=()):
    in_vmem = pl.BlockSpec(memory_space=pltpu.VMEM)
    n, m, k = len(fetched), len(held), len(out_shape)

    def body(*refs):
        sources, refs = refs[:n], refs[n:]
        held_refs, refs = refs[:m], refs[m:]
        outs, refs = refs[:k], refs[k:]
        arrived, refs = refs[:n], refs[n:]
        if n == 0:
            kernel(place_of_device(), *held_refs, *outs, *refs)
            return
        copies = [
            pltpu.make_async_copy(source, target, refs[0].at[i])
            for i, (source, target) in enumerate(zip(sources, arrived))
        ]
        for copy in copies:
            copy.start()
        waits = [copy.wait for copy in copies]
        kernel(place_of_device(), waits, *arrived, *held_refs, *outs, *refs[1:])

    return pl.pallas_call(
        body,
        out_shape=list(out_shape) + [jax.ShapeDtypeStruct(x.shape, x.dtype) for x in fetched],
        in_specs=[pl.BlockSpec(memory_space=pltpu.HBM)] * n + [in_vmem] * m,
        out_specs=[in_vmem] * (k + n),
        scratch_shapes=([pltpu.SemaphoreType.DMA((n,))] if n else []) + scratch,
        compiler_params=pltpu.CompilerParams(vmem_limit_bytes=LIMIT),
        cost_estimate=pl.CostEstimate(flops=flops, bytes_accessed=moved, transcendentals=0),
    )(*[pltpu.with_memory_space_constraint(x, pltpu.HBM) for x in fetched], *held)


def merge_kernel(
    width4, place, waits, c4, lat4, top, c3, lat3, cot, m3, col, row_a, row_b, up4,
):
    n4, n5 = c4.shape[0], top.shape[0]
    n3 = c3.shape[0]
    width3, width5 = 2 * width4, width4 // 2
    row = lax.broadcasted_iota(jnp.int32, (n4, n5), 0)
    at = lax.broadcasted_iota(jnp.int32, (n4, n5), 1)
    source = (row // width4 // 2) * width5 + (row % width4) // 2
    pick = jnp.where(source == at, 1.0, 0.0).astype(BF16)
    for wait in waits[:3]:
        wait()
    m4 = dot(c4[...], lat4[...]) + dot(pick, top[...])
    for h in range(2):
        half = m4[:, 128 * h : 128 * h + 128]
        up4[h, pl.ds(0, n4, stride=2), :] = half
        up4[h, pl.ds(1, n4, stride=2), :] = half
    for wait in waits[3:5]:
        wait()
    lat = dot(c3[...], lat3[...])
    for y in range(n3 // width3):
        rows = slice(y * width3, (y + 1) * width3)
        above = slice((y // 2) * width3, (y // 2 + 1) * width3)
        for h in range(2):
            cols = slice(128 * h, 128 * h + 128)
            m3[rows, cols] = (lat[rows, cols] + up4[h, above]).astype(BF16)
    waits[5]()
    edge = jnp.where(place[1] == 0, width3 - 1, 0)
    lines = n3 // width3
    row = lax.broadcasted_iota(jnp.int32, (2 * lines, n3), 0)
    at = lax.broadcasted_iota(jnp.int32, (2 * lines, n3), 1)
    take_cot = jnp.where(at == row * width3 + edge, 1.0, 0.0).astype(BF16)
    take_m3 = jnp.where(at == (row - lines) * width3 + edge, 1.0, 0.0).astype(BF16)
    col[...] = (dot(take_cot, cot[...]) + dot(take_m3, m3[...])).astype(BF16)
    odd = place[2] == 1
    first = pl.multiple_of(jnp.where(odd, 0, n3 - width3), width3)
    second = pl.multiple_of(jnp.where(odd, n3 - width3, 0), width3)
    for start, out in ((first, row_a), (second, row_b)):
        out[:width3] = cot[pl.ds(start, width3)]
        out[width3 : 2 * width3] = m3[pl.ds(start, width3)]
        out[2 * width3 :] = jnp.zeros((2 * lines, out.shape[1]), BF16)


def shift_line(line, left, right):
    width = line.shape[0]
    at = lax.broadcasted_iota(jnp.int32, line.shape, 0)
    before = jnp.where(at == 0, left, pltpu.roll(line, 1, 0))
    after = jnp.where(at == width - 1, right, pltpu.roll(line, width - 1, 0))
    return before.astype(BF16), line.astype(BF16), after.astype(BF16)


def outer_lines(place, field, row_a, row_b, lines, width):
    odd = place[2] == 1
    rows = slice(field * width, (field + 1) * width)
    corner = slice(2 * width, 2 * width + 2 * lines)
    line_a, line_b = row_a[rows].astype(F32), row_b[rows].astype(F32)
    ends_a, ends_b = row_a[corner].astype(F32), row_b[corner].astype(F32)
    first, last = field * lines, (field + 1) * lines - 1
    return (
        (jnp.where(odd, line_a, line_b), jnp.where(odd, ends_a, ends_b)[last : last + 1]),
        (jnp.where(odd, line_b, line_a), jnp.where(odd, ends_b, ends_a)[first : first + 1]),
    )


def fill_line(place, shifted, y, line, side):
    to_the_left = jnp.where(place[1] == 1, 1.0, 0.0)
    width = line.shape[0]
    planes = shift_line(line, side * to_the_left, side * (1.0 - to_the_left))
    for i in range(3):
        shifted[i, y * width : (y + 1) * width] = planes[i]


def fill_inner(place, field, own, col, shifted, width):
    lines = own.shape[0] // width
    sides = col[...].astype(F32)
    for y in range(lines):
        side = sides[field * lines + y : field * lines + y + 1]
        fill_line(place, shifted, y + 1, own[y * width : (y + 1) * width].astype(F32), side)


def pieces_of(block, each):
    per = each // 16
    return block // per // 2, (block // per) % 2, block % per


def groups_of(core, x, y, z):
    x, y, z = (x + core) % SIZES["x"], (y + core) % SIZES["y"], (z + core) % SIZES["z"]
    return (x % 2) * 4 + (y % 2) * 2 + z % 2, (x // 2) * 16 + (y // 2) * 4 + z // 2


def group_lists():
    near, far = {}, {}
    index = 0
    for y in range(SIZES["y"]):
        for core in range(2):
            for x in range(SIZES["x"]):
                for z in range(SIZES["z"]):
                    in_near, in_far = groups_of(core, x, y, z)
                    near.setdefault((core, in_far), [None] * 8)[in_near] = index
                    far.setdefault((core, in_near), [None] * 32)[in_far] = index
                    index += 1
    return list(near.values()), list(far.values())


def early_kernel(width, place, cot, conv, m3, col, partial, gradc, shifted):
    n3, chans = cot.shape
    blank = jnp.zeros((3, width, chans), BF16)
    shifted[:, :width] = blank
    shifted[:, n3 + width :] = blank
    fill_inner(place, 0, cot, col, shifted, width)
    m3_t = m3[...].T
    total = None
    for a in range(3):
        for b in range(3):
            tap = slice((3 * a + b) * chans, (3 * a + b + 1) * chans)
            field = shifted[2 - b, (2 - a) * width : (2 - a) * width + n3]
            part = dot(field, conv[tap], NT)
            total = part if total is None else total + part
            gradc[tap] = dot(m3_t, field)
    partial[...] = total


def grads_kernel(
    width, each, scale, place, partial, gradc, conv, m4_cot, c3, c4, m3, row_a, row_b,
    m3_grad_b, m4_grad_b, top_grad, term, total, sums, sums5,
):
    n3, chans = partial.shape
    n4 = c4.shape[0]
    me = place[0]
    per = each // 16

    def put(first, value):
        value = (value * scale).astype(BF16)
        for k in range(value.shape[0] // 16):
            y, owner, r = pieces_of(first // 16 + k, each)
            slot = jnp.where(me == owner, 0, 1)
            for h in range(2):
                p = h * 16 + r
                near, far = groups_of(owner, p // SIZES["z"], y, p % SIZES["z"])
                term[slot, near, far] = value[16 * k : 16 * k + 16, 128 * h : 128 * h + 128]

    blank = jnp.zeros((16, 128), BF16)
    for y in range(SIZES["y"]):
        for p in [h * 16 + r for r in range(per, 16) for h in range(2)]:
            for owner in range(2):
                near, far = groups_of(owner, p // SIZES["z"], y, p % SIZES["z"])
                term[jnp.where(me == owner, 0, 1), near, far] = blank

    before, after = outer_lines(place, 0, row_a, row_b, n3 // width, width)
    to_the_left = jnp.where(place[1] == 1, 1.0, 0.0)
    total[...] = partial[...]
    added = {}
    for a, rows, (line, side) in (
        (2, slice(0, width), before),
        (0, slice(n3 - width, n3), after),
    ):
        planes = shift_line(line, side * to_the_left, side * (1.0 - to_the_left))
        part = total[rows]
        for b in range(3):
            tap = 3 * a + b
            part = part + dot(planes[2 - b], conv[tap * chans : (tap + 1) * chans], NT)
            added[tap] = (rows, planes[2 - b])
        total[rows] = part
    m3_grad_b[...] = total[...].astype(BF16)
    for y in range(n4 // (width // 2)):
        pair = total[2 * y * width : (2 * y + 1) * width] + total[(2 * y + 1) * width : (2 * y + 2) * width]
        sums[0, y * width : (y + 1) * width] = pair[:, :128]
        sums[1, y * width : (y + 1) * width] = pair[:, 128:]
    for h in range(2):
        cols = slice(128 * h, 128 * h + 128)
        m4_grad = (
            m4_cot[:, cols].astype(F32)
            + sums[h, pl.ds(0, n4, stride=2), :]
            + sums[h, pl.ds(1, n4, stride=2), :]
        )
        m4_grad_b[:, cols] = m4_grad.astype(BF16)
        half = width // 2
        for y in range(n4 // width):
            sums5[h, y * half : (y + 1) * half] = (
                m4_grad[2 * y * half : (2 * y + 1) * half]
                + m4_grad[(2 * y + 1) * half : (2 * y + 2) * half]
            )
        n5 = n4 // 4
        top_grad[:, cols] = (
            sums5[h, pl.ds(0, n5, stride=2), :] + sums5[h, pl.ds(1, n5, stride=2), :]
        ).astype(BF16)

    depth3, depth4 = c3.shape[1], c4.shape[1]
    put(0, dot(c3[...], m3_grad_b[...], TN))
    put(depth3, dot(c4[...], m4_grad_b[...], TN))
    for tap in range(9):
        value = gradc[tap * chans : (tap + 1) * chans]
        if tap in added:
            rows, plane = added[tap]
            value = value + dot(m3[rows], plane, TN)
        put(depth3 + depth4 + tap * chans, value)


def outputs_kernel(
    width, place, conv, lat3, lat4, m3, row_a, row_b, col, m3_grad_b, m4_grad_b,
    p3, c3_grad, c4_grad, shifted,
):
    n3, chans = m3.shape
    fill_inner(place, 1, m3, col, shifted, width)
    before, after = outer_lines(place, 1, row_a, row_b, n3 // width, width)
    fill_line(place, shifted, 0, *before)
    fill_line(place, shifted, n3 // width + 1, *after)
    total = None
    for a in range(3):
        for b in range(3):
            tap = 3 * a + b
            part = dot(shifted[b, a * width : a * width + n3], conv[tap * chans : (tap + 1) * chans])
            total = part if total is None else total + part
    p3[...] = total.astype(BF16)
    c3_grad[...] = dot(m3_grad_b[...], lat3[...], NT).astype(BF16)
    c4_grad[...] = dot(m4_grad_b[...], lat4[...], NT).astype(BF16)


def shape_of(*dims):
    return jax.ShapeDtypeStruct(dims, BF16)


def run_merge(width, c3, c4, top, lat3, lat4, cot):
    n3, n4, chans = c3.shape[0], c4.shape[0], lat3.shape[1]
    lines = n3 // width
    border = shape_of(2 * width + 2 * lines, chans)
    return call(
        functools.partial(merge_kernel, width // 2),
        [shape_of(n3, chans), shape_of(2 * lines, chans), border, border],
        [pltpu.VMEM((2, 2 * n4, 128), F32)],
        2 * chans * (c3.size + c4.size),
        2 * (c3.size + c4.size + lat3.size + lat4.size + 2 * cot.size),
        (c4, lat4, top, c3, lat3, cot),
    )


def fetch_kernel(place, waits, *refs):
    for wait in waits:
        wait()


def run_fetch(after, *arrays):
    moved = 2 * sum(x.size for x in arrays)
    return call(fetch_kernel, [], [], 0, moved, arrays, (after,))


def run_early(width, cot, conv, m3, col):
    n3, chans = cot.shape
    return call(
        functools.partial(early_kernel, width),
        [jax.ShapeDtypeStruct((n3, chans), F32), jax.ShapeDtypeStruct(conv.shape, F32)],
        [pltpu.VMEM((3, n3 + 2 * width, chans), BF16)],
        2 * chans * 2 * 9 * n3 * chans,
        8 * conv.size,
        (),
        (cot, conv, m3, col),
    )


def run_grads(width, each, scale, partial, gradc, conv, m4_cot, c3, c4, m3, row_a, row_b):
    n3, chans = partial.shape
    n4 = c4.shape[0]
    return call(
        functools.partial(grads_kernel, width, each, scale),
        [
            shape_of(n3, chans),
            shape_of(n4, chans),
            shape_of(n4 // 4, chans),
            shape_of(2, 8, 32, 16, 128),
        ],
        [
            pltpu.VMEM((n3, chans), F32),
            pltpu.VMEM((2, n3 // 2, 128), F32),
            pltpu.VMEM((2, n4 // 2, 128), F32),
        ],
        2 * chans * (c3.size + c4.size + 6 * width * chans),
        2 * (c3.size + c4.size + 4 * conv.size),
        (),
        (partial, gradc, conv, m4_cot, c3, c4, m3, row_a, row_b),
    )


def run_outputs(width, conv, lat3, lat4, m3, row_a, row_b, col, m3_grad_b, m4_grad_b):
    n3, chans = m3.shape
    n4 = m4_grad_b.shape[0]
    return call(
        functools.partial(outputs_kernel, width),
        [shape_of(n3, chans), shape_of(n3, lat3.shape[0]), shape_of(n4, lat4.shape[0])],
        [pltpu.VMEM((3, n3 + 2 * width, chans), BF16)],
        2 * chans * (n3 * lat3.shape[0] + n4 * lat4.shape[0] + 9 * n3 * chans),
        4 * (n3 * lat3.shape[0] + n4 * lat4.shape[0] + conv.size),
        (),
        (conv, lat3, lat4, m3, row_a, row_b, col, m3_grad_b, m4_grad_b),
    )


def swap_borders(col, row_a, row_b):
    col = lax.ppermute(col, "z_lo", [(0, 1), (1, 0)])
    n_rows = lax.axis_size(ROWS)
    pairs = [(i, i + 1) for i in range(0, n_rows - 1, 2)]
    between = [(i, i + 1) for i in range(1, n_rows - 1, 2)]
    start = (row_a.shape[0] - col.shape[0], 0)
    row_a = lax.dynamic_update_slice(row_a, col, start)
    row_b = lax.dynamic_update_slice(row_b, col, start)
    row_a = lax.ppermute(row_a, ROWS, pairs + [(j, i) for i, j in pairs])
    row_b = lax.ppermute(row_b, ROWS, between + [(j, i) for i, j in between])
    return row_a, row_b, col


def add_kernel(count, *refs):
    parts, out = refs[:-1], refs[-1]
    total = None
    for part in parts:
        for i in range(part.shape[0]):
            value = part[i].astype(F32)
            total = value if total is None else total + value
    total = total.astype(BF16)
    if count is None:
        out[...] = total
    else:
        for i in range(count):
            out[i] = total


def add_up(*parts, count=None):
    shape = parts[0].shape[1:]
    in_vmem = pl.BlockSpec(memory_space=pltpu.VMEM)
    return pl.pallas_call(
        functools.partial(add_kernel, count),
        out_shape=shape_of(*shape) if count is None else shape_of(count, *shape),
        in_specs=[in_vmem] * len(parts),
        out_specs=in_vmem,
        compiler_params=pltpu.CompilerParams(vmem_limit_bytes=LIMIT),
        cost_estimate=pl.CostEstimate(
            flops=sum(p.size for p in parts),
            bytes_accessed=2 * sum(p.size for p in parts),
            transcendentals=0,
        ),
    )(*parts)


def add_grads(term, each):
    everyone = OWNERS + SHARED
    near_groups, far_groups = group_lists()
    _, near, far, rows, cols = term.shape
    got = lax.ppermute(term[1], "core", [(0, 1), (1, 0)])
    part = add_up(term[:1].reshape(1, -1, cols), got.reshape(1, -1, cols))
    part = lax.all_to_all(part.reshape(near, far * rows, cols), everyone, 0, 0, axis_index_groups=near_groups, tiled=True)
    part = add_up(part)
    part = lax.all_to_all(part.reshape(far, rows, cols), everyone, 0, 0, axis_index_groups=far_groups, tiled=True)
    part = add_up(part, count=lax.axis_size(SHARED))
    part = lax.all_to_all(part, SHARED, 0, 0, tiled=True)
    halves = part.reshape(2, -1, cols)[:, :each].astype(F32)
    return jnp.concatenate([halves[0], halves[1]], axis=1)


def shards(c3, c4, top_down, lat3_weight, lat4_weight, conv_weight, p3_cot, m4_cot):
    count, height, width, depth3 = c3.shape
    depth4 = c4.shape[3]
    chans = conv_weight.shape[1]
    n3 = height * width
    n4 = n3 // 4
    n5 = n4 // 4
    stacked = depth3 + depth4 + 9 * chans
    owners = lax.axis_size(OWNERS)
    each = stacked // owners
    total_pixels = n3 * owners * lax.axis_size(SHARED)
    scale = 1.0 / math.sqrt(total_pixels)

    m3, col, row_a, row_b, *fetched = run_merge(
        width, c3.reshape(n3, depth3), c4.reshape(n4, depth4), top_down.reshape(n5, chans),
        lat3_weight, lat4_weight, p3_cot.reshape(n3, chans),
    )
    c4_v, lat4_v, _, c3_v, lat3_v, cot_v = fetched
    conv_v, m4_cot_v = run_fetch(m3, conv_weight, m4_cot.reshape(n4, chans))
    borders = swap_borders(col, row_a, row_b)
    partial, gradc = run_early(width, cot_v, conv_v, m3, borders[2])
    m3_grad_b, m4_grad_b, top_grad, term = run_grads(
        width, each, scale, partial, gradc, conv_v, m4_cot_v, c3_v, c4_v, m3, *borders[:2]
    )
    weight_grads = add_grads(term, each)
    p3, c3_grad, c4_grad = run_outputs(
        width, conv_v, lat3_v, lat4_v, m3, *borders, m3_grad_b, m4_grad_b
    )
    return (
        p3.reshape(count, height, width, chans),
        c3_grad.reshape(count, height, width, depth3),
        c4_grad.reshape(count, height // 2, width // 2, depth4),
        top_grad.reshape(top_down.shape),
        weight_grads,
    )


def solution(mesh):
    split = jax.sharding.Mesh(
        mesh.devices.reshape(8, 2, 4, 4, 2), ("y", "core", "x", "z_hi", "z_lo")
    )
    tiles = P(OWNERS, ROWS, "z_lo", None)
    return jax.shard_map(
        shards,
        mesh=split,
        in_specs=(tiles, tiles, tiles, P(), P(), P(), tiles, tiles),
        out_specs=(tiles, tiles, tiles, tiles, P(OWNERS, None)),
        check_vma=False,
    )
```

```python
import functools
import math

import jax
import jax.numpy as jnp
from jax import lax
from jax.experimental import pallas as pl
from jax.experimental.pallas import tpu as pltpu
from jax.sharding import PartitionSpec as P

F32 = jnp.float32
BF16 = jnp.bfloat16
ROWS = ("x", "z_hi")
OWNERS = ("y", "core")
SHARED = ("x", "z_hi", "z_lo")
SIZES = {"x": 4, "y": 8, "z": 8}
LIMIT = 32 * 1024 * 1024
NT = (((1,), (1,)), ((), ()))
TN = (((0,), (0,)), ((), ()))


def dot(lhs, rhs, dims=(((1,), (0,)), ((), ()))):
    return lax.dot_general(lhs, rhs, dims, preferred_element_type=F32)


def place_of_device():
    return lax.axis_index("core"), lax.axis_index("z_lo"), lax.axis_index("z_hi") % 2


def call(kernel, out_shape, scratch, flops, moved, fetched, held=()):
    in_vmem = pl.BlockSpec(memory_space=pltpu.VMEM)
    n, m, k = len(fetched), len(held), len(out_shape)

    def body(*refs):
        sources, refs = refs[:n], refs[n:]
        held_refs, refs = refs[:m], refs[m:]
        outs, refs = refs[:k], refs[k:]
        arrived, refs = refs[:n], refs[n:]
        if n == 0:
            kernel(place_of_device(), *held_refs, *outs, *refs)
            return
        copies = [
            pltpu.make_async_copy(source, target, refs[0].at[i])
            for i, (source, target) in enumerate(zip(sources, arrived))
        ]
        for copy in copies:
            copy.start()
        waits = [copy.wait for copy in copies]
        kernel(place_of_device(), waits, *arrived, *held_refs, *outs, *refs[1:])

    return pl.pallas_call(
        body,
        out_shape=list(out_shape) + [jax.ShapeDtypeStruct(x.shape, x.dtype) for x in fetched],
        in_specs=[pl.BlockSpec(memory_space=pltpu.HBM)] * n + [in_vmem] * m,
        out_specs=[in_vmem] * (k + n),
        scratch_shapes=([pltpu.SemaphoreType.DMA((n,))] if n else []) + scratch,
        compiler_params=pltpu.CompilerParams(vmem_limit_bytes=LIMIT),
        cost_estimate=pl.CostEstimate(flops=flops, bytes_accessed=moved, transcendentals=0),
    )(*[pltpu.with_memory_space_constraint(x, pltpu.HBM) for x in fetched], *held)


def merge_kernel(
    width4, place, waits, c4, lat4, top, c3, lat3, cot, m3, col, row_a, row_b, up4,
):
    n4, n5 = c4.shape[0], top.shape[0]
    n3 = c3.shape[0]
    width3, width5 = 2 * width4, width4 // 2
    row = lax.broadcasted_iota(jnp.int32, (n4, n5), 0)
    at = lax.broadcasted_iota(jnp.int32, (n4, n5), 1)
    source = (row // width4 // 2) * width5 + (row % width4) // 2
    pick = jnp.where(source == at, 1.0, 0.0).astype(BF16)
    for wait in waits[:3]:
        wait()
    m4 = dot(c4[...], lat4[...]) + dot(pick, top[...])
    for h in range(2):
        half = m4[:, 128 * h : 128 * h + 128]
        up4[h, pl.ds(0, n4, stride=2), :] = half
        up4[h, pl.ds(1, n4, stride=2), :] = half
    for wait in waits[3:5]:
        wait()
    lat = dot(c3[...], lat3[...])
    for y in range(n3 // width3):
        rows = slice(y * width3, (y + 1) * width3)
        above = slice((y // 2) * width3, (y // 2 + 1) * width3)
        for h in range(2):
            cols = slice(128 * h, 128 * h + 128)
            m3[rows, cols] = (lat[rows, cols] + up4[h, above]).astype(BF16)
    waits[5]()
    edge = jnp.where(place[1] == 0, width3 - 1, 0)
    lines = n3 // width3
    row = lax.broadcasted_iota(jnp.int32, (2 * lines, n3), 0)
    at = lax.broadcasted_iota(jnp.int32, (2 * lines, n3), 1)
    take_cot = jnp.where(at == row * width3 + edge, 1.0, 0.0).astype(BF16)
    take_m3 = jnp.where(at == (row - lines) * width3 + edge, 1.0, 0.0).astype(BF16)
    col[...] = (dot(take_cot, cot[...]) + dot(take_m3, m3[...])).astype(BF16)
    odd = place[2] == 1
    first = pl.multiple_of(jnp.where(odd, 0, n3 - width3), width3)
    second = pl.multiple_of(jnp.where(odd, n3 - width3, 0), width3)
    for start, out in ((first, row_a), (second, row_b)):
        out[:width3] = cot[pl.ds(start, width3)]
        out[width3 : 2 * width3] = m3[pl.ds(start, width3)]
        out[2 * width3 :] = jnp.zeros((2 * lines, out.shape[1]), BF16)


def shift_line(line, left, right):
    width = line.shape[0]
    at = lax.broadcasted_iota(jnp.int32, line.shape, 0)
    before = jnp.where(at == 0, left, pltpu.roll(line, 1, 0))
    after = jnp.where(at == width - 1, right, pltpu.roll(line, width - 1, 0))
    return before.astype(BF16), line.astype(BF16), after.astype(BF16)


def outer_lines(place, field, row_a, row_b, lines, width):
    odd = place[2] == 1
    rows = slice(field * width, (field + 1) * width)
    corner = slice(2 * width, 2 * width + 2 * lines)
    line_a, line_b = row_a[rows].astype(F32), row_b[rows].astype(F32)
    ends_a, ends_b = row_a[corner].astype(F32), row_b[corner].astype(F32)
    first, last = field * lines, (field + 1) * lines - 1
    return (
        (jnp.where(odd, line_a, line_b), jnp.where(odd, ends_a, ends_b)[last : last + 1]),
        (jnp.where(odd, line_b, line_a), jnp.where(odd, ends_b, ends_a)[first : first + 1]),
    )


def fill_line(place, shifted, y, line, side):
    to_the_left = jnp.where(place[1] == 1, 1.0, 0.0)
    width = line.shape[0]
    planes = shift_line(line, side * to_the_left, side * (1.0 - to_the_left))
    for i in range(3):
        shifted[i, y * width : (y + 1) * width] = planes[i]


def fill_inner(place, field, own, col, shifted, width):
    lines = own.shape[0] // width
    sides = col[...].astype(F32)
    for y in range(lines):
        side = sides[field * lines + y : field * lines + y + 1]
        fill_line(place, shifted, y + 1, own[y * width : (y + 1) * width].astype(F32), side)


def pieces_of(block, each):
    per = each // 16
    return block // per // 2, (block // per) % 2, block % per


def groups_of(core, x, y, z):
    x, y, z = (x + core) % SIZES["x"], (y + core) % SIZES["y"], (z + core) % SIZES["z"]
    return (x % 2) * 4 + (y % 2) * 2 + z % 2, (x // 2) * 16 + (y // 2) * 4 + z // 2


def group_lists():
    near, far = {}, {}
    index = 0
    for y in range(SIZES["y"]):
        for core in range(2):
            for x in range(SIZES["x"]):
                for z in range(SIZES["z"]):
                    in_near, in_far = groups_of(core, x, y, z)
                    near.setdefault((core, in_far), [None] * 8)[in_near] = index
                    far.setdefault((core, in_near), [None] * 32)[in_far] = index
                    index += 1
    return list(near.values()), list(far.values())


def early_kernel(width, place, cot, conv, m3, col, partial, gradc, shifted):
    n3, chans = cot.shape
    blank = jnp.zeros((3, width, chans), BF16)
    shifted[:, :width] = blank
    shifted[:, n3 + width :] = blank
    fill_inner(place, 0, cot, col, shifted, width)
    m3_t = m3[...].T
    total = None
    for a in range(3):
        for b in range(3):
            tap = slice((3 * a + b) * chans, (3 * a + b + 1) * chans)
            field = shifted[2 - b, (2 - a) * width : (2 - a) * width + n3]
            part = dot(field, conv[tap], NT)
            total = part if total is None else total + part
            gradc[tap] = dot(m3_t, field)
    partial[...] = total


def grads_kernel(
    width, each, scale, place, partial, gradc, conv, m4_cot, c3, c4, m3, row_a, row_b,
    m3_grad_b, m4_grad_b, top_grad, term, total, sums, sums5,
):
    n3, chans = partial.shape
    n4 = c4.shape[0]
    me = place[0]
    per = each // 16

    def put(first, value):
        value = (value * scale).astype(BF16)
        for k in range(value.shape[0] // 16):
            y, owner, r = pieces_of(first // 16 + k, each)
            slot = jnp.where(me == owner, 0, 1)
            for h in range(2):
                p = h * 16 + r
                near, far = groups_of(owner, p // SIZES["z"], y, p % SIZES["z"])
                term[slot, near, far] = value[16 * k : 16 * k + 16, 128 * h : 128 * h + 128]

    blank = jnp.zeros((16, 128), BF16)
    for y in range(SIZES["y"]):
        for p in [h * 16 + r for r in range(per, 16) for h in range(2)]:
            for owner in range(2):
                near, far = groups_of(owner, p // SIZES["z"], y, p % SIZES["z"])
                term[jnp.where(me == owner, 0, 1), near, far] = blank

    before, after = outer_lines(place, 0, row_a, row_b, n3 // width, width)
    to_the_left = jnp.where(place[1] == 1, 1.0, 0.0)
    total[...] = partial[...]
    added = {}
    for a, rows, (line, side) in (
        (2, slice(0, width), before),
        (0, slice(n3 - width, n3), after),
    ):
        planes = shift_line(line, side * to_the_left, side * (1.0 - to_the_left))
        part = total[rows]
        for b in range(3):
            tap = 3 * a + b
            part = part + dot(planes[2 - b], conv[tap * chans : (tap + 1) * chans], NT)
            added[tap] = (rows, planes[2 - b])
        total[rows] = part
    m3_grad_b[...] = total[...].astype(BF16)
    for y in range(n4 // (width // 2)):
        pair = total[2 * y * width : (2 * y + 1) * width] + total[(2 * y + 1) * width : (2 * y + 2) * width]
        sums[0, y * width : (y + 1) * width] = pair[:, :128]
        sums[1, y * width : (y + 1) * width] = pair[:, 128:]
    for h in range(2):
        cols = slice(128 * h, 128 * h + 128)
        m4_grad = (
            m4_cot[:, cols].astype(F32)
            + sums[h, pl.ds(0, n4, stride=2), :]
            + sums[h, pl.ds(1, n4, stride=2), :]
        )
        m4_grad_b[:, cols] = m4_grad.astype(BF16)
        half = width // 2
        for y in range(n4 // width):
            sums5[h, y * half : (y + 1) * half] = (
                m4_grad[2 * y * half : (2 * y + 1) * half]
                + m4_grad[(2 * y + 1) * half : (2 * y + 2) * half]
            )
        n5 = n4 // 4
        top_grad[:, cols] = (
            sums5[h, pl.ds(0, n5, stride=2), :] + sums5[h, pl.ds(1, n5, stride=2), :]
        ).astype(BF16)

    depth3, depth4 = c3.shape[1], c4.shape[1]
    put(0, dot(c3[...], m3_grad_b[...], TN))
    put(depth3, dot(c4[...], m4_grad_b[...], TN))
    for tap in range(9):
        value = gradc[tap * chans : (tap + 1) * chans]
        if tap in added:
            rows, plane = added[tap]
            value = value + dot(m3[rows], plane, TN)
        put(depth3 + depth4 + tap * chans, value)


def outputs_kernel(
    width, place, conv, lat3, lat4, m3, row_a, row_b, col, m3_grad_b, m4_grad_b,
    p3, c3_grad, c4_grad, shifted,
):
    n3, chans = m3.shape
    fill_inner(place, 1, m3, col, shifted, width)
    before, after = outer_lines(place, 1, row_a, row_b, n3 // width, width)
    fill_line(place, shifted, 0, *before)
    fill_line(place, shifted, n3 // width + 1, *after)
    total = None
    for a in range(3):
        for b in range(3):
            tap = 3 * a + b
            part = dot(shifted[b, a * width : a * width + n3], conv[tap * chans : (tap + 1) * chans])
            total = part if total is None else total + part
    p3[...] = total.astype(BF16)
    c3_grad[...] = dot(m3_grad_b[...], lat3[...], NT).astype(BF16)
    c4_grad[...] = dot(m4_grad_b[...], lat4[...], NT).astype(BF16)


def shape_of(*dims):
    return jax.ShapeDtypeStruct(dims, BF16)


def run_merge(width, c3, c4, top, lat3, lat4, cot):
    n3, n4, chans = c3.shape[0], c4.shape[0], lat3.shape[1]
    lines = n3 // width
    border = shape_of(2 * width + 2 * lines, chans)
    return call(
        functools.partial(merge_kernel, width // 2),
        [shape_of(n3, chans), shape_of(2 * lines, chans), border, border],
        [pltpu.VMEM((2, 2 * n4, 128), F32)],
        2 * chans * (c3.size + c4.size),
        2 * (c3.size + c4.size + lat3.size + lat4.size + 2 * cot.size),
        (c4, lat4, top, c3, lat3, cot),
    )


def fetch_kernel(place, waits, *refs):
    for wait in waits:
        wait()


def run_fetch(after, *arrays):
    moved = 2 * sum(x.size for x in arrays)
    return call(fetch_kernel, [], [], 0, moved, arrays, (after,))


def run_early(width, cot, conv, m3, col):
    n3, chans = cot.shape
    return call(
        functools.partial(early_kernel, width),
        [jax.ShapeDtypeStruct((n3, chans), F32), jax.ShapeDtypeStruct(conv.shape, F32)],
        [pltpu.VMEM((3, n3 + 2 * width, chans), BF16)],
        2 * chans * 2 * 9 * n3 * chans,
        8 * conv.size,
        (),
        (cot, conv, m3, col),
    )


def run_grads(width, each, scale, partial, gradc, conv, m4_cot, c3, c4, m3, row_a, row_b):
    n3, chans = partial.shape
    n4 = c4.shape[0]
    return call(
        functools.partial(grads_kernel, width, each, scale),
        [
            shape_of(n3, chans),
            shape_of(n4, chans),
            shape_of(n4 // 4, chans),
            shape_of(2, 8, 32, 16, 128),
        ],
        [
            pltpu.VMEM((n3, chans), F32),
            pltpu.VMEM((2, n3 // 2, 128), F32),
            pltpu.VMEM((2, n4 // 2, 128), F32),
        ],
        2 * chans * (c3.size + c4.size + 6 * width * chans),
        2 * (c3.size + c4.size + 4 * conv.size),
        (),
        (partial, gradc, conv, m4_cot, c3, c4, m3, row_a, row_b),
    )


def run_outputs(width, conv, lat3, lat4, m3, row_a, row_b, col, m3_grad_b, m4_grad_b):
    n3, chans = m3.shape
    n4 = m4_grad_b.shape[0]
    return call(
        functools.partial(outputs_kernel, width),
        [shape_of(n3, chans), shape_of(n3, lat3.shape[0]), shape_of(n4, lat4.shape[0])],
        [pltpu.VMEM((3, n3 + 2 * width, chans), BF16)],
        2 * chans * (n3 * lat3.shape[0] + n4 * lat4.shape[0] + 9 * n3 * chans),
        4 * (n3 * lat3.shape[0] + n4 * lat4.shape[0] + conv.size),
        (),
        (conv, lat3, lat4, m3, row_a, row_b, col, m3_grad_b, m4_grad_b),
    )


def swap_borders(col, row_a, row_b):
    col = lax.ppermute(col, "z_lo", [(0, 1), (1, 0)])
    n_rows = lax.axis_size(ROWS)
    pairs = [(i, i + 1) for i in range(0, n_rows - 1, 2)]
    between = [(i, i + 1) for i in range(1, n_rows - 1, 2)]
    start = (row_a.shape[0] - col.shape[0], 0)
    row_a = lax.dynamic_update_slice(row_a, col, start)
    row_b = lax.dynamic_update_slice(row_b, col, start)
    row_a = lax.ppermute(row_a, ROWS, pairs + [(j, i) for i, j in pairs])
    row_b = lax.ppermute(row_b, ROWS, between + [(j, i) for i, j in between])
    return row_a, row_b, col


def add_cores_kernel(term, got, out):
    out[...] = (term[0].astype(F32) + got[...].astype(F32)).astype(BF16)


def add_cores(term, got):
    in_vmem = pl.BlockSpec(memory_space=pltpu.VMEM)
    return pl.pallas_call(
        add_cores_kernel,
        out_shape=shape_of(*got.shape),
        in_specs=[in_vmem] * 2,
        out_specs=in_vmem,
        compiler_params=pltpu.CompilerParams(vmem_limit_bytes=LIMIT),
        cost_estimate=pl.CostEstimate(
            flops=got.size, bytes_accessed=6 * got.size, transcendentals=0
        ),
    )(term, got)


def add_kernel(count, *refs):
    parts, out = refs[:-1], refs[-1]
    total = None
    for part in parts:
        for i in range(part.shape[0]):
            value = part[i].astype(F32)
            total = value if total is None else total + value
    total = total.astype(BF16)
    if count is None:
        out[...] = total
    else:
        for i in range(count):
            out[i] = total


def add_up(*parts, count=None):
    shape = parts[0].shape[1:]
    in_vmem = pl.BlockSpec(memory_space=pltpu.VMEM)
    return pl.pallas_call(
        functools.partial(add_kernel, count),
        out_shape=shape_of(*shape) if count is None else shape_of(count, *shape),
        in_specs=[in_vmem] * len(parts),
        out_specs=in_vmem,
        compiler_params=pltpu.CompilerParams(vmem_limit_bytes=LIMIT),
        cost_estimate=pl.CostEstimate(
            flops=sum(p.size for p in parts),
            bytes_accessed=2 * sum(p.size for p in parts),
            transcendentals=0,
        ),
    )(*parts)


def add_grads(term, got, each):
    everyone = OWNERS + SHARED
    near_groups, far_groups = group_lists()
    _, near, far, rows, cols = term.shape
    part = add_cores(term, got)
    part = lax.all_to_all(part.reshape(near, far * rows, cols), everyone, 0, 0, axis_index_groups=near_groups, tiled=True)
    part = add_up(part)
    part = lax.all_to_all(part.reshape(far, rows, cols), everyone, 0, 0, axis_index_groups=far_groups, tiled=True)
    part = add_up(part, count=lax.axis_size(SHARED))
    part = lax.all_to_all(part, SHARED, 0, 0, tiled=True)
    halves = part.reshape(2, -1, cols)[:, :each].astype(F32)
    return jnp.concatenate([halves[0], halves[1]], axis=1)


def shards(c3, c4, top_down, lat3_weight, lat4_weight, conv_weight, p3_cot, m4_cot):
    count, height, width, depth3 = c3.shape
    depth4 = c4.shape[3]
    chans = conv_weight.shape[1]
    n3 = height * width
    n4 = n3 // 4
    n5 = n4 // 4
    stacked = depth3 + depth4 + 9 * chans
    owners = lax.axis_size(OWNERS)
    each = stacked // owners
    total_pixels = n3 * owners * lax.axis_size(SHARED)
    scale = 1.0 / math.sqrt(total_pixels)

    m3, col, row_a, row_b, *fetched = run_merge(
        width, c3.reshape(n3, depth3), c4.reshape(n4, depth4), top_down.reshape(n5, chans),
        lat3_weight, lat4_weight, p3_cot.reshape(n3, chans),
    )
    c4_v, lat4_v, _, c3_v, lat3_v, cot_v = fetched
    conv_v, m4_cot_v = run_fetch(m3, conv_weight, m4_cot.reshape(n4, chans))
    borders = swap_borders(col, row_a, row_b)
    partial, gradc = run_early(width, cot_v, conv_v, m3, borders[2])
    m3_grad_b, m4_grad_b, top_grad, term = run_grads(
        width, each, scale, partial, gradc, conv_v, m4_cot_v, c3_v, c4_v, m3, *borders[:2]
    )
    got = lax.ppermute(term[1], "core", [(0, 1), (1, 0)])
    p3, c3_grad, c4_grad = run_outputs(
        width, conv_v, lat3_v, lat4_v, m3, *borders, m3_grad_b, m4_grad_b
    )
    got, p3, c3_grad, c4_grad = lax.optimization_barrier((got, p3, c3_grad, c4_grad))
    weight_grads = add_grads(term, got, each)
    return (
        p3.reshape(count, height, width, chans),
        c3_grad.reshape(count, height, width, depth3),
        c4_grad.reshape(count, height // 2, width // 2, depth4),
        top_grad.reshape(top_down.shape),
        weight_grads,
    )


def solution(mesh):
    split = jax.sharding.Mesh(
        mesh.devices.reshape(8, 2, 4, 4, 2), ("y", "core", "x", "z_hi", "z_lo")
    )
    tiles = P(OWNERS, ROWS, "z_lo", None)
    return jax.shard_map(
        shards,
        mesh=split,
        in_specs=(tiles, tiles, tiles, P(), P(), P(), tiles, tiles),
        out_specs=(tiles, tiles, tiles, tiles, P(OWNERS, None)),
        check_vma=False,
    )
```

```python
import functools
import math

import jax
import jax.numpy as jnp
from jax import lax
from jax.experimental import pallas as pl
from jax.experimental.pallas import tpu as pltpu
from jax.sharding import PartitionSpec as P

F32 = jnp.float32
BF16 = jnp.bfloat16
ROWS = ("x", "z_hi")
OWNERS = ("y", "core")
SHARED = ("x", "z_hi", "z_lo")
SIZES = {"x": 4, "y": 8, "z": 8}
LIMIT = 32 * 1024 * 1024
NT = (((1,), (1,)), ((), ()))
TN = (((0,), (0,)), ((), ()))


def dot(lhs, rhs, dims=(((1,), (0,)), ((), ()))):
    return lax.dot_general(lhs, rhs, dims, preferred_element_type=F32)


def place_of_device():
    return lax.axis_index("core"), lax.axis_index("z_lo"), lax.axis_index("z_hi") % 2


def call(kernel, out_shape, scratch, flops, moved, fetched, held=()):
    in_vmem = pl.BlockSpec(memory_space=pltpu.VMEM)
    n, m, k = len(fetched), len(held), len(out_shape)

    def body(*refs):
        sources, refs = refs[:n], refs[n:]
        held_refs, refs = refs[:m], refs[m:]
        outs, refs = refs[:k], refs[k:]
        arrived, refs = refs[:n], refs[n:]
        if n == 0:
            kernel(place_of_device(), *held_refs, *outs, *refs)
            return
        copies = [
            pltpu.make_async_copy(source, target, refs[0].at[i])
            for i, (source, target) in enumerate(zip(sources, arrived))
        ]
        for copy in copies:
            copy.start()
        waits = [copy.wait for copy in copies]
        kernel(place_of_device(), waits, *arrived, *held_refs, *outs, *refs[1:])

    return pl.pallas_call(
        body,
        out_shape=list(out_shape) + [jax.ShapeDtypeStruct(x.shape, x.dtype) for x in fetched],
        in_specs=[pl.BlockSpec(memory_space=pltpu.HBM)] * n + [in_vmem] * m,
        out_specs=[in_vmem] * (k + n),
        scratch_shapes=([pltpu.SemaphoreType.DMA((n,))] if n else []) + scratch,
        compiler_params=pltpu.CompilerParams(vmem_limit_bytes=LIMIT),
        cost_estimate=pl.CostEstimate(flops=flops, bytes_accessed=moved, transcendentals=0),
    )(*[pltpu.with_memory_space_constraint(x, pltpu.HBM) for x in fetched], *held)


def merge_kernel(
    width4, place, waits, c4, lat4, top, c3, lat3, cot, m3, col, row_a, row_b, up4,
):
    n4, n5 = c4.shape[0], top.shape[0]
    n3 = c3.shape[0]
    width3, width5 = 2 * width4, width4 // 2
    row = lax.broadcasted_iota(jnp.int32, (n4, n5), 0)
    at = lax.broadcasted_iota(jnp.int32, (n4, n5), 1)
    source = (row // width4 // 2) * width5 + (row % width4) // 2
    pick = jnp.where(source == at, 1.0, 0.0).astype(BF16)
    for wait in waits[:3]:
        wait()
    m4 = dot(c4[...], lat4[...]) + dot(pick, top[...])
    for h in range(2):
        half = m4[:, 128 * h : 128 * h + 128]
        up4[h, pl.ds(0, n4, stride=2), :] = half
        up4[h, pl.ds(1, n4, stride=2), :] = half
    for wait in waits[3:5]:
        wait()
    lat = dot(c3[...], lat3[...])
    for y in range(n3 // width3):
        rows = slice(y * width3, (y + 1) * width3)
        above = slice((y // 2) * width3, (y // 2 + 1) * width3)
        for h in range(2):
            cols = slice(128 * h, 128 * h + 128)
            m3[rows, cols] = (lat[rows, cols] + up4[h, above]).astype(BF16)
    waits[5]()
    edge = jnp.where(place[1] == 0, width3 - 1, 0)
    lines = n3 // width3
    row = lax.broadcasted_iota(jnp.int32, (2 * lines, n3), 0)
    at = lax.broadcasted_iota(jnp.int32, (2 * lines, n3), 1)
    take_cot = jnp.where(at == row * width3 + edge, 1.0, 0.0).astype(BF16)
    take_m3 = jnp.where(at == (row - lines) * width3 + edge, 1.0, 0.0).astype(BF16)
    col[...] = (dot(take_cot, cot[...]) + dot(take_m3, m3[...])).astype(BF16)
    odd = place[2] == 1
    first = pl.multiple_of(jnp.where(odd, 0, n3 - width3), width3)
    second = pl.multiple_of(jnp.where(odd, n3 - width3, 0), width3)
    for start, out in ((first, row_a), (second, row_b)):
        out[:width3] = cot[pl.ds(start, width3)]
        out[width3 : 2 * width3] = m3[pl.ds(start, width3)]
        out[2 * width3 :] = jnp.zeros((2 * lines, out.shape[1]), BF16)


def shift_line(line, left, right):
    width = line.shape[0]
    at = lax.broadcasted_iota(jnp.int32, line.shape, 0)
    before = jnp.where(at == 0, left, pltpu.roll(line, 1, 0))
    after = jnp.where(at == width - 1, right, pltpu.roll(line, width - 1, 0))
    return before.astype(BF16), line.astype(BF16), after.astype(BF16)


def outer_lines(place, field, row_a, row_b, lines, width):
    odd = place[2] == 1
    rows = slice(field * width, (field + 1) * width)
    corner = slice(2 * width, 2 * width + 2 * lines)
    line_a, line_b = row_a[rows].astype(F32), row_b[rows].astype(F32)
    ends_a, ends_b = row_a[corner].astype(F32), row_b[corner].astype(F32)
    first, last = field * lines, (field + 1) * lines - 1
    return (
        (jnp.where(odd, line_a, line_b), jnp.where(odd, ends_a, ends_b)[last : last + 1]),
        (jnp.where(odd, line_b, line_a), jnp.where(odd, ends_b, ends_a)[first : first + 1]),
    )


def fill_line(place, shifted, y, line, side):
    to_the_left = jnp.where(place[1] == 1, 1.0, 0.0)
    width = line.shape[0]
    planes = shift_line(line, side * to_the_left, side * (1.0 - to_the_left))
    for i in range(3):
        shifted[i, y * width : (y + 1) * width] = planes[i]


def fill_inner(place, field, own, col, shifted, width):
    lines = own.shape[0] // width
    sides = col[...].astype(F32)
    for y in range(lines):
        side = sides[field * lines + y : field * lines + y + 1]
        fill_line(place, shifted, y + 1, own[y * width : (y + 1) * width].astype(F32), side)


def pieces_of(block, each):
    per = each // 16
    return block // per // 2, (block // per) % 2, block % per


def groups_of(core, x_lo, y, z):
    near = x_lo * 4 + (y + core) % 2 * 2 + (z + core) % 2
    return near, (y // 2) * (SIZES["z"] // 2) + z // 2


def group_lists():
    near, far = {}, {}
    index = 0
    for y in range(SIZES["y"]):
        for core in range(2):
            for x in range(SIZES["x"]):
                pair_x, x_lo = divmod((x + core) % SIZES["x"], 2)
                for z in range(SIZES["z"]):
                    pair_y = (y + core) % SIZES["y"] // 2
                    pair_z = (z + core) % SIZES["z"] // 2
                    in_near, in_far = groups_of(core, x_lo, y, z)
                    near.setdefault((core, pair_x, pair_y, pair_z), [None] * 8)[in_near] = index
                    far.setdefault((core, pair_x, in_near), [None] * 16)[in_far] = index
                    index += 1
    return list(near.values()), list(far.values())


def early_kernel(width, place, cot, conv, m3, col, partial, gradc, shifted):
    n3, chans = cot.shape
    blank = jnp.zeros((3, width, chans), BF16)
    shifted[:, :width] = blank
    shifted[:, n3 + width :] = blank
    fill_inner(place, 0, cot, col, shifted, width)
    m3_t = m3[...].T
    total = None
    for a in range(3):
        for b in range(3):
            tap = slice((3 * a + b) * chans, (3 * a + b + 1) * chans)
            field = shifted[2 - b, (2 - a) * width : (2 - a) * width + n3]
            part = dot(field, conv[tap], NT)
            total = part if total is None else total + part
            gradc[tap] = dot(m3_t, field)
    partial[...] = total


def grads_kernel(
    width, each, scale, place, partial, gradc, conv, m4_cot, c3, c4, m3, row_a, row_b,
    m3_grad_b, m4_grad_b, top_grad, term, total, sums, sums5,
):
    n3, chans = partial.shape
    n4 = c4.shape[0]
    me = place[0]
    per = each // 16

    def put(first, value):
        value = (value * scale).astype(BF16)
        for k in range(value.shape[0] // 16):
            y, owner, p = pieces_of(first // 16 + k, each)
            near, far = groups_of(owner, p // SIZES["z"], y, p % SIZES["z"])
            slot = jnp.where(me == owner, 0, 1)
            term[slot, near, far] = value[16 * k : 16 * k + 16]

    blank = jnp.zeros((16, chans), BF16)
    for y in range(SIZES["y"]):
        for p in range(per, 16):
            for owner in range(2):
                near, far = groups_of(owner, p // SIZES["z"], y, p % SIZES["z"])
                term[jnp.where(me == owner, 0, 1), near, far] = blank

    before, after = outer_lines(place, 0, row_a, row_b, n3 // width, width)
    to_the_left = jnp.where(place[1] == 1, 1.0, 0.0)
    total[...] = partial[...]
    added = {}
    for a, rows, (line, side) in (
        (2, slice(0, width), before),
        (0, slice(n3 - width, n3), after),
    ):
        planes = shift_line(line, side * to_the_left, side * (1.0 - to_the_left))
        part = total[rows]
        for b in range(3):
            tap = 3 * a + b
            part = part + dot(planes[2 - b], conv[tap * chans : (tap + 1) * chans], NT)
            added[tap] = (rows, planes[2 - b])
        total[rows] = part
    m3_grad_b[...] = total[...].astype(BF16)
    for y in range(n4 // (width // 2)):
        pair = total[2 * y * width : (2 * y + 1) * width] + total[(2 * y + 1) * width : (2 * y + 2) * width]
        sums[0, y * width : (y + 1) * width] = pair[:, :128]
        sums[1, y * width : (y + 1) * width] = pair[:, 128:]
    for h in range(2):
        cols = slice(128 * h, 128 * h + 128)
        m4_grad = (
            m4_cot[:, cols].astype(F32)
            + sums[h, pl.ds(0, n4, stride=2), :]
            + sums[h, pl.ds(1, n4, stride=2), :]
        )
        m4_grad_b[:, cols] = m4_grad.astype(BF16)
        half = width // 2
        for y in range(n4 // width):
            sums5[h, y * half : (y + 1) * half] = (
                m4_grad[2 * y * half : (2 * y + 1) * half]
                + m4_grad[(2 * y + 1) * half : (2 * y + 2) * half]
            )
        n5 = n4 // 4
        top_grad[:, cols] = (
            sums5[h, pl.ds(0, n5, stride=2), :] + sums5[h, pl.ds(1, n5, stride=2), :]
        ).astype(BF16)

    depth3, depth4 = c3.shape[1], c4.shape[1]
    put(0, dot(c3[...], m3_grad_b[...], TN))
    put(depth3, dot(c4[...], m4_grad_b[...], TN))
    for tap in range(9):
        value = gradc[tap * chans : (tap + 1) * chans]
        if tap in added:
            rows, plane = added[tap]
            value = value + dot(m3[rows], plane, TN)
        put(depth3 + depth4 + tap * chans, value)


def outputs_kernel(
    width, place, conv, lat3, lat4, m3, row_a, row_b, col, m3_grad_b, m4_grad_b,
    p3, c3_grad, c4_grad, shifted,
):
    n3, chans = m3.shape
    fill_inner(place, 1, m3, col, shifted, width)
    before, after = outer_lines(place, 1, row_a, row_b, n3 // width, width)
    fill_line(place, shifted, 0, *before)
    fill_line(place, shifted, n3 // width + 1, *after)
    total = None
    for a in range(3):
        for b in range(3):
            tap = 3 * a + b
            part = dot(shifted[b, a * width : a * width + n3], conv[tap * chans : (tap + 1) * chans])
            total = part if total is None else total + part
    p3[...] = total.astype(BF16)
    c3_grad[...] = dot(m3_grad_b[...], lat3[...], NT).astype(BF16)
    c4_grad[...] = dot(m4_grad_b[...], lat4[...], NT).astype(BF16)


def shape_of(*dims):
    return jax.ShapeDtypeStruct(dims, BF16)


def run_merge(width, c3, c4, top, lat3, lat4, cot):
    n3, n4, chans = c3.shape[0], c4.shape[0], lat3.shape[1]
    lines = n3 // width
    border = shape_of(2 * width + 2 * lines, chans)
    return call(
        functools.partial(merge_kernel, width // 2),
        [shape_of(n3, chans), shape_of(2 * lines, chans), border, border],
        [pltpu.VMEM((2, 2 * n4, 128), F32)],
        2 * chans * (c3.size + c4.size),
        2 * (c3.size + c4.size + lat3.size + lat4.size + 2 * cot.size),
        (c4, lat4, top, c3, lat3, cot),
    )


def fetch_kernel(place, waits, *refs):
    for wait in waits:
        wait()


def run_fetch(after, *arrays):
    moved = 2 * sum(x.size for x in arrays)
    return call(fetch_kernel, [], [], 0, moved, arrays, (after,))


def run_early(width, cot, conv, m3, col):
    n3, chans = cot.shape
    return call(
        functools.partial(early_kernel, width),
        [jax.ShapeDtypeStruct((n3, chans), F32), jax.ShapeDtypeStruct(conv.shape, F32)],
        [pltpu.VMEM((3, n3 + 2 * width, chans), BF16)],
        2 * chans * 2 * 9 * n3 * chans,
        8 * conv.size,
        (),
        (cot, conv, m3, col),
    )


def run_grads(width, each, scale, partial, gradc, conv, m4_cot, c3, c4, m3, row_a, row_b):
    n3, chans = partial.shape
    n4 = c4.shape[0]
    return call(
        functools.partial(grads_kernel, width, each, scale),
        [
            shape_of(n3, chans),
            shape_of(n4, chans),
            shape_of(n4 // 4, chans),
            shape_of(2, 8, 16, 16, chans),
        ],
        [
            pltpu.VMEM((n3, chans), F32),
            pltpu.VMEM((2, n3 // 2, 128), F32),
            pltpu.VMEM((2, n4 // 2, 128), F32),
        ],
        2 * chans * (c3.size + c4.size + 6 * width * chans),
        2 * (c3.size + c4.size + 4 * conv.size),
        (),
        (partial, gradc, conv, m4_cot, c3, c4, m3, row_a, row_b),
    )


def run_outputs(width, conv, lat3, lat4, m3, row_a, row_b, col, m3_grad_b, m4_grad_b):
    n3, chans = m3.shape
    n4 = m4_grad_b.shape[0]
    return call(
        functools.partial(outputs_kernel, width),
        [shape_of(n3, chans), shape_of(n3, lat3.shape[0]), shape_of(n4, lat4.shape[0])],
        [pltpu.VMEM((3, n3 + 2 * width, chans), BF16)],
        2 * chans * (n3 * lat3.shape[0] + n4 * lat4.shape[0] + 9 * n3 * chans),
        4 * (n3 * lat3.shape[0] + n4 * lat4.shape[0] + conv.size),
        (),
        (conv, lat3, lat4, m3, row_a, row_b, col, m3_grad_b, m4_grad_b),
    )


def swap_borders(col, row_a, row_b):
    col = lax.ppermute(col, "z_lo", [(0, 1), (1, 0)])
    n_rows = lax.axis_size(ROWS)
    pairs = [(i, i + 1) for i in range(0, n_rows - 1, 2)]
    between = [(i, i + 1) for i in range(1, n_rows - 1, 2)]
    start = (row_a.shape[0] - col.shape[0], 0)
    row_a = lax.dynamic_update_slice(row_a, col, start)
    row_b = lax.dynamic_update_slice(row_b, col, start)
    row_a = lax.ppermute(row_a, ROWS, pairs + [(j, i) for i, j in pairs])
    row_b = lax.ppermute(row_b, ROWS, between + [(j, i) for i, j in between])
    return row_a, row_b, col


def add_cores_kernel(term, got, out):
    out[...] = (term[0].astype(F32) + got[...].astype(F32)).astype(BF16)


def add_cores(term, got):
    in_vmem = pl.BlockSpec(memory_space=pltpu.VMEM)
    return pl.pallas_call(
        add_cores_kernel,
        out_shape=shape_of(*got.shape),
        in_specs=[in_vmem] * 2,
        out_specs=in_vmem,
        compiler_params=pltpu.CompilerParams(vmem_limit_bytes=LIMIT),
        cost_estimate=pl.CostEstimate(
            flops=got.size, bytes_accessed=6 * got.size, transcendentals=0
        ),
    )(term, got)


def add_kernel(count, *refs):
    parts, out = refs[:-1], refs[-1]
    total = None
    for part in parts:
        for i in range(part.shape[0]):
            value = part[i].astype(F32)
            total = value if total is None else total + value
    total = total.astype(BF16)
    if count is None:
        out[...] = total
    else:
        for i in range(count):
            out[i] = total


def add_up(*parts, count=None):
    shape = parts[0].shape[1:]
    in_vmem = pl.BlockSpec(memory_space=pltpu.VMEM)
    return pl.pallas_call(
        functools.partial(add_kernel, count),
        out_shape=shape_of(*shape) if count is None else shape_of(count, *shape),
        in_specs=[in_vmem] * len(parts),
        out_specs=in_vmem,
        compiler_params=pltpu.CompilerParams(vmem_limit_bytes=LIMIT),
        cost_estimate=pl.CostEstimate(
            flops=sum(p.size for p in parts),
            bytes_accessed=2 * sum(p.size for p in parts),
            transcendentals=0,
        ),
    )(*parts)


def finish_kernel(parts, out):
    core = lax.axis_index("core")
    rows = parts.shape[2]
    for x_lo in range(2):
        x = jnp.where(core == x_lo, 0, 1)
        for z in range(parts.shape[1]):
            first = (x_lo * parts.shape[1] + z) * rows
            if first < out.shape[0]:
                value = parts[x, z].astype(F32) + parts[x + 2, z].astype(F32)
                out[first : first + rows] = value


def add_grads(term, got, each):
    everyone = OWNERS + SHARED
    near_groups, far_groups = group_lists()
    _, near, far, rows, cols = term.shape
    part = add_cores(term, got)
    part = lax.all_to_all(part.reshape(near, far * rows, cols), everyone, 0, 0, axis_index_groups=near_groups, tiled=True)
    part = add_up(part)
    part = lax.all_to_all(part.reshape(far, rows, cols), everyone, 0, 0, axis_index_groups=far_groups, tiled=True)
    part = add_up(part, count=lax.axis_size(SHARED))
    part = lax.all_to_all(part, SHARED, 0, 0, tiled=True)
    in_vmem = pl.BlockSpec(memory_space=pltpu.VMEM)
    return pl.pallas_call(
        finish_kernel,
        out_shape=jax.ShapeDtypeStruct((each, cols), F32),
        in_specs=[in_vmem],
        out_specs=in_vmem,
        compiler_params=pltpu.CompilerParams(vmem_limit_bytes=LIMIT),
    )(part.reshape(SIZES["x"], SIZES["z"], rows, cols))


def shards(c3, c4, top_down, lat3_weight, lat4_weight, conv_weight, p3_cot, m4_cot):
    count, height, width, depth3 = c3.shape
    depth4 = c4.shape[3]
    chans = conv_weight.shape[1]
    n3 = height * width
    n4 = n3 // 4
    n5 = n4 // 4
    stacked = depth3 + depth4 + 9 * chans
    owners = lax.axis_size(OWNERS)
    each = stacked // owners
    total_pixels = n3 * owners * lax.axis_size(SHARED)
    scale = 1.0 / math.sqrt(total_pixels)

    m3, col, row_a, row_b, *fetched = run_merge(
        width, c3.reshape(n3, depth3), c4.reshape(n4, depth4), top_down.reshape(n5, chans),
        lat3_weight, lat4_weight, p3_cot.reshape(n3, chans),
    )
    c4_v, lat4_v, _, c3_v, lat3_v, cot_v = fetched
    conv_v, m4_cot_v = run_fetch(m3, conv_weight, m4_cot.reshape(n4, chans))
    borders = swap_borders(col, row_a, row_b)
    partial, gradc = run_early(width, cot_v, conv_v, m3, borders[2])
    m3_grad_b, m4_grad_b, top_grad, term = run_grads(
        width, each, scale, partial, gradc, conv_v, m4_cot_v, c3_v, c4_v, m3, *borders[:2]
    )
    got = lax.ppermute(term[1], "core", [(0, 1), (1, 0)])
    p3, c3_grad, c4_grad = run_outputs(
        width, conv_v, lat3_v, lat4_v, m3, *borders, m3_grad_b, m4_grad_b
    )
    got, p3, c3_grad, c4_grad = lax.optimization_barrier((got, p3, c3_grad, c4_grad))
    weight_grads = add_grads(term, got, each)
    return (
        p3.reshape(count, height, width, chans),
        c3_grad.reshape(count, height, width, depth3),
        c4_grad.reshape(count, height // 2, width // 2, depth4),
        top_grad.reshape(top_down.shape),
        weight_grads,
    )


def solution(mesh):
    split = jax.sharding.Mesh(
        mesh.devices.reshape(8, 2, 4, 4, 2), ("y", "core", "x", "z_hi", "z_lo")
    )
    tiles = P(OWNERS, ROWS, "z_lo", None)
    return jax.shard_map(
        shards,
        mesh=split,
        in_specs=(tiles, tiles, tiles, P(), P(), P(), tiles, tiles),
        out_specs=(tiles, tiles, tiles, tiles, P(OWNERS, None)),
        check_vma=False,
    )
```

```python
import functools
import math

import jax
import jax.numpy as jnp
from jax import lax
from jax.experimental import pallas as pl
from jax.experimental.pallas import tpu as pltpu
from jax.sharding import PartitionSpec as P

F32 = jnp.float32
BF16 = jnp.bfloat16
ROWS = ("x", "z_hi")
OWNERS = ("y", "core")
SHARED = ("x", "z_hi", "z_lo")
SIZES = {"x": 4, "y": 8, "z": 8}
LIMIT = 32 * 1024 * 1024
NT = (((1,), (1,)), ((), ()))
TN = (((0,), (0,)), ((), ()))


def dot(lhs, rhs, dims=(((1,), (0,)), ((), ()))):
    return lax.dot_general(lhs, rhs, dims, preferred_element_type=F32)


def place_of_device():
    return lax.axis_index("core"), lax.axis_index("z_lo"), lax.axis_index("z_hi") % 2


def call(kernel, out_shape, scratch, flops, moved, fetched, held=()):
    in_vmem = pl.BlockSpec(memory_space=pltpu.VMEM)
    n, m, k = len(fetched), len(held), len(out_shape)

    def body(*refs):
        sources, refs = refs[:n], refs[n:]
        held_refs, refs = refs[:m], refs[m:]
        outs, refs = refs[:k], refs[k:]
        arrived, refs = refs[:n], refs[n:]
        if n == 0:
            kernel(place_of_device(), *held_refs, *outs, *refs)
            return
        copies = [
            pltpu.make_async_copy(source, target, refs[0].at[i])
            for i, (source, target) in enumerate(zip(sources, arrived))
        ]
        for copy in copies:
            copy.start()
        waits = [copy.wait for copy in copies]
        kernel(place_of_device(), waits, *arrived, *held_refs, *outs, *refs[1:])

    return pl.pallas_call(
        body,
        out_shape=list(out_shape) + [jax.ShapeDtypeStruct(x.shape, x.dtype) for x in fetched],
        in_specs=[pl.BlockSpec(memory_space=pltpu.HBM)] * n + [in_vmem] * m,
        out_specs=[in_vmem] * (k + n),
        scratch_shapes=([pltpu.SemaphoreType.DMA((n,))] if n else []) + scratch,
        compiler_params=pltpu.CompilerParams(vmem_limit_bytes=LIMIT),
        cost_estimate=pl.CostEstimate(flops=flops, bytes_accessed=moved, transcendentals=0),
    )(*[pltpu.with_memory_space_constraint(x, pltpu.HBM) for x in fetched], *held)


def merge_kernel(
    width4, place, waits, c4, lat4, top, c3, lat3, cot, m3, col, row_a, row_b, up4,
):
    n4, n5 = c4.shape[0], top.shape[0]
    n3 = c3.shape[0]
    width3, width5 = 2 * width4, width4 // 2
    row = lax.broadcasted_iota(jnp.int32, (n4, n5), 0)
    at = lax.broadcasted_iota(jnp.int32, (n4, n5), 1)
    source = (row // width4 // 2) * width5 + (row % width4) // 2
    pick = jnp.where(source == at, 1.0, 0.0).astype(BF16)
    for wait in waits[:3]:
        wait()
    m4 = dot(c4[...], lat4[...]) + dot(pick, top[...])
    for h in range(2):
        half = m4[:, 128 * h : 128 * h + 128]
        up4[h, pl.ds(0, n4, stride=2), :] = half
        up4[h, pl.ds(1, n4, stride=2), :] = half
    for wait in waits[3:5]:
        wait()
    lat = dot(c3[...], lat3[...])
    for y in range(n3 // width3):
        rows = slice(y * width3, (y + 1) * width3)
        above = slice((y // 2) * width3, (y // 2 + 1) * width3)
        for h in range(2):
            cols = slice(128 * h, 128 * h + 128)
            m3[rows, cols] = (lat[rows, cols] + up4[h, above]).astype(BF16)
    waits[5]()
    edge = jnp.where(place[1] == 0, width3 - 1, 0)
    lines = n3 // width3
    row = lax.broadcasted_iota(jnp.int32, (2 * lines, n3), 0)
    at = lax.broadcasted_iota(jnp.int32, (2 * lines, n3), 1)
    take_cot = jnp.where(at == row * width3 + edge, 1.0, 0.0).astype(BF16)
    take_m3 = jnp.where(at == (row - lines) * width3 + edge, 1.0, 0.0).astype(BF16)
    col[...] = (dot(take_cot, cot[...]) + dot(take_m3, m3[...])).astype(BF16)
    odd = place[2] == 1
    first = pl.multiple_of(jnp.where(odd, 0, n3 - width3), width3)
    second = pl.multiple_of(jnp.where(odd, n3 - width3, 0), width3)
    for start, out in ((first, row_a), (second, row_b)):
        out[:width3] = cot[pl.ds(start, width3)]
        out[width3 : 2 * width3] = m3[pl.ds(start, width3)]


def shift_line(line, left, right):
    width = line.shape[0]
    at = lax.broadcasted_iota(jnp.int32, line.shape, 0)
    before = jnp.where(at == 0, left, pltpu.roll(line, 1, 0))
    after = jnp.where(at == width - 1, right, pltpu.roll(line, width - 1, 0))
    return before.astype(BF16), line.astype(BF16), after.astype(BF16)


def outer_lines(place, field, row_a, row_b, end_a, end_b, lines, width):
    odd = place[2] == 1
    rows = slice(field * width, (field + 1) * width)
    line_a, line_b = row_a[rows].astype(F32), row_b[rows].astype(F32)
    ends_a, ends_b = end_a[...].astype(F32), end_b[...].astype(F32)
    first, last = field * lines, (field + 1) * lines - 1
    return (
        (jnp.where(odd, line_a, line_b), jnp.where(odd, ends_a, ends_b)[last : last + 1]),
        (jnp.where(odd, line_b, line_a), jnp.where(odd, ends_b, ends_a)[first : first + 1]),
    )


def fill_line(place, shifted, y, line, side):
    to_the_left = jnp.where(place[1] == 1, 1.0, 0.0)
    width = line.shape[0]
    planes = shift_line(line, side * to_the_left, side * (1.0 - to_the_left))
    for i in range(3):
        shifted[i, y * width : (y + 1) * width] = planes[i]


def fill_inner(place, field, own, col, shifted, width):
    lines = own.shape[0] // width
    sides = col[...].astype(F32)
    for y in range(lines):
        side = sides[field * lines + y : field * lines + y + 1]
        fill_line(place, shifted, y + 1, own[y * width : (y + 1) * width].astype(F32), side)


def pieces_of(block, each):
    per = each // 16
    return block // per // 2, (block // per) % 2, block % per


def groups_of(x_lo, y, z):
    return x_lo * 4 + y % 2 * 2 + z % 2, (y // 2) * (SIZES["z"] // 2) + z // 2


def group_lists():
    near, far = {}, {}
    index = 0
    for y in range(SIZES["y"]):
        for core in range(2):
            for x in range(SIZES["x"]):
                pair_x = (x + core) % SIZES["x"] // 2
                for z in range(SIZES["z"]):
                    pair_y = (y + core) % SIZES["y"] // 2
                    pair_z = (z + core) % SIZES["z"] // 2
                    in_near, in_far = groups_of(x % 2, y, z)
                    near.setdefault((core, pair_x, pair_y, pair_z), [None] * 8)[in_near] = index
                    far.setdefault((core, pair_x, in_near), [None] * 16)[in_far] = index
                    index += 1
    return list(near.values()), list(far.values())


def early_kernel(width, place, cot, conv, m3, col, partial, gradc, shifted):
    n3, chans = cot.shape
    blank = jnp.zeros((3, width, chans), BF16)
    shifted[:, :width] = blank
    shifted[:, n3 + width :] = blank
    fill_inner(place, 0, cot, col, shifted, width)
    m3_t = m3[...].T
    total = None
    for a in range(3):
        for b in range(3):
            tap = slice((3 * a + b) * chans, (3 * a + b + 1) * chans)
            field = shifted[2 - b, (2 - a) * width : (2 - a) * width + n3]
            part = dot(field, conv[tap], NT)
            total = part if total is None else total + part
            gradc[tap] = dot(m3_t, field)
    partial[...] = total


def grads_kernel(
    width, each, scale, place, partial, gradc, conv, m4_cot, c3, c4, m3, row_a, row_b, end_a, end_b,
    m3_grad_b, m4_grad_b, top_grad, term, total, sums, sums5,
):
    n3, chans = partial.shape
    n4 = c4.shape[0]
    me = place[0]
    per = each // 16

    def put(first, value):
        value = (value * scale).astype(BF16)
        for k in range(value.shape[0] // 16):
            y, owner, p = pieces_of(first // 16 + k, each)
            near, far = groups_of(p // SIZES["z"], y, p % SIZES["z"])
            slot = jnp.where(me == owner, 0, 1)
            term[slot, near, far] = value[16 * k : 16 * k + 16]

    blank = jnp.zeros((16, chans), BF16)
    for y in range(SIZES["y"]):
        for p in range(per, 16):
            near, far = groups_of(p // SIZES["z"], y, p % SIZES["z"])
            for slot in range(2):
                term[slot, near, far] = blank

    before, after = outer_lines(place, 0, row_a, row_b, end_a, end_b, n3 // width, width)
    to_the_left = jnp.where(place[1] == 1, 1.0, 0.0)
    total[...] = partial[...]
    added = {}
    for a, rows, (line, side) in (
        (2, slice(0, width), before),
        (0, slice(n3 - width, n3), after),
    ):
        planes = shift_line(line, side * to_the_left, side * (1.0 - to_the_left))
        part = total[rows]
        for b in range(3):
            tap = 3 * a + b
            part = part + dot(planes[2 - b], conv[tap * chans : (tap + 1) * chans], NT)
            added[tap] = (rows, planes[2 - b])
        total[rows] = part
    m3_grad_b[...] = total[...].astype(BF16)
    for y in range(n4 // (width // 2)):
        pair = total[2 * y * width : (2 * y + 1) * width] + total[(2 * y + 1) * width : (2 * y + 2) * width]
        sums[0, y * width : (y + 1) * width] = pair[:, :128]
        sums[1, y * width : (y + 1) * width] = pair[:, 128:]
    for h in range(2):
        cols = slice(128 * h, 128 * h + 128)
        m4_grad = (
            m4_cot[:, cols].astype(F32)
            + sums[h, pl.ds(0, n4, stride=2), :]
            + sums[h, pl.ds(1, n4, stride=2), :]
        )
        m4_grad_b[:, cols] = m4_grad.astype(BF16)
        half = width // 2
        for y in range(n4 // width):
            sums5[h, y * half : (y + 1) * half] = (
                m4_grad[2 * y * half : (2 * y + 1) * half]
                + m4_grad[(2 * y + 1) * half : (2 * y + 2) * half]
            )
        n5 = n4 // 4
        top_grad[:, cols] = (
            sums5[h, pl.ds(0, n5, stride=2), :] + sums5[h, pl.ds(1, n5, stride=2), :]
        ).astype(BF16)

    depth3, depth4 = c3.shape[1], c4.shape[1]
    put(0, dot(c3[...], m3_grad_b[...], TN))
    put(depth3, dot(c4[...], m4_grad_b[...], TN))
    for tap in range(9):
        value = gradc[tap * chans : (tap + 1) * chans]
        if tap in added:
            rows, plane = added[tap]
            value = value + dot(m3[rows], plane, TN)
        put(depth3 + depth4 + tap * chans, value)


def outputs_kernel(
    width, place, conv, lat3, lat4, m3, row_a, row_b, end_a, end_b, col, m3_grad_b, m4_grad_b,
    p3, c3_grad, c4_grad, shifted,
):
    n3, chans = m3.shape
    fill_inner(place, 1, m3, col, shifted, width)
    before, after = outer_lines(place, 1, row_a, row_b, end_a, end_b, n3 // width, width)
    fill_line(place, shifted, 0, *before)
    fill_line(place, shifted, n3 // width + 1, *after)
    total = None
    for a in range(3):
        for b in range(3):
            tap = 3 * a + b
            part = dot(shifted[b, a * width : a * width + n3], conv[tap * chans : (tap + 1) * chans])
            total = part if total is None else total + part
    p3[...] = total.astype(BF16)
    c3_grad[...] = dot(m3_grad_b[...], lat3[...], NT).astype(BF16)
    c4_grad[...] = dot(m4_grad_b[...], lat4[...], NT).astype(BF16)


def shape_of(*dims):
    return jax.ShapeDtypeStruct(dims, BF16)


def run_merge(width, c3, c4, top, lat3, lat4, cot):
    n3, n4, chans = c3.shape[0], c4.shape[0], lat3.shape[1]
    lines = n3 // width
    border = shape_of(2 * width, chans)
    return call(
        functools.partial(merge_kernel, width // 2),
        [shape_of(n3, chans), shape_of(2 * lines, chans), border, border],
        [pltpu.VMEM((2, 2 * n4, 128), F32)],
        2 * chans * (c3.size + c4.size),
        2 * (c3.size + c4.size + lat3.size + lat4.size + 2 * cot.size),
        (c4, lat4, top, c3, lat3, cot),
    )


def fetch_kernel(place, waits, *refs):
    for wait in waits:
        wait()


def run_fetch(after, *arrays):
    moved = 2 * sum(x.size for x in arrays)
    return call(fetch_kernel, [], [], 0, moved, arrays, (after,))


def run_early(width, cot, conv, m3, col):
    n3, chans = cot.shape
    return call(
        functools.partial(early_kernel, width),
        [jax.ShapeDtypeStruct((n3, chans), F32), jax.ShapeDtypeStruct(conv.shape, F32)],
        [pltpu.VMEM((3, n3 + 2 * width, chans), BF16)],
        2 * chans * 2 * 9 * n3 * chans,
        8 * conv.size,
        (),
        (cot, conv, m3, col),
    )


def run_grads(width, each, scale, partial, gradc, conv, m4_cot, c3, c4, m3, *borders):
    n3, chans = partial.shape
    n4 = c4.shape[0]
    return call(
        functools.partial(grads_kernel, width, each, scale),
        [
            shape_of(n3, chans),
            shape_of(n4, chans),
            shape_of(n4 // 4, chans),
            shape_of(2, 8, 16, 16, chans),
        ],
        [
            pltpu.VMEM((n3, chans), F32),
            pltpu.VMEM((2, n3 // 2, 128), F32),
            pltpu.VMEM((2, n4 // 2, 128), F32),
        ],
        2 * chans * (c3.size + c4.size + 6 * width * chans),
        2 * (c3.size + c4.size + 4 * conv.size),
        (),
        (partial, gradc, conv, m4_cot, c3, c4, m3, *borders),
    )


def run_outputs(width, conv, lat3, lat4, m3, row_a, row_b, end_a, end_b, col, m3_grad_b, m4_grad_b):
    n3, chans = m3.shape
    n4 = m4_grad_b.shape[0]
    return call(
        functools.partial(outputs_kernel, width),
        [shape_of(n3, chans), shape_of(n3, lat3.shape[0]), shape_of(n4, lat4.shape[0])],
        [pltpu.VMEM((3, n3 + 2 * width, chans), BF16)],
        2 * chans * (n3 * lat3.shape[0] + n4 * lat4.shape[0] + 9 * n3 * chans),
        4 * (n3 * lat3.shape[0] + n4 * lat4.shape[0] + conv.size),
        (),
        (conv, lat3, lat4, m3, row_a, row_b, end_a, end_b, col, m3_grad_b, m4_grad_b),
    )


def swap_borders(col, row_a, row_b):
    n_rows = lax.axis_size(ROWS)

    def both_ways(pairs):
        return pairs + [(j, i) for i, j in pairs]

    swapped = []
    for first, row in ((0, row_a), (1, row_b)):
        pairs = [(i, i + 1) for i in range(first, n_rows - 1, 2)]
        across = [(2 * i + z, 2 * j + 1 - z) for i, j in pairs for z in range(2)]
        swapped.append(
            (
                lax.ppermute(row, ROWS, both_ways(pairs)),
                lax.ppermute(col, ROWS + ("z_lo",), both_ways(across)),
            )
        )
    col = lax.ppermute(col, "z_lo", [(0, 1), (1, 0)])
    (row_a, end_a), (row_b, end_b) = swapped
    return row_a, row_b, end_a, end_b, col


def add_cores_kernel(term, got, out):
    out[...] = (term[0].astype(F32) + got[...].astype(F32)).astype(BF16)


def add_cores(term, got):
    in_vmem = pl.BlockSpec(memory_space=pltpu.VMEM)
    return pl.pallas_call(
        add_cores_kernel,
        out_shape=shape_of(*got.shape),
        in_specs=[in_vmem] * 2,
        out_specs=in_vmem,
        compiler_params=pltpu.CompilerParams(vmem_limit_bytes=LIMIT),
        cost_estimate=pl.CostEstimate(
            flops=got.size, bytes_accessed=6 * got.size, transcendentals=0
        ),
    )(term, got)


def add_kernel(count, *refs):
    parts, out = refs[:-1], refs[-1]
    total = None
    for part in parts:
        for i in range(part.shape[0]):
            value = part[i].astype(F32)
            total = value if total is None else total + value
    total = total.astype(BF16)
    if count is None:
        out[...] = total
    else:
        for i in range(count):
            out[i] = total


def add_up(*parts, count=None):
    shape = parts[0].shape[1:]
    in_vmem = pl.BlockSpec(memory_space=pltpu.VMEM)
    return pl.pallas_call(
        functools.partial(add_kernel, count),
        out_shape=shape_of(*shape) if count is None else shape_of(count, *shape),
        in_specs=[in_vmem] * len(parts),
        out_specs=in_vmem,
        compiler_params=pltpu.CompilerParams(vmem_limit_bytes=LIMIT),
        cost_estimate=pl.CostEstimate(
            flops=sum(p.size for p in parts),
            bytes_accessed=2 * sum(p.size for p in parts),
            transcendentals=0,
        ),
    )(*parts)


def finish_kernel(parts, out):
    rows = parts.shape[2]
    for x in range(2):
        for z in range(parts.shape[1]):
            first = (x * parts.shape[1] + z) * rows
            if first < out.shape[0]:
                out[first : first + rows] = parts[x, z].astype(F32) + parts[x + 2, z].astype(F32)


def add_grads(term, got, each):
    everyone = OWNERS + SHARED
    near_groups, far_groups = group_lists()
    _, near, far, rows, cols = term.shape
    part = add_cores(term, got)
    part = lax.all_to_all(part.reshape(near, far * rows, cols), everyone, 0, 0, axis_index_groups=near_groups, tiled=True)
    part = add_up(part)
    part = lax.all_to_all(part.reshape(far, rows, cols), everyone, 0, 0, axis_index_groups=far_groups, tiled=True)
    part = add_up(part, count=lax.axis_size(SHARED))
    part = lax.all_to_all(part, SHARED, 0, 0, tiled=True)
    in_vmem = pl.BlockSpec(memory_space=pltpu.VMEM)
    return pl.pallas_call(
        finish_kernel,
        out_shape=jax.ShapeDtypeStruct((each, cols), F32),
        in_specs=[in_vmem],
        out_specs=in_vmem,
        compiler_params=pltpu.CompilerParams(vmem_limit_bytes=LIMIT),
    )(part.reshape(SIZES["x"], SIZES["z"], rows, cols))


def shards(c3, c4, top_down, lat3_weight, lat4_weight, conv_weight, p3_cot, m4_cot):
    count, height, width, depth3 = c3.shape
    depth4 = c4.shape[3]
    chans = conv_weight.shape[1]
    n3 = height * width
    n4 = n3 // 4
    n5 = n4 // 4
    stacked = depth3 + depth4 + 9 * chans
    owners = lax.axis_size(OWNERS)
    each = stacked // owners
    total_pixels = n3 * owners * lax.axis_size(SHARED)
    scale = 1.0 / math.sqrt(total_pixels)

    m3, col, row_a, row_b, *fetched = run_merge(
        width, c3.reshape(n3, depth3), c4.reshape(n4, depth4), top_down.reshape(n5, chans),
        lat3_weight, lat4_weight, p3_cot.reshape(n3, chans),
    )
    c4_v, lat4_v, _, c3_v, lat3_v, cot_v = fetched
    conv_v, m4_cot_v = run_fetch(m3, conv_weight, m4_cot.reshape(n4, chans))
    borders = swap_borders(col, row_a, row_b)
    partial, gradc = run_early(width, cot_v, conv_v, m3, borders[-1])
    m3_grad_b, m4_grad_b, top_grad, term = run_grads(
        width, each, scale, partial, gradc, conv_v, m4_cot_v, c3_v, c4_v, m3, *borders[:-1]
    )
    got = lax.ppermute(term[1], "core", [(0, 1), (1, 0)])
    p3, c3_grad, c4_grad = run_outputs(
        width, conv_v, lat3_v, lat4_v, m3, *borders, m3_grad_b, m4_grad_b
    )
    got, p3, c3_grad, c4_grad = lax.optimization_barrier((got, p3, c3_grad, c4_grad))
    weight_grads = add_grads(term, got, each)
    return (
        p3.reshape(count, height, width, chans),
        c3_grad.reshape(count, height, width, depth3),
        c4_grad.reshape(count, height // 2, width // 2, depth4),
        top_grad.reshape(top_down.shape),
        weight_grads,
    )


def solution(mesh):
    split = jax.sharding.Mesh(
        mesh.devices.reshape(8, 2, 4, 4, 2), ("y", "core", "x", "z_hi", "z_lo")
    )
    tiles = P(OWNERS, ROWS, "z_lo", None)
    return jax.shard_map(
        shards,
        mesh=split,
        in_specs=(tiles, tiles, tiles, P(), P(), P(), tiles, tiles),
        out_specs=(tiles, tiles, tiles, tiles, P(OWNERS, None)),
        check_vma=False,
    )
```

```python
import functools
import math

import jax
import jax.numpy as jnp
from jax import lax
from jax.experimental import pallas as pl
from jax.experimental.pallas import tpu as pltpu
from jax.sharding import PartitionSpec as P

F32 = jnp.float32
BF16 = jnp.bfloat16
ROWS = ("x", "z_hi")
OWNERS = ("y", "core")
SHARED = ("x", "z_hi", "z_lo")
SIZES = {"x": 4, "y": 8, "z": 8}
LIMIT = 32 * 1024 * 1024
NT = (((1,), (1,)), ((), ()))
TN = (((0,), (0,)), ((), ()))


def dot(lhs, rhs, dims=(((1,), (0,)), ((), ()))):
    return lax.dot_general(lhs, rhs, dims, preferred_element_type=F32)


def place_of_device():
    core = lax.axis_index("core")
    return core, lax.axis_index("z_lo"), (lax.axis_index("z_hi") + core) % 2


def call(kernel, out_shape, scratch, flops, moved, fetched, held=()):
    in_vmem = pl.BlockSpec(memory_space=pltpu.VMEM)
    n, m, k = len(fetched), len(held), len(out_shape)

    def body(*refs):
        sources, refs = refs[:n], refs[n:]
        held_refs, refs = refs[:m], refs[m:]
        outs, refs = refs[:k], refs[k:]
        arrived, refs = refs[:n], refs[n:]
        if n == 0:
            kernel(place_of_device(), *held_refs, *outs, *refs)
            return
        copies = [
            pltpu.make_async_copy(source, target, refs[0].at[i])
            for i, (source, target) in enumerate(zip(sources, arrived))
        ]
        for copy in copies:
            copy.start()
        waits = [copy.wait for copy in copies]
        kernel(place_of_device(), waits, *arrived, *held_refs, *outs, *refs[1:])

    return pl.pallas_call(
        body,
        out_shape=list(out_shape) + [jax.ShapeDtypeStruct(x.shape, x.dtype) for x in fetched],
        in_specs=[pl.BlockSpec(memory_space=pltpu.HBM)] * n + [in_vmem] * m,
        out_specs=[in_vmem] * (k + n),
        scratch_shapes=([pltpu.SemaphoreType.DMA((n,))] if n else []) + scratch,
        compiler_params=pltpu.CompilerParams(vmem_limit_bytes=LIMIT),
        cost_estimate=pl.CostEstimate(flops=flops, bytes_accessed=moved, transcendentals=0),
    )(*[pltpu.with_memory_space_constraint(x, pltpu.HBM) for x in fetched], *held)


def merge_kernel(
    width4, place, waits, c4, lat4, top, c3, lat3, cot, m3, col, row_a, row_b, up4,
):
    n4, n5 = c4.shape[0], top.shape[0]
    n3 = c3.shape[0]
    width3, width5 = 2 * width4, width4 // 2
    row = lax.broadcasted_iota(jnp.int32, (n4, n5), 0)
    at = lax.broadcasted_iota(jnp.int32, (n4, n5), 1)
    source = (row // width4 // 2) * width5 + (row % width4) // 2
    pick = jnp.where(source == at, 1.0, 0.0).astype(BF16)
    for wait in waits[:3]:
        wait()
    m4 = dot(c4[...], lat4[...]) + dot(pick, top[...])
    for h in range(2):
        half = m4[:, 128 * h : 128 * h + 128]
        up4[h, pl.ds(0, n4, stride=2), :] = half
        up4[h, pl.ds(1, n4, stride=2), :] = half
    for wait in waits[3:5]:
        wait()
    lat = dot(c3[...], lat3[...])
    for y in range(n3 // width3):
        rows = slice(y * width3, (y + 1) * width3)
        above = slice((y // 2) * width3, (y // 2 + 1) * width3)
        for h in range(2):
            cols = slice(128 * h, 128 * h + 128)
            m3[rows, cols] = (lat[rows, cols] + up4[h, above]).astype(BF16)
    waits[5]()
    edge = jnp.where(place[1] == 0, width3 - 1, 0)
    lines = n3 // width3
    row = lax.broadcasted_iota(jnp.int32, (2 * lines, n3), 0)
    at = lax.broadcasted_iota(jnp.int32, (2 * lines, n3), 1)
    take_cot = jnp.where(at == row * width3 + edge, 1.0, 0.0).astype(BF16)
    take_m3 = jnp.where(at == (row - lines) * width3 + edge, 1.0, 0.0).astype(BF16)
    col[...] = (dot(take_cot, cot[...]) + dot(take_m3, m3[...])).astype(BF16)
    odd = place[2] == 1
    first = pl.multiple_of(jnp.where(odd, 0, n3 - width3), width3)
    second = pl.multiple_of(jnp.where(odd, n3 - width3, 0), width3)
    for start, out in ((first, row_a), (second, row_b)):
        out[:width3] = cot[pl.ds(start, width3)]
        out[width3 : 2 * width3] = m3[pl.ds(start, width3)]
        out[2 * width3 :] = jnp.zeros((2 * lines, out.shape[1]), BF16)


def shift_line(line, left, right):
    width = line.shape[0]
    at = lax.broadcasted_iota(jnp.int32, line.shape, 0)
    before = jnp.where(at == 0, left, pltpu.roll(line, 1, 0))
    after = jnp.where(at == width - 1, right, pltpu.roll(line, width - 1, 0))
    return before.astype(BF16), line.astype(BF16), after.astype(BF16)


def outer_lines(place, field, row_a, row_b, lines, width):
    odd = place[2] == 1
    rows = slice(field * width, (field + 1) * width)
    corner = slice(2 * width, 2 * width + 2 * lines)
    line_a, line_b = row_a[rows].astype(F32), row_b[rows].astype(F32)
    ends_a, ends_b = row_a[corner].astype(F32), row_b[corner].astype(F32)
    first, last = field * lines, (field + 1) * lines - 1
    return (
        (jnp.where(odd, line_a, line_b), jnp.where(odd, ends_a, ends_b)[last : last + 1]),
        (jnp.where(odd, line_b, line_a), jnp.where(odd, ends_b, ends_a)[first : first + 1]),
    )


def fill_line(place, shifted, y, line, side):
    to_the_left = jnp.where(place[1] == 1, 1.0, 0.0)
    width = line.shape[0]
    planes = shift_line(line, side * to_the_left, side * (1.0 - to_the_left))
    for i in range(3):
        shifted[i, y * width : (y + 1) * width] = planes[i]


def fill_inner(place, field, own, col, shifted, width):
    lines = own.shape[0] // width
    sides = col[...].astype(F32)
    for y in range(lines):
        side = sides[field * lines + y : field * lines + y + 1]
        fill_line(place, shifted, y + 1, own[y * width : (y + 1) * width].astype(F32), side)


def pieces_of(block, each):
    per = each // 16
    return block // per // 2, (block // per) % 2, block % per


def groups_of(core, x_lo, y, z):
    near = x_lo * 4 + (y + core) % 2 * 2 + (z + core) % 2
    return near, (y // 2) * (SIZES["z"] // 2) + z // 2


def group_lists():
    near, far = {}, {}
    index = 0
    for y in range(SIZES["y"]):
        for core in range(2):
            for x in range(SIZES["x"]):
                pair_x, x_lo = divmod((x + core) % SIZES["x"], 2)
                for z in range(SIZES["z"]):
                    pair_y = (y + core) % SIZES["y"] // 2
                    pair_z = (z + core) % SIZES["z"] // 2
                    in_near, in_far = groups_of(core, x_lo, y, z)
                    near.setdefault((core, pair_x, pair_y, pair_z), [None] * 8)[in_near] = index
                    far.setdefault((core, pair_x, in_near), [None] * 16)[in_far] = index
                    index += 1
    return list(near.values()), list(far.values())


def shared_lists():
    n = SIZES["x"] * SIZES["z"]
    lists = []
    for owner in range(2 * SIZES["y"]):
        group = [owner * n + i for i in range(n)]
        turn = owner % 2 * (n // 2)
        lists.append(group[turn:] + group[:turn])
    return lists


def early_kernel(width, place, cot, conv, m3, col, partial, gradc, shifted):
    n3, chans = cot.shape
    blank = jnp.zeros((3, width, chans), BF16)
    shifted[:, :width] = blank
    shifted[:, n3 + width :] = blank
    fill_inner(place, 0, cot, col, shifted, width)
    m3_t = m3[...].T
    total = None
    for a in range(3):
        for b in range(3):
            tap = slice((3 * a + b) * chans, (3 * a + b + 1) * chans)
            field = shifted[2 - b, (2 - a) * width : (2 - a) * width + n3]
            part = dot(field, conv[tap], NT)
            total = part if total is None else total + part
            gradc[tap] = dot(m3_t, field)
    partial[...] = total


def grads_kernel(
    width, each, scale, place, partial, gradc, conv, m4_cot, c3, c4, m3, row_a, row_b,
    m3_grad_b, m4_grad_b, top_grad, term, total, sums, sums5,
):
    n3, chans = partial.shape
    n4 = c4.shape[0]
    me = place[0]
    per = each // 16

    def put(first, value):
        value = (value * scale).astype(BF16)
        for k in range(value.shape[0] // 16):
            y, owner, p = pieces_of(first // 16 + k, each)
            near, far = groups_of(owner, p // SIZES["z"], y, p % SIZES["z"])
            slot = jnp.where(me == owner, 0, 1)
            term[slot, near, far] = value[16 * k : 16 * k + 16]

    blank = jnp.zeros((16, chans), BF16)
    for y in range(SIZES["y"]):
        for p in range(per, 16):
            for owner in range(2):
                near, far = groups_of(owner, p // SIZES["z"], y, p % SIZES["z"])
                term[jnp.where(me == owner, 0, 1), near, far] = blank

    before, after = outer_lines(place, 0, row_a, row_b, n3 // width, width)
    to_the_left = jnp.where(place[1] == 1, 1.0, 0.0)
    total[...] = partial[...]
    added = {}
    for a, rows, (line, side) in (
        (2, slice(0, width), before),
        (0, slice(n3 - width, n3), after),
    ):
        planes = shift_line(line, side * to_the_left, side * (1.0 - to_the_left))
        part = total[rows]
        for b in range(3):
            tap = 3 * a + b
            part = part + dot(planes[2 - b], conv[tap * chans : (tap + 1) * chans], NT)
            added[tap] = (rows, planes[2 - b])
        total[rows] = part
    m3_grad_b[...] = total[...].astype(BF16)
    for y in range(n4 // (width // 2)):
        pair = total[2 * y * width : (2 * y + 1) * width] + total[(2 * y + 1) * width : (2 * y + 2) * width]
        sums[0, y * width : (y + 1) * width] = pair[:, :128]
        sums[1, y * width : (y + 1) * width] = pair[:, 128:]
    for h in range(2):
        cols = slice(128 * h, 128 * h + 128)
        m4_grad = (
            m4_cot[:, cols].astype(F32)
            + sums[h, pl.ds(0, n4, stride=2), :]
            + sums[h, pl.ds(1, n4, stride=2), :]
        )
        m4_grad_b[:, cols] = m4_grad.astype(BF16)
        half = width // 2
        for y in range(n4 // width):
            sums5[h, y * half : (y + 1) * half] = (
                m4_grad[2 * y * half : (2 * y + 1) * half]
                + m4_grad[(2 * y + 1) * half : (2 * y + 2) * half]
            )
        n5 = n4 // 4
        top_grad[:, cols] = (
            sums5[h, pl.ds(0, n5, stride=2), :] + sums5[h, pl.ds(1, n5, stride=2), :]
        ).astype(BF16)

    depth3, depth4 = c3.shape[1], c4.shape[1]
    put(0, dot(c3[...], m3_grad_b[...], TN))
    put(depth3, dot(c4[...], m4_grad_b[...], TN))
    for tap in range(9):
        value = gradc[tap * chans : (tap + 1) * chans]
        if tap in added:
            rows, plane = added[tap]
            value = value + dot(m3[rows], plane, TN)
        put(depth3 + depth4 + tap * chans, value)


def outputs_kernel(
    width, place, conv, lat3, lat4, m3, row_a, row_b, col, m3_grad_b, m4_grad_b,
    p3, c3_grad, c4_grad, shifted,
):
    n3, chans = m3.shape
    fill_inner(place, 1, m3, col, shifted, width)
    before, after = outer_lines(place, 1, row_a, row_b, n3 // width, width)
    fill_line(place, shifted, 0, *before)
    fill_line(place, shifted, n3 // width + 1, *after)
    total = None
    for a in range(3):
        for b in range(3):
            tap = 3 * a + b
            part = dot(shifted[b, a * width : a * width + n3], conv[tap * chans : (tap + 1) * chans])
            total = part if total is None else total + part
    p3[...] = total.astype(BF16)
    c3_grad[...] = dot(m3_grad_b[...], lat3[...], NT).astype(BF16)
    c4_grad[...] = dot(m4_grad_b[...], lat4[...], NT).astype(BF16)


def shape_of(*dims):
    return jax.ShapeDtypeStruct(dims, BF16)


def run_merge(width, c3, c4, top, lat3, lat4, cot):
    n3, n4, chans = c3.shape[0], c4.shape[0], lat3.shape[1]
    lines = n3 // width
    border = shape_of(2 * width + 2 * lines, chans)
    return call(
        functools.partial(merge_kernel, width // 2),
        [shape_of(n3, chans), shape_of(2 * lines, chans), border, border],
        [pltpu.VMEM((2, 2 * n4, 128), F32)],
        2 * chans * (c3.size + c4.size),
        2 * (c3.size + c4.size + lat3.size + lat4.size + 2 * cot.size),
        (c4, lat4, top, c3, lat3, cot),
    )


def fetch_kernel(place, waits, *refs):
    for wait in waits:
        wait()


def run_fetch(after, *arrays):
    moved = 2 * sum(x.size for x in arrays)
    return call(fetch_kernel, [], [], 0, moved, arrays, (after,))


def run_early(width, cot, conv, m3, col):
    n3, chans = cot.shape
    return call(
        functools.partial(early_kernel, width),
        [jax.ShapeDtypeStruct((n3, chans), F32), jax.ShapeDtypeStruct(conv.shape, F32)],
        [pltpu.VMEM((3, n3 + 2 * width, chans), BF16)],
        2 * chans * 2 * 9 * n3 * chans,
        8 * conv.size,
        (),
        (cot, conv, m3, col),
    )


def run_grads(width, each, scale, partial, gradc, conv, m4_cot, c3, c4, m3, row_a, row_b):
    n3, chans = partial.shape
    n4 = c4.shape[0]
    return call(
        functools.partial(grads_kernel, width, each, scale),
        [
            shape_of(n3, chans),
            shape_of(n4, chans),
            shape_of(n4 // 4, chans),
            shape_of(2, 8, 16, 16, chans),
        ],
        [
            pltpu.VMEM((n3, chans), F32),
            pltpu.VMEM((2, n3 // 2, 128), F32),
            pltpu.VMEM((2, n4 // 2, 128), F32),
        ],
        2 * chans * (c3.size + c4.size + 6 * width * chans),
        2 * (c3.size + c4.size + 4 * conv.size),
        (),
        (partial, gradc, conv, m4_cot, c3, c4, m3, row_a, row_b),
    )


def run_outputs(width, conv, lat3, lat4, m3, row_a, row_b, col, m3_grad_b, m4_grad_b):
    n3, chans = m3.shape
    n4 = m4_grad_b.shape[0]
    return call(
        functools.partial(outputs_kernel, width),
        [shape_of(n3, chans), shape_of(n3, lat3.shape[0]), shape_of(n4, lat4.shape[0])],
        [pltpu.VMEM((3, n3 + 2 * width, chans), BF16)],
        2 * chans * (n3 * lat3.shape[0] + n4 * lat4.shape[0] + 9 * n3 * chans),
        4 * (n3 * lat3.shape[0] + n4 * lat4.shape[0] + conv.size),
        (),
        (conv, lat3, lat4, m3, row_a, row_b, col, m3_grad_b, m4_grad_b),
    )


def swap_borders(col, row_a, row_b):
    col = lax.ppermute(col, "z_lo", [(0, 1), (1, 0)])
    n_rows = lax.axis_size(ROWS)

    def pairs(first):
        found = []
        for core in range(2):
            for i in range((first + core) % 2, n_rows - 1, 2):
                at = core * n_rows + i
                found += [(at, at + 1), (at + 1, at)]
        return found

    start = (row_a.shape[0] - col.shape[0], 0)
    row_a = lax.dynamic_update_slice(row_a, col, start)
    row_b = lax.dynamic_update_slice(row_b, col, start)
    row_a = lax.ppermute(row_a, ("core",) + ROWS, pairs(0))
    row_b = lax.ppermute(row_b, ("core",) + ROWS, pairs(1))
    return row_a, row_b, col


def add_cores_kernel(term, got, out):
    out[...] = (term[0].astype(F32) + got[...].astype(F32)).astype(BF16)


def add_cores(term, got):
    in_vmem = pl.BlockSpec(memory_space=pltpu.VMEM)
    return pl.pallas_call(
        add_cores_kernel,
        out_shape=shape_of(*got.shape),
        in_specs=[in_vmem] * 2,
        out_specs=in_vmem,
        compiler_params=pltpu.CompilerParams(vmem_limit_bytes=LIMIT),
        cost_estimate=pl.CostEstimate(
            flops=got.size, bytes_accessed=6 * got.size, transcendentals=0
        ),
    )(term, got)


def add_kernel(count, *refs):
    parts, out = refs[:-1], refs[-1]
    total = None
    for part in parts:
        for i in range(part.shape[0]):
            value = part[i].astype(F32)
            total = value if total is None else total + value
    total = total.astype(BF16)
    if count is None:
        out[...] = total
    else:
        for i in range(count):
            out[i] = total


def add_up(*parts, count=None):
    shape = parts[0].shape[1:]
    in_vmem = pl.BlockSpec(memory_space=pltpu.VMEM)
    return pl.pallas_call(
        functools.partial(add_kernel, count),
        out_shape=shape_of(*shape) if count is None else shape_of(count, *shape),
        in_specs=[in_vmem] * len(parts),
        out_specs=in_vmem,
        compiler_params=pltpu.CompilerParams(vmem_limit_bytes=LIMIT),
        cost_estimate=pl.CostEstimate(
            flops=sum(p.size for p in parts),
            bytes_accessed=2 * sum(p.size for p in parts),
            transcendentals=0,
        ),
    )(*parts)


def finish_kernel(parts, out):
    core = lax.axis_index("core")
    rows = parts.shape[2]
    for x_lo in range(2):
        x = jnp.where(core == x_lo, 0, 1)
        for z in range(parts.shape[1]):
            first = (x_lo * parts.shape[1] + z) * rows
            if first < out.shape[0]:
                value = parts[x, z].astype(F32) + parts[x + 2, z].astype(F32)
                out[first : first + rows] = value


def add_grads(term, got, each):
    everyone = OWNERS + SHARED
    near_groups, far_groups = group_lists()
    _, near, far, rows, cols = term.shape
    part = add_cores(term, got)
    part = lax.all_to_all(part.reshape(near, far * rows, cols), everyone, 0, 0, axis_index_groups=near_groups, tiled=True)
    part = add_up(part)
    part = lax.all_to_all(part.reshape(far, rows, cols), everyone, 0, 0, axis_index_groups=far_groups, tiled=True)
    part = add_up(part, count=lax.axis_size(SHARED))
    part = lax.all_to_all(part, everyone, 0, 0, axis_index_groups=shared_lists(), tiled=True)
    in_vmem = pl.BlockSpec(memory_space=pltpu.VMEM)
    return pl.pallas_call(
        finish_kernel,
        out_shape=jax.ShapeDtypeStruct((each, cols), F32),
        in_specs=[in_vmem],
        out_specs=in_vmem,
        compiler_params=pltpu.CompilerParams(vmem_limit_bytes=LIMIT),
    )(part.reshape(SIZES["x"], SIZES["z"], rows, cols))


def shards(c3, c4, top_down, lat3_weight, lat4_weight, conv_weight, p3_cot, m4_cot):
    count, height, width, depth3 = c3.shape
    depth4 = c4.shape[3]
    chans = conv_weight.shape[1]
    n3 = height * width
    n4 = n3 // 4
    n5 = n4 // 4
    stacked = depth3 + depth4 + 9 * chans
    owners = lax.axis_size(OWNERS)
    each = stacked // owners
    total_pixels = n3 * owners * lax.axis_size(SHARED)
    scale = 1.0 / math.sqrt(total_pixels)

    m3, col, row_a, row_b, *fetched = run_merge(
        width, c3.reshape(n3, depth3), c4.reshape(n4, depth4), top_down.reshape(n5, chans),
        lat3_weight, lat4_weight, p3_cot.reshape(n3, chans),
    )
    c4_v, lat4_v, _, c3_v, lat3_v, cot_v = fetched
    conv_v, m4_cot_v = run_fetch(m3, conv_weight, m4_cot.reshape(n4, chans))
    borders = swap_borders(col, row_a, row_b)
    partial, gradc = run_early(width, cot_v, conv_v, m3, borders[2])
    m3_grad_b, m4_grad_b, top_grad, term = run_grads(
        width, each, scale, partial, gradc, conv_v, m4_cot_v, c3_v, c4_v, m3, *borders[:2]
    )
    got = lax.ppermute(term[1], "core", [(0, 1), (1, 0)])
    p3, c3_grad, c4_grad = run_outputs(
        width, conv_v, lat3_v, lat4_v, m3, *borders, m3_grad_b, m4_grad_b
    )
    got, p3, c3_grad, c4_grad = lax.optimization_barrier((got, p3, c3_grad, c4_grad))
    weight_grads = add_grads(term, got, each)
    return (
        p3.reshape(count, height, width, chans),
        c3_grad.reshape(count, height, width, depth3),
        c4_grad.reshape(count, height // 2, width // 2, depth4),
        top_grad.reshape(top_down.shape),
        weight_grads,
    )


def solution(mesh):
    split = jax.sharding.Mesh(
        mesh.devices.reshape(8, 2, 4, 4, 2), ("y", "core", "x", "z_hi", "z_lo")
    )
    tiles = P(OWNERS, ROWS, "z_lo", None)
    return jax.shard_map(
        shards,
        mesh=split,
        in_specs=(tiles, tiles, tiles, P(), P(), P(), tiles, tiles),
        out_specs=(tiles, tiles, tiles, tiles, P(OWNERS, None)),
        check_vma=False,
    )
```

```python
import functools
import math

import jax
import jax.numpy as jnp
from jax import lax
from jax.experimental import pallas as pl
from jax.experimental.pallas import tpu as pltpu
from jax.sharding import PartitionSpec as P

F32 = jnp.float32
BF16 = jnp.bfloat16
ROWS = ("x", "z_hi")
OWNERS = ("y", "core")
SHARED = ("x", "z_hi", "z_lo")
SIZES = {"x": 4, "y": 8, "z": 8}
LIMIT = 32 * 1024 * 1024
NT = (((1,), (1,)), ((), ()))
TN = (((0,), (0,)), ((), ()))


def dot(lhs, rhs, dims=(((1,), (0,)), ((), ()))):
    return lax.dot_general(lhs, rhs, dims, preferred_element_type=F32)


def place_of_device():
    return lax.axis_index("core"), lax.axis_index("z_lo"), lax.axis_index("z_hi") % 2


def call(kernel, out_shape, scratch, flops, moved, fetched, held=()):
    in_vmem = pl.BlockSpec(memory_space=pltpu.VMEM)
    n, m, k = len(fetched), len(held), len(out_shape)

    def body(*refs):
        sources, refs = refs[:n], refs[n:]
        held_refs, refs = refs[:m], refs[m:]
        outs, refs = refs[:k], refs[k:]
        arrived, refs = refs[:n], refs[n:]
        if n == 0:
            kernel(place_of_device(), *held_refs, *outs, *refs)
            return
        copies = [
            pltpu.make_async_copy(source, target, refs[0].at[i])
            for i, (source, target) in enumerate(zip(sources, arrived))
        ]
        for copy in copies:
            copy.start()
        waits = [copy.wait for copy in copies]
        kernel(place_of_device(), waits, *arrived, *held_refs, *outs, *refs[1:])

    return pl.pallas_call(
        body,
        out_shape=list(out_shape) + [jax.ShapeDtypeStruct(x.shape, x.dtype) for x in fetched],
        in_specs=[pl.BlockSpec(memory_space=pltpu.HBM)] * n + [in_vmem] * m,
        out_specs=[in_vmem] * (k + n),
        scratch_shapes=([pltpu.SemaphoreType.DMA((n,))] if n else []) + scratch,
        compiler_params=pltpu.CompilerParams(vmem_limit_bytes=LIMIT),
        cost_estimate=pl.CostEstimate(flops=flops, bytes_accessed=moved, transcendentals=0),
    )(*[pltpu.with_memory_space_constraint(x, pltpu.HBM) for x in fetched], *held)


def merge_kernel(
    width4, place, waits, c4, lat4, top, c3, lat3, cot, m3, col, row_a, row_b, up4,
):
    n4, n5 = c4.shape[0], top.shape[0]
    n3 = c3.shape[0]
    width3, width5 = 2 * width4, width4 // 2
    row = lax.broadcasted_iota(jnp.int32, (n4, n5), 0)
    at = lax.broadcasted_iota(jnp.int32, (n4, n5), 1)
    source = (row // width4 // 2) * width5 + (row % width4) // 2
    pick = jnp.where(source == at, 1.0, 0.0).astype(BF16)
    for wait in waits[:3]:
        wait()
    m4 = dot(c4[...], lat4[...]) + dot(pick, top[...])
    for h in range(2):
        half = m4[:, 128 * h : 128 * h + 128]
        up4[h, pl.ds(0, n4, stride=2), :] = half
        up4[h, pl.ds(1, n4, stride=2), :] = half
    for wait in waits[3:5]:
        wait()
    lat = dot(c3[...], lat3[...])
    for y in range(n3 // width3):
        rows = slice(y * width3, (y + 1) * width3)
        above = slice((y // 2) * width3, (y // 2 + 1) * width3)
        for h in range(2):
            cols = slice(128 * h, 128 * h + 128)
            m3[rows, cols] = (lat[rows, cols] + up4[h, above]).astype(BF16)
    waits[5]()
    edge = jnp.where(place[1] == 0, width3 - 1, 0)
    lines = n3 // width3
    row = lax.broadcasted_iota(jnp.int32, (2 * lines, n3), 0)
    at = lax.broadcasted_iota(jnp.int32, (2 * lines, n3), 1)
    take_cot = jnp.where(at == row * width3 + edge, 1.0, 0.0).astype(BF16)
    take_m3 = jnp.where(at == (row - lines) * width3 + edge, 1.0, 0.0).astype(BF16)
    col[...] = (dot(take_cot, cot[...]) + dot(take_m3, m3[...])).astype(BF16)
    odd = place[2] == 1
    first = pl.multiple_of(jnp.where(odd, 0, n3 - width3), width3)
    second = pl.multiple_of(jnp.where(odd, n3 - width3, 0), width3)
    for start, out in ((first, row_a), (second, row_b)):
        out[:width3] = cot[pl.ds(start, width3)]
        out[width3 : 2 * width3] = m3[pl.ds(start, width3)]
        out[2 * width3 :] = jnp.zeros((2 * lines, out.shape[1]), BF16)


def shift_line(line, left, right):
    width = line.shape[0]
    at = lax.broadcasted_iota(jnp.int32, line.shape, 0)
    before = jnp.where(at == 0, left, pltpu.roll(line, 1, 0))
    after = jnp.where(at == width - 1, right, pltpu.roll(line, width - 1, 0))
    return before.astype(BF16), line.astype(BF16), after.astype(BF16)


def outer_lines(place, field, row_a, row_b, lines, width):
    odd = place[2] == 1
    rows = slice(field * width, (field + 1) * width)
    corner = slice(2 * width, 2 * width + 2 * lines)
    line_a, line_b = row_a[rows].astype(F32), row_b[rows].astype(F32)
    ends_a, ends_b = row_a[corner].astype(F32), row_b[corner].astype(F32)
    first, last = field * lines, (field + 1) * lines - 1
    return (
        (jnp.where(odd, line_a, line_b), jnp.where(odd, ends_a, ends_b)[last : last + 1]),
        (jnp.where(odd, line_b, line_a), jnp.where(odd, ends_b, ends_a)[first : first + 1]),
    )


def fill_line(place, shifted, y, line, side):
    to_the_left = jnp.where(place[1] == 1, 1.0, 0.0)
    width = line.shape[0]
    planes = shift_line(line, side * to_the_left, side * (1.0 - to_the_left))
    for i in range(3):
        shifted[i, y * width : (y + 1) * width] = planes[i]


def fill_inner(place, field, own, col, shifted, width):
    lines = own.shape[0] // width
    sides = col[...].astype(F32)
    for y in range(lines):
        side = sides[field * lines + y : field * lines + y + 1]
        fill_line(place, shifted, y + 1, own[y * width : (y + 1) * width].astype(F32), side)


def pieces_of(block, each):
    per = each // 16
    return block // per // 2, (block // per) % 2, block % per


def groups_of(core, x_lo, y, z):
    near = x_lo * 4 + (y + core) % 2 * 2 + (z + core) % 2
    return near, (y // 2) * (SIZES["z"] // 2) + z // 2


def group_lists():
    near, far = {}, {}
    index = 0
    for y in range(SIZES["y"]):
        for core in range(2):
            for x in range(SIZES["x"]):
                pair_x, x_lo = divmod((x + core) % SIZES["x"], 2)
                for z in range(SIZES["z"]):
                    pair_y = (y + core) % SIZES["y"] // 2
                    pair_z = (z + core) % SIZES["z"] // 2
                    in_near, in_far = groups_of(core, x_lo, y, z)
                    near.setdefault((core, pair_x, pair_y, pair_z), [None] * 8)[in_near] = index
                    far.setdefault((core, pair_x, in_near), [None] * 16)[in_far] = index
                    index += 1
    return list(near.values()), list(far.values())


def shared_lists():
    n = SIZES["x"] * SIZES["z"]
    return [
        [owner * n + x * SIZES["z"] + z for z in range(SIZES["z"]) for x in range(SIZES["x"])]
        for owner in range(2 * SIZES["y"])
    ]


def early_kernel(width, place, cot, conv, m3, col, partial, gradc, shifted):
    n3, chans = cot.shape
    blank = jnp.zeros((3, width, chans), BF16)
    shifted[:, :width] = blank
    shifted[:, n3 + width :] = blank
    fill_inner(place, 0, cot, col, shifted, width)
    m3_t = m3[...].T
    total = None
    for a in range(3):
        for b in range(3):
            tap = slice((3 * a + b) * chans, (3 * a + b + 1) * chans)
            field = shifted[2 - b, (2 - a) * width : (2 - a) * width + n3]
            part = dot(field, conv[tap], NT)
            total = part if total is None else total + part
            gradc[tap] = dot(m3_t, field)
    partial[...] = total


def grads_kernel(
    width, each, scale, place, partial, gradc, conv, m4_cot, c3, c4, m3, row_a, row_b,
    m3_grad_b, m4_grad_b, top_grad, term, total, sums, sums5,
):
    n3, chans = partial.shape
    n4 = c4.shape[0]
    me = place[0]
    per = each // 16

    def put(first, value):
        value = (value * scale).astype(BF16)
        for k in range(value.shape[0] // 16):
            y, owner, p = pieces_of(first // 16 + k, each)
            near, far = groups_of(owner, p // SIZES["z"], y, p % SIZES["z"])
            slot = jnp.where(me == owner, 0, 1)
            term[slot, near, far] = value[16 * k : 16 * k + 16]

    blank = jnp.zeros((16, chans), BF16)
    for y in range(SIZES["y"]):
        for p in range(per, 16):
            for owner in range(2):
                near, far = groups_of(owner, p // SIZES["z"], y, p % SIZES["z"])
                term[jnp.where(me == owner, 0, 1), near, far] = blank

    before, after = outer_lines(place, 0, row_a, row_b, n3 // width, width)
    to_the_left = jnp.where(place[1] == 1, 1.0, 0.0)
    total[...] = partial[...]
    added = {}
    for a, rows, (line, side) in (
        (2, slice(0, width), before),
        (0, slice(n3 - width, n3), after),
    ):
        planes = shift_line(line, side * to_the_left, side * (1.0 - to_the_left))
        part = total[rows]
        for b in range(3):
            tap = 3 * a + b
            part = part + dot(planes[2 - b], conv[tap * chans : (tap + 1) * chans], NT)
            added[tap] = (rows, planes[2 - b])
        total[rows] = part
    m3_grad_b[...] = total[...].astype(BF16)
    for y in range(n4 // (width // 2)):
        pair = total[2 * y * width : (2 * y + 1) * width] + total[(2 * y + 1) * width : (2 * y + 2) * width]
        sums[0, y * width : (y + 1) * width] = pair[:, :128]
        sums[1, y * width : (y + 1) * width] = pair[:, 128:]
    for h in range(2):
        cols = slice(128 * h, 128 * h + 128)
        m4_grad = (
            m4_cot[:, cols].astype(F32)
            + sums[h, pl.ds(0, n4, stride=2), :]
            + sums[h, pl.ds(1, n4, stride=2), :]
        )
        m4_grad_b[:, cols] = m4_grad.astype(BF16)
        half = width // 2
        for y in range(n4 // width):
            sums5[h, y * half : (y + 1) * half] = (
                m4_grad[2 * y * half : (2 * y + 1) * half]
                + m4_grad[(2 * y + 1) * half : (2 * y + 2) * half]
            )
        n5 = n4 // 4
        top_grad[:, cols] = (
            sums5[h, pl.ds(0, n5, stride=2), :] + sums5[h, pl.ds(1, n5, stride=2), :]
        ).astype(BF16)

    depth3, depth4 = c3.shape[1], c4.shape[1]
    put(0, dot(c3[...], m3_grad_b[...], TN))
    put(depth3, dot(c4[...], m4_grad_b[...], TN))
    for tap in range(9):
        value = gradc[tap * chans : (tap + 1) * chans]
        if tap in added:
            rows, plane = added[tap]
            value = value + dot(m3[rows], plane, TN)
        put(depth3 + depth4 + tap * chans, value)


def outputs_kernel(
    width, place, conv, lat3, lat4, m3, row_a, row_b, col, m3_grad_b, m4_grad_b,
    p3, c3_grad, c4_grad, shifted,
):
    n3, chans = m3.shape
    fill_inner(place, 1, m3, col, shifted, width)
    before, after = outer_lines(place, 1, row_a, row_b, n3 // width, width)
    fill_line(place, shifted, 0, *before)
    fill_line(place, shifted, n3 // width + 1, *after)
    total = None
    for a in range(3):
        for b in range(3):
            tap = 3 * a + b
            part = dot(shifted[b, a * width : a * width + n3], conv[tap * chans : (tap + 1) * chans])
            total = part if total is None else total + part
    p3[...] = total.astype(BF16)
    c3_grad[...] = dot(m3_grad_b[...], lat3[...], NT).astype(BF16)
    c4_grad[...] = dot(m4_grad_b[...], lat4[...], NT).astype(BF16)


def shape_of(*dims):
    return jax.ShapeDtypeStruct(dims, BF16)


def run_merge(width, c3, c4, top, lat3, lat4, cot):
    n3, n4, chans = c3.shape[0], c4.shape[0], lat3.shape[1]
    lines = n3 // width
    border = shape_of(2 * width + 2 * lines, chans)
    return call(
        functools.partial(merge_kernel, width // 2),
        [shape_of(n3, chans), shape_of(2 * lines, chans), border, border],
        [pltpu.VMEM((2, 2 * n4, 128), F32)],
        2 * chans * (c3.size + c4.size),
        2 * (c3.size + c4.size + lat3.size + lat4.size + 2 * cot.size),
        (c4, lat4, top, c3, lat3, cot),
    )


def fetch_kernel(place, waits, *refs):
    for wait in waits:
        wait()


def run_fetch(after, *arrays):
    moved = 2 * sum(x.size for x in arrays)
    return call(fetch_kernel, [], [], 0, moved, arrays, (after,))


def run_early(width, cot, conv, m3, col):
    n3, chans = cot.shape
    return call(
        functools.partial(early_kernel, width),
        [jax.ShapeDtypeStruct((n3, chans), F32), jax.ShapeDtypeStruct(conv.shape, F32)],
        [pltpu.VMEM((3, n3 + 2 * width, chans), BF16)],
        2 * chans * 2 * 9 * n3 * chans,
        8 * conv.size,
        (),
        (cot, conv, m3, col),
    )


def run_grads(width, each, scale, partial, gradc, conv, m4_cot, c3, c4, m3, row_a, row_b):
    n3, chans = partial.shape
    n4 = c4.shape[0]
    return call(
        functools.partial(grads_kernel, width, each, scale),
        [
            shape_of(n3, chans),
            shape_of(n4, chans),
            shape_of(n4 // 4, chans),
            shape_of(2, 8, 16, 16, chans),
        ],
        [
            pltpu.VMEM((n3, chans), F32),
            pltpu.VMEM((2, n3 // 2, 128), F32),
            pltpu.VMEM((2, n4 // 2, 128), F32),
        ],
        2 * chans * (c3.size + c4.size + 6 * width * chans),
        2 * (c3.size + c4.size + 4 * conv.size),
        (),
        (partial, gradc, conv, m4_cot, c3, c4, m3, row_a, row_b),
    )


def run_outputs(width, conv, lat3, lat4, m3, row_a, row_b, col, m3_grad_b, m4_grad_b):
    n3, chans = m3.shape
    n4 = m4_grad_b.shape[0]
    return call(
        functools.partial(outputs_kernel, width),
        [shape_of(n3, chans), shape_of(n3, lat3.shape[0]), shape_of(n4, lat4.shape[0])],
        [pltpu.VMEM((3, n3 + 2 * width, chans), BF16)],
        2 * chans * (n3 * lat3.shape[0] + n4 * lat4.shape[0] + 9 * n3 * chans),
        4 * (n3 * lat3.shape[0] + n4 * lat4.shape[0] + conv.size),
        (),
        (conv, lat3, lat4, m3, row_a, row_b, col, m3_grad_b, m4_grad_b),
    )


def swap_borders(col, row_a, row_b):
    col = lax.ppermute(col, "z_lo", [(0, 1), (1, 0)])
    n_rows = lax.axis_size(ROWS)
    pairs = [(i, i + 1) for i in range(0, n_rows - 1, 2)]
    between = [(i, i + 1) for i in range(1, n_rows - 1, 2)]
    start = (row_a.shape[0] - col.shape[0], 0)
    row_a = lax.dynamic_update_slice(row_a, col, start)
    row_b = lax.dynamic_update_slice(row_b, col, start)
    row_a = lax.ppermute(row_a, ROWS, pairs + [(j, i) for i, j in pairs])
    row_b = lax.ppermute(row_b, ROWS, between + [(j, i) for i, j in between])
    return row_a, row_b, col


def add_cores_kernel(term, got, out):
    out[...] = (term[0].astype(F32) + got[...].astype(F32)).astype(BF16)


def add_cores(term, got):
    in_vmem = pl.BlockSpec(memory_space=pltpu.VMEM)
    return pl.pallas_call(
        add_cores_kernel,
        out_shape=shape_of(*got.shape),
        in_specs=[in_vmem] * 2,
        out_specs=in_vmem,
        compiler_params=pltpu.CompilerParams(vmem_limit_bytes=LIMIT),
        cost_estimate=pl.CostEstimate(
            flops=got.size, bytes_accessed=6 * got.size, transcendentals=0
        ),
    )(term, got)


def add_kernel(count, *refs):
    parts, out = refs[:-1], refs[-1]
    total = None
    for part in parts:
        for i in range(part.shape[0]):
            value = part[i].astype(F32)
            total = value if total is None else total + value
    total = total.astype(BF16)
    if count is None:
        out[...] = total
    else:
        for i in range(count):
            out[i] = total


def add_up(*parts, count=None):
    shape = parts[0].shape[1:]
    in_vmem = pl.BlockSpec(memory_space=pltpu.VMEM)
    return pl.pallas_call(
        functools.partial(add_kernel, count),
        out_shape=shape_of(*shape) if count is None else shape_of(count, *shape),
        in_specs=[in_vmem] * len(parts),
        out_specs=in_vmem,
        compiler_params=pltpu.CompilerParams(vmem_limit_bytes=LIMIT),
        cost_estimate=pl.CostEstimate(
            flops=sum(p.size for p in parts),
            bytes_accessed=2 * sum(p.size for p in parts),
            transcendentals=0,
        ),
    )(*parts)


def finish_kernel(parts, out):
    core = lax.axis_index("core")
    rows = parts.shape[2]
    for x_lo in range(2):
        x = jnp.where(core == x_lo, 0, 1)
        for z in range(parts.shape[0]):
            first = (x_lo * parts.shape[0] + z) * rows
            if first < out.shape[0]:
                value = parts[z, x].astype(F32) + parts[z, x + 2].astype(F32)
                out[first : first + rows] = value


def add_grads(term, got, each):
    everyone = OWNERS + SHARED
    near_groups, far_groups = group_lists()
    _, near, far, rows, cols = term.shape
    part = add_cores(term, got)
    part = lax.all_to_all(part.reshape(near, far * rows, cols), everyone, 0, 0, axis_index_groups=near_groups, tiled=True)
    part = add_up(part)
    part = lax.all_to_all(part.reshape(far, rows, cols), everyone, 0, 0, axis_index_groups=far_groups, tiled=True)
    part = add_up(part, count=lax.axis_size(SHARED))
    part = lax.all_to_all(part, everyone, 0, 0, axis_index_groups=shared_lists(), tiled=True)
    in_vmem = pl.BlockSpec(memory_space=pltpu.VMEM)
    return pl.pallas_call(
        finish_kernel,
        out_shape=jax.ShapeDtypeStruct((each, cols), F32),
        in_specs=[in_vmem],
        out_specs=in_vmem,
        compiler_params=pltpu.CompilerParams(vmem_limit_bytes=LIMIT),
    )(part.reshape(SIZES["z"], SIZES["x"], rows, cols))


def shards(c3, c4, top_down, lat3_weight, lat4_weight, conv_weight, p3_cot, m4_cot):
    count, height, width, depth3 = c3.shape
    depth4 = c4.shape[3]
    chans = conv_weight.shape[1]
    n3 = height * width
    n4 = n3 // 4
    n5 = n4 // 4
    stacked = depth3 + depth4 + 9 * chans
    owners = lax.axis_size(OWNERS)
    each = stacked // owners
    total_pixels = n3 * owners * lax.axis_size(SHARED)
    scale = 1.0 / math.sqrt(total_pixels)

    m3, col, row_a, row_b, *fetched = run_merge(
        width, c3.reshape(n3, depth3), c4.reshape(n4, depth4), top_down.reshape(n5, chans),
        lat3_weight, lat4_weight, p3_cot.reshape(n3, chans),
    )
    c4_v, lat4_v, _, c3_v, lat3_v, cot_v = fetched
    conv_v, m4_cot_v = run_fetch(m3, conv_weight, m4_cot.reshape(n4, chans))
    borders = swap_borders(col, row_a, row_b)
    partial, gradc = run_early(width, cot_v, conv_v, m3, borders[2])
    m3_grad_b, m4_grad_b, top_grad, term = run_grads(
        width, each, scale, partial, gradc, conv_v, m4_cot_v, c3_v, c4_v, m3, *borders[:2]
    )
    got = lax.ppermute(term[1], "core", [(0, 1), (1, 0)])
    p3, c3_grad, c4_grad = run_outputs(
        width, conv_v, lat3_v, lat4_v, m3, *borders, m3_grad_b, m4_grad_b
    )
    got, p3, c3_grad, c4_grad = lax.optimization_barrier((got, p3, c3_grad, c4_grad))
    weight_grads = add_grads(term, got, each)
    return (
        p3.reshape(count, height, width, chans),
        c3_grad.reshape(count, height, width, depth3),
        c4_grad.reshape(count, height // 2, width // 2, depth4),
        top_grad.reshape(top_down.shape),
        weight_grads,
    )


def solution(mesh):
    split = jax.sharding.Mesh(
        mesh.devices.reshape(8, 2, 4, 4, 2), ("y", "core", "x", "z_hi", "z_lo")
    )
    tiles = P(OWNERS, ROWS, "z_lo", None)
    return jax.shard_map(
        shards,
        mesh=split,
        in_specs=(tiles, tiles, tiles, P(), P(), P(), tiles, tiles),
        out_specs=(tiles, tiles, tiles, tiles, P(OWNERS, None)),
        check_vma=False,
    )
```

```python
import functools
import math

import jax
import jax.numpy as jnp
from jax import lax
from jax.experimental import pallas as pl
from jax.experimental.pallas import tpu as pltpu
from jax.sharding import PartitionSpec as P

F32 = jnp.float32
BF16 = jnp.bfloat16
ROWS = ("x", "z_hi")
OWNERS = ("y", "core")
SHARED = ("x", "z_hi", "z_lo")
SIZES = {"x": 4, "y": 8, "z": 8}
LIMIT = 32 * 1024 * 1024
NT = (((1,), (1,)), ((), ()))
TN = (((0,), (0,)), ((), ()))


def dot(lhs, rhs, dims=(((1,), (0,)), ((), ()))):
    return lax.dot_general(lhs, rhs, dims, preferred_element_type=F32)


def place_of_device():
    return lax.axis_index("core"), lax.axis_index("z_lo"), lax.axis_index("z_hi") % 2


def call(kernel, out_shape, scratch, flops, moved, fetched, held=()):
    in_vmem = pl.BlockSpec(memory_space=pltpu.VMEM)
    n, m, k = len(fetched), len(held), len(out_shape)

    def body(*refs):
        sources, refs = refs[:n], refs[n:]
        held_refs, refs = refs[:m], refs[m:]
        outs, refs = refs[:k], refs[k:]
        arrived, refs = refs[:n], refs[n:]
        if n == 0:
            kernel(place_of_device(), *held_refs, *outs, *refs)
            return
        copies = [
            pltpu.make_async_copy(source, target, refs[0].at[i])
            for i, (source, target) in enumerate(zip(sources, arrived))
        ]
        for copy in copies:
            copy.start()
        waits = [copy.wait for copy in copies]
        kernel(place_of_device(), waits, *arrived, *held_refs, *outs, *refs[1:])

    return pl.pallas_call(
        body,
        out_shape=list(out_shape) + [jax.ShapeDtypeStruct(x.shape, x.dtype) for x in fetched],
        in_specs=[pl.BlockSpec(memory_space=pltpu.HBM)] * n + [in_vmem] * m,
        out_specs=[in_vmem] * (k + n),
        scratch_shapes=([pltpu.SemaphoreType.DMA((n,))] if n else []) + scratch,
        compiler_params=pltpu.CompilerParams(vmem_limit_bytes=LIMIT),
        cost_estimate=pl.CostEstimate(flops=flops, bytes_accessed=moved, transcendentals=0),
    )(*[pltpu.with_memory_space_constraint(x, pltpu.HBM) for x in fetched], *held)


def merge_kernel(
    width4, place, waits, c4, lat4, top, c3, lat3, cot, m3, col, row_a, row_b, up4,
):
    n4, n5 = c4.shape[0], top.shape[0]
    n3 = c3.shape[0]
    width3, width5 = 2 * width4, width4 // 2
    row = lax.broadcasted_iota(jnp.int32, (n4, n5), 0)
    at = lax.broadcasted_iota(jnp.int32, (n4, n5), 1)
    source = (row // width4 // 2) * width5 + (row % width4) // 2
    pick = jnp.where(source == at, 1.0, 0.0).astype(BF16)
    for wait in waits[:3]:
        wait()
    m4 = dot(c4[...], lat4[...]) + dot(pick, top[...])
    for h in range(2):
        half = m4[:, 128 * h : 128 * h + 128]
        up4[h, pl.ds(0, n4, stride=2), :] = half
        up4[h, pl.ds(1, n4, stride=2), :] = half
    for wait in waits[3:5]:
        wait()
    lat = dot(c3[...], lat3[...])
    for y in range(n3 // width3):
        rows = slice(y * width3, (y + 1) * width3)
        above = slice((y // 2) * width3, (y // 2 + 1) * width3)
        for h in range(2):
            cols = slice(128 * h, 128 * h + 128)
            m3[rows, cols] = (lat[rows, cols] + up4[h, above]).astype(BF16)
    waits[5]()
    edge = jnp.where(place[1] == 0, width3 - 1, 0)
    lines = n3 // width3
    row = lax.broadcasted_iota(jnp.int32, (2 * lines, n3), 0)
    at = lax.broadcasted_iota(jnp.int32, (2 * lines, n3), 1)
    take_cot = jnp.where(at == row * width3 + edge, 1.0, 0.0).astype(BF16)
    take_m3 = jnp.where(at == (row - lines) * width3 + edge, 1.0, 0.0).astype(BF16)
    col[...] = (dot(take_cot, cot[...]) + dot(take_m3, m3[...])).astype(BF16)
    odd = place[2] == 1
    first = pl.multiple_of(jnp.where(odd, 0, n3 - width3), width3)
    second = pl.multiple_of(jnp.where(odd, n3 - width3, 0), width3)
    for start, out in ((first, row_a), (second, row_b)):
        out[:width3] = cot[pl.ds(start, width3)]
        out[width3 : 2 * width3] = m3[pl.ds(start, width3)]
        out[2 * width3 :] = jnp.zeros((2 * lines, out.shape[1]), BF16)


def shift_line(line, left, right):
    width = line.shape[0]
    at = lax.broadcasted_iota(jnp.int32, line.shape, 0)
    before = jnp.where(at == 0, left, pltpu.roll(line, 1, 0))
    after = jnp.where(at == width - 1, right, pltpu.roll(line, width - 1, 0))
    return before.astype(BF16), line.astype(BF16), after.astype(BF16)


def outer_lines(place, field, row_a, row_b, lines, width):
    odd = place[2] == 1
    rows = slice(field * width, (field + 1) * width)
    corner = slice(2 * width, 2 * width + 2 * lines)
    line_a, line_b = row_a[rows].astype(F32), row_b[rows].astype(F32)
    ends_a, ends_b = row_a[corner].astype(F32), row_b[corner].astype(F32)
    first, last = field * lines, (field + 1) * lines - 1
    return (
        (jnp.where(odd, line_a, line_b), jnp.where(odd, ends_a, ends_b)[last : last + 1]),
        (jnp.where(odd, line_b, line_a), jnp.where(odd, ends_b, ends_a)[first : first + 1]),
    )


def fill_line(place, shifted, y, line, side):
    to_the_left = jnp.where(place[1] == 1, 1.0, 0.0)
    width = line.shape[0]
    planes = shift_line(line, side * to_the_left, side * (1.0 - to_the_left))
    for i in range(3):
        shifted[i, y * width : (y + 1) * width] = planes[i]


def fill_inner(place, field, own, col, shifted, width):
    lines = own.shape[0] // width
    sides = col[...].astype(F32)
    for y in range(lines):
        side = sides[field * lines + y : field * lines + y + 1]
        fill_line(place, shifted, y + 1, own[y * width : (y + 1) * width].astype(F32), side)


def pieces_of(block, each):
    per = each // 16
    return block // per // 2, (block // per) % 2, block % per


def groups_of(core, x_lo, y, z):
    near = x_lo * 4 + (y + core) % 2 * 2 + (z + core) % 2
    return near, (y // 2) * (SIZES["z"] // 2) + z // 2


def group_lists():
    near, far = {}, {}
    index = 0
    for y in range(SIZES["y"]):
        for core in range(2):
            for x in range(SIZES["x"]):
                pair_x, x_lo = divmod((x + core) % SIZES["x"], 2)
                for z in range(SIZES["z"]):
                    pair_y = (y + core) % SIZES["y"] // 2
                    pair_z = (z + core) % SIZES["z"] // 2
                    in_near, in_far = groups_of(core, x_lo, y, z)
                    near.setdefault((core, pair_x, pair_y, pair_z), [None] * 8)[in_near] = index
                    far.setdefault((core, pair_x, in_near), [None] * 16)[in_far] = index
                    index += 1
    return list(near.values()), list(far.values())


def shared_lists():
    n = SIZES["x"] * SIZES["z"]
    lists = []
    for owner in range(2 * SIZES["y"]):
        group = [owner * n + i for i in range(n)]
        turn = owner % 2 * (n // 2)
        lists.append(group[turn:] + group[:turn])
    return lists


def early_kernel(width, place, cot, conv, m3, col, partial, gradc, shifted):
    n3, chans = cot.shape
    blank = jnp.zeros((3, width, chans), BF16)
    shifted[:, :width] = blank
    shifted[:, n3 + width :] = blank
    fill_inner(place, 0, cot, col, shifted, width)
    m3_t = m3[...].T
    total = None
    for a in range(3):
        for b in range(3):
            tap = slice((3 * a + b) * chans, (3 * a + b + 1) * chans)
            field = shifted[2 - b, (2 - a) * width : (2 - a) * width + n3]
            part = dot(field, conv[tap], NT)
            total = part if total is None else total + part
            gradc[tap] = dot(m3_t, field)
    partial[...] = total


def grads_kernel(
    width, each, scale, place, partial, gradc, conv, m4_cot, c3, c4, m3, row_a, row_b,
    m3_grad_b, m4_grad_b, top_grad, term, total, sums, sums5,
):
    n3, chans = partial.shape
    n4 = c4.shape[0]
    me = place[0]
    per = each // 16

    def put(first, value):
        value = (value * scale).astype(BF16)
        for k in range(value.shape[0] // 16):
            y, owner, p = pieces_of(first // 16 + k, each)
            near, far = groups_of(owner, p // SIZES["z"], y, p % SIZES["z"])
            slot = jnp.where(me == owner, 0, 1)
            term[slot, near, far] = value[16 * k : 16 * k + 16]

    blank = jnp.zeros((16, chans), BF16)
    for y in range(SIZES["y"]):
        for p in range(per, 16):
            for owner in range(2):
                near, far = groups_of(owner, p // SIZES["z"], y, p % SIZES["z"])
                term[jnp.where(me == owner, 0, 1), near, far] = blank

    before, after = outer_lines(place, 0, row_a, row_b, n3 // width, width)
    to_the_left = jnp.where(place[1] == 1, 1.0, 0.0)
    total[...] = partial[...]
    added = {}
    for a, rows, (line, side) in (
        (2, slice(0, width), before),
        (0, slice(n3 - width, n3), after),
    ):
        planes = shift_line(line, side * to_the_left, side * (1.0 - to_the_left))
        part = total[rows]
        for b in range(3):
            tap = 3 * a + b
            part = part + dot(planes[2 - b], conv[tap * chans : (tap + 1) * chans], NT)
            added[tap] = (rows, planes[2 - b])
        total[rows] = part
    m3_grad_b[...] = total[...].astype(BF16)
    for y in range(n4 // (width // 2)):
        pair = total[2 * y * width : (2 * y + 1) * width] + total[(2 * y + 1) * width : (2 * y + 2) * width]
        sums[0, y * width : (y + 1) * width] = pair[:, :128]
        sums[1, y * width : (y + 1) * width] = pair[:, 128:]
    for h in range(2):
        cols = slice(128 * h, 128 * h + 128)
        m4_grad = (
            m4_cot[:, cols].astype(F32)
            + sums[h, pl.ds(0, n4, stride=2), :]
            + sums[h, pl.ds(1, n4, stride=2), :]
        )
        m4_grad_b[:, cols] = m4_grad.astype(BF16)
        half = width // 2
        for y in range(n4 // width):
            sums5[h, y * half : (y + 1) * half] = (
                m4_grad[2 * y * half : (2 * y + 1) * half]
                + m4_grad[(2 * y + 1) * half : (2 * y + 2) * half]
            )
        n5 = n4 // 4
        top_grad[:, cols] = (
            sums5[h, pl.ds(0, n5, stride=2), :] + sums5[h, pl.ds(1, n5, stride=2), :]
        ).astype(BF16)

    depth3, depth4 = c3.shape[1], c4.shape[1]
    put(0, dot(c3[...], m3_grad_b[...], TN))
    put(depth3, dot(c4[...], m4_grad_b[...], TN))
    for tap in range(9):
        value = gradc[tap * chans : (tap + 1) * chans]
        if tap in added:
            rows, plane = added[tap]
            value = value + dot(m3[rows], plane, TN)
        put(depth3 + depth4 + tap * chans, value)


def outputs_kernel(
    width, place, conv, lat3, lat4, m3, row_a, row_b, col, m3_grad_b, m4_grad_b,
    p3, c3_grad, c4_grad, shifted,
):
    n3, chans = m3.shape
    fill_inner(place, 1, m3, col, shifted, width)
    before, after = outer_lines(place, 1, row_a, row_b, n3 // width, width)
    fill_line(place, shifted, 0, *before)
    fill_line(place, shifted, n3 // width + 1, *after)
    total = None
    for a in range(3):
        for b in range(3):
            tap = 3 * a + b
            part = dot(shifted[b, a * width : a * width + n3], conv[tap * chans : (tap + 1) * chans])
            total = part if total is None else total + part
    p3[...] = total.astype(BF16)
    c3_grad[...] = dot(m3_grad_b[...], lat3[...], NT).astype(BF16)
    c4_grad[...] = dot(m4_grad_b[...], lat4[...], NT).astype(BF16)


def shape_of(*dims):
    return jax.ShapeDtypeStruct(dims, BF16)


def run_merge(width, c3, c4, top, lat3, lat4, cot):
    n3, n4, chans = c3.shape[0], c4.shape[0], lat3.shape[1]
    lines = n3 // width
    border = shape_of(2 * width + 2 * lines, chans)
    return call(
        functools.partial(merge_kernel, width // 2),
        [shape_of(n3, chans), shape_of(2 * lines, chans), border, border],
        [pltpu.VMEM((2, 2 * n4, 128), F32)],
        2 * chans * (c3.size + c4.size),
        2 * (c3.size + c4.size + lat3.size + lat4.size + 2 * cot.size),
        (c4, lat4, top, c3, lat3, cot),
    )


def fetch_kernel(place, waits, *refs):
    for wait in waits:
        wait()


def run_fetch(after, *arrays):
    moved = 2 * sum(x.size for x in arrays)
    return call(fetch_kernel, [], [], 0, moved, arrays, (after,))


def run_early(width, cot, conv, m3, col):
    n3, chans = cot.shape
    return call(
        functools.partial(early_kernel, width),
        [jax.ShapeDtypeStruct((n3, chans), F32), jax.ShapeDtypeStruct(conv.shape, F32)],
        [pltpu.VMEM((3, n3 + 2 * width, chans), BF16)],
        2 * chans * 2 * 9 * n3 * chans,
        8 * conv.size,
        (),
        (cot, conv, m3, col),
    )


def run_grads(width, each, scale, partial, gradc, conv, m4_cot, c3, c4, m3, row_a, row_b):
    n3, chans = partial.shape
    n4 = c4.shape[0]
    return call(
        functools.partial(grads_kernel, width, each, scale),
        [
            shape_of(n3, chans),
            shape_of(n4, chans),
            shape_of(n4 // 4, chans),
            shape_of(2, 8, 16, 16, chans),
        ],
        [
            pltpu.VMEM((n3, chans), F32),
            pltpu.VMEM((2, n3 // 2, 128), F32),
            pltpu.VMEM((2, n4 // 2, 128), F32),
        ],
        2 * chans * (c3.size + c4.size + 6 * width * chans),
        2 * (c3.size + c4.size + 4 * conv.size),
        (),
        (partial, gradc, conv, m4_cot, c3, c4, m3, row_a, row_b),
    )


def run_outputs(width, conv, lat3, lat4, m3, row_a, row_b, col, m3_grad_b, m4_grad_b):
    n3, chans = m3.shape
    n4 = m4_grad_b.shape[0]
    return call(
        functools.partial(outputs_kernel, width),
        [shape_of(n3, chans), shape_of(n3, lat3.shape[0]), shape_of(n4, lat4.shape[0])],
        [pltpu.VMEM((3, n3 + 2 * width, chans), BF16)],
        2 * chans * (n3 * lat3.shape[0] + n4 * lat4.shape[0] + 9 * n3 * chans),
        4 * (n3 * lat3.shape[0] + n4 * lat4.shape[0] + conv.size),
        (),
        (conv, lat3, lat4, m3, row_a, row_b, col, m3_grad_b, m4_grad_b),
    )


def swap_borders(col, row_a, row_b):
    col = lax.ppermute(col, "z_lo", [(0, 1), (1, 0)])
    n_rows = lax.axis_size(ROWS)
    pairs = [(i, i + 1) for i in range(0, n_rows - 1, 2)]
    between = [(i, i + 1) for i in range(1, n_rows - 1, 2)]
    start = (row_a.shape[0] - col.shape[0], 0)
    row_a = lax.dynamic_update_slice(row_a, col, start)
    row_b = lax.dynamic_update_slice(row_b, col, start)
    row_a = lax.ppermute(row_a, ROWS, pairs + [(j, i) for i, j in pairs])
    row_b = lax.ppermute(row_b, ROWS, between + [(j, i) for i, j in between])
    return row_a, row_b, col


def add_cores_kernel(term, got, out):
    out[...] = (term[0].astype(F32) + got[...].astype(F32)).astype(BF16)


def add_cores(term, got):
    in_vmem = pl.BlockSpec(memory_space=pltpu.VMEM)
    return pl.pallas_call(
        add_cores_kernel,
        out_shape=shape_of(*got.shape),
        in_specs=[in_vmem] * 2,
        out_specs=in_vmem,
        compiler_params=pltpu.CompilerParams(vmem_limit_bytes=LIMIT),
        cost_estimate=pl.CostEstimate(
            flops=got.size, bytes_accessed=6 * got.size, transcendentals=0
        ),
    )(term, got)


def add_kernel(count, *refs):
    parts, out = refs[:-1], refs[-1]
    total = None
    for part in parts:
        for i in range(part.shape[0]):
            value = part[i].astype(F32)
            total = value if total is None else total + value
    total = total.astype(BF16)
    if count is None:
        out[...] = total
    else:
        for i in range(count):
            out[i] = total


def add_up(*parts, count=None):
    shape = parts[0].shape[1:]
    in_vmem = pl.BlockSpec(memory_space=pltpu.VMEM)
    return pl.pallas_call(
        functools.partial(add_kernel, count),
        out_shape=shape_of(*shape) if count is None else shape_of(count, *shape),
        in_specs=[in_vmem] * len(parts),
        out_specs=in_vmem,
        compiler_params=pltpu.CompilerParams(vmem_limit_bytes=LIMIT),
        cost_estimate=pl.CostEstimate(
            flops=sum(p.size for p in parts),
            bytes_accessed=2 * sum(p.size for p in parts),
            transcendentals=0,
        ),
    )(*parts)


def finish_kernel(parts, out):
    core = lax.axis_index("core")
    rows = parts.shape[2]
    for x_lo in range(2):
        x = jnp.where(core == x_lo, 0, 1)
        for z in range(parts.shape[1]):
            first = (x_lo * parts.shape[1] + z) * rows
            if first < out.shape[0]:
                value = parts[x, z].astype(F32) + parts[x + 2, z].astype(F32)
                out[first : first + rows] = value


def add_grads(term, got, each):
    everyone = OWNERS + SHARED
    near_groups, far_groups = group_lists()
    _, near, far, rows, cols = term.shape
    part = add_cores(term, got)
    part = lax.all_to_all(part.reshape(near, far * rows, cols), everyone, 0, 0, axis_index_groups=near_groups, tiled=True)
    part = add_up(part)
    part = lax.all_to_all(part.reshape(far, rows, cols), everyone, 0, 0, axis_index_groups=far_groups, tiled=True)
    part = add_up(part, count=lax.axis_size(SHARED))
    part = lax.all_to_all(part, everyone, 0, 0, axis_index_groups=shared_lists(), tiled=True)
    in_vmem = pl.BlockSpec(memory_space=pltpu.VMEM)
    return pl.pallas_call(
        finish_kernel,
        out_shape=jax.ShapeDtypeStruct((each, cols), F32),
        in_specs=[in_vmem],
        out_specs=in_vmem,
        compiler_params=pltpu.CompilerParams(vmem_limit_bytes=LIMIT),
    )(part.reshape(SIZES["x"], SIZES["z"], rows, cols))


def shards(c3, c4, top_down, lat3_weight, lat4_weight, conv_weight, p3_cot, m4_cot):
    count, height, width, depth3 = c3.shape
    depth4 = c4.shape[3]
    chans = conv_weight.shape[1]
    n3 = height * width
    n4 = n3 // 4
    n5 = n4 // 4
    stacked = depth3 + depth4 + 9 * chans
    owners = lax.axis_size(OWNERS)
    each = stacked // owners
    total_pixels = n3 * owners * lax.axis_size(SHARED)
    scale = 1.0 / math.sqrt(total_pixels)

    m3, col, row_a, row_b, *fetched = run_merge(
        width, c3.reshape(n3, depth3), c4.reshape(n4, depth4), top_down.reshape(n5, chans),
        lat3_weight, lat4_weight, p3_cot.reshape(n3, chans),
    )
    c4_v, lat4_v, _, c3_v, lat3_v, cot_v = fetched
    conv_v, m4_cot_v = run_fetch(m3, conv_weight, m4_cot.reshape(n4, chans))
    borders = swap_borders(col, row_a, row_b)
    partial, gradc = run_early(width, cot_v, conv_v, m3, borders[2])
    m3_grad_b, m4_grad_b, top_grad, term = run_grads(
        width, each, scale, partial, gradc, conv_v, m4_cot_v, c3_v, c4_v, m3, *borders[:2]
    )
    got = lax.ppermute(term[1], "core", [(0, 1), (1, 0)])
    p3, c3_grad, c4_grad = run_outputs(
        width, conv_v, lat3_v, lat4_v, m3, *borders, m3_grad_b, m4_grad_b
    )
    got, p3, c3_grad, c4_grad = lax.optimization_barrier((got, p3, c3_grad, c4_grad))
    weight_grads = add_grads(term, got, each)
    return (
        p3.reshape(count, height, width, chans),
        c3_grad.reshape(count, height, width, depth3),
        c4_grad.reshape(count, height // 2, width // 2, depth4),
        top_grad.reshape(top_down.shape),
        weight_grads,
    )


def solution(mesh):
    split = jax.sharding.Mesh(
        mesh.devices.reshape(8, 2, 4, 4, 2), ("y", "core", "x", "z_hi", "z_lo")
    )
    tiles = P(OWNERS, ROWS, "z_lo", None)
    return jax.shard_map(
        shards,
        mesh=split,
        in_specs=(tiles, tiles, tiles, P(), P(), P(), tiles, tiles),
        out_specs=(tiles, tiles, tiles, tiles, P(OWNERS, None)),
        check_vma=False,
    )
```
